256 devices in a mesh: tm: 32 (over y, z_lo, core), video: 8 (over x, z_hi).
Axes of the slice: x: 4, y: 4, z: 8 (z_hi: 2, z_lo: 4; z = z_hi * 4 + z_lo), core: 2. Of those that a mesh axis runs over, the one named last changes fastest.
Arguments:
- memory: bfloat16 [8, 32, 1, 64, 768], P('video', 'tm'), may hold values from -24 to 24
- frames: float32 [8, 32, 1, 128, 768], P('video', 'tm'), may hold values from -6 to 6
- mem_cot: bfloat16 [8, 32, 1, 64, 768], P('video', 'tm'), may hold values from -3 to 3
- slot_used: int32 [8, 32, 1], P('video', 'tm'), may hold values 0 or 1
- key_bias: float32 [8, 32, 1, 12, 128], P('video', 'tm'), may hold values from -6 to 300
- start_offset: int32 [8, 1], P('video'), may hold values from 0 to 4095
- norm_gain: float32 [768], replicated, may hold values from 0.5 to 1.5
- w_query: bfloat16 [768, 768], replicated, may hold values from -0.21875 to 0.21875
- w_key: bfloat16 [768, 768], replicated, may hold values from -0.21875 to 0.21875
- w_value: bfloat16 [768, 768], replicated, may hold values from -0.21875 to 0.21875
- w_out: bfloat16 [768, 768], replicated, may hold values from -0.21875 to 0.21875
Outputs:
- grad_memory: float32 [8, 32, 1, 64, 768], P('video', 'tm')
- grad_query: float32 [768, 768], P('tm', 'video')
- grad_key: float32 [768, 768], P('tm', 'video')
- grad_value: float32 [768, 768], P('tm', 'video')
- grad_out: float32 [768, 768], P('tm', 'video')
- grad_gain: float32 [768], replicated
The draws below stay inside these ranges and needn't reach their ends.
All inputs are finite; a program needn't handle non-finite values. No bound on the sum of `slot_used` on one device may be relied on, other than what follows from the above.
Results may differ from the reference program's by a relative error of at most 0.019.
Values sent between devices are 32-bit elements; how exact they have to be, the bound alone decides.
No kernel may reach another device: no remote copies, remote signals or barrier semaphores. Data moves between devices by JAX's collectives and lax.ppermute only.
A program may use at most 64 MiB of HBM per device.

```python
import math
import jax
import jax.numpy as jnp
from jax import lax

D = 768
H = 12
HD = 64
R = 64
L = 128
STREAMS = 1
GROUPS = 8
OWNERS = 32


def draw_memory(key, part):
    full_shape = (GROUPS, OWNERS, STREAMS, R, D)
    key_noise, key_rows, key_cols = jax.random.split(key, 3)
    gaussian = jax.random.normal(key_noise, full_shape, jnp.float32)
    row_scale = jnp.exp(jax.random.uniform(key_rows, full_shape[:4] + (1,), jnp.float32, math.log(0.3), math.log(3.0)))
    column_scale = jnp.exp(jax.random.uniform(key_cols, (D,), jnp.float32, math.log(0.3), math.log(3.0)))
    values_drawn = gaussian * row_scale * column_scale
    return jnp.clip(values_drawn, -24.0, 24.0).astype(jnp.bfloat16)


def draw_key_bias(key, part):
    full_shape = (GROUPS, OWNERS, STREAMS, H, L)
    key_noise = jax.random.fold_in(key, 0)
    values_drawn = jnp.clip(jax.random.normal(key_noise, full_shape, jnp.float32), -6.0, 6.0)
    return values_drawn


def with_ends(entries, stream_key, least, top_value):
    shape = entries.shape
    index_at = [jax.random.randint(jax.random.fold_in(stream_key, axis), (), 0, shape[axis]) for axis in range(len(shape))]
    entries = entries.at[tuple(index_at)].set(least)
    longest = shape.index(max(shape))
    index_at[longest] = (index_at[longest] + 1) % shape[longest]
    return entries.at[tuple(index_at)].set(top_value)


def block_levels(stream_key, shape, cuts, low, high):
    def one(dim, blocks):
        heights = jax.random.uniform(jax.random.fold_in(jax.random.fold_in(stream_key, 6), dim), (blocks,), jnp.float32, low / len(cuts), high / len(cuts))
        return jnp.repeat(jnp.exp(heights), shape[dim] // blocks).reshape((-1,) + (1,) * (len(shape) - dim - 1))

    loudness = one(*cuts[0])
    for cut in cuts[1:]:
        loudness = loudness * one(*cut)
    return loudness


def normal_values(key, dims, scale, bound, cuts=(), kind=jnp.bfloat16):
    result = jax.random.normal(key, dims, jnp.float32) * scale
    if len(cuts) > 0:
        result = block_levels(key, dims, cuts, -0.22, 0.18) * result
    return jnp.clip(result, min=-bound, max=bound).astype(kind)


def setup_inputs(seed: int = 0) -> dict:
    key_list = jax.random.split(jax.random.key(seed), 12)
    return {
        "memory": draw_memory(jax.random.fold_in(key_list[11], 71), 0),
        "frames": normal_values(key_list[1], (GROUPS, OWNERS, STREAMS, L, D), 1.0, 6.0, ((0, 8), (1, 32)), jnp.float32),
        "mem_cot": normal_values(key_list[2], (GROUPS, OWNERS, STREAMS, R, D), 0.5, 3.0, ((0, 8), (1, 32))),
        "slot_used": with_ends((jax.random.randint(key_list[3], (GROUPS, OWNERS, STREAMS), 0, 4) < 3).astype(jnp.int32), jax.random.fold_in(key_list[3], 1), 0, 1),
        "key_bias": draw_key_bias(jax.random.fold_in(key_list[11], 71), 0),
        "start_offset": with_ends(jax.random.randint(key_list[5], (GROUPS, STREAMS), 0, L * OWNERS), jax.random.fold_in(key_list[5], 1), 0, (L * OWNERS) - 1).astype(jnp.int32),
        "norm_gain": jnp.clip(1.0 + 0.1 * jax.random.normal(key_list[6], (D,), jnp.float32), 0.5, 1.5),
        "w_query": normal_values(key_list[7], (D, D), D ** -0.5, 0.21875),
        "w_key": normal_values(key_list[8], (D, D), D ** -0.5, 0.21875),
        "w_value": normal_values(key_list[9], (D, D), D ** -0.5, 0.21875),
        "w_out": normal_values(key_list[10], (D, D), D ** -0.5, 0.21875),
    }


NORM_EPSILON = 1e-06

def product(form, left, right):
    return jnp.einsum(form, left.astype(jnp.float32), right.astype(jnp.float32), precision=lax.Precision.HIGHEST)

def encoding(offsets, position, clip_len, features):
    within = jnp.arange(clip_len, dtype=jnp.int32)
    frame_time = offsets[:, None] + position * clip_len + within[None, :]
    half_width = features // 2
    frequency = 0.0625 * jnp.exp(-math.log(1000.0) * jnp.arange(half_width, dtype=jnp.float32) / half_width)
    phases = frame_time.astype(jnp.float32)[:, :, None] * frequency
    return jnp.concatenate([jnp.sin(phases), jnp.cos(phases)], axis=-1)

def recompute(memory_full, frame_rows, bias_rows, offsets, position, norm_gain, w_query, w_key, w_value):
    batch, row_count, features = memory_full.shape
    inv_rms = lax.rsqrt(lax.optimization_barrier(jnp.mean(memory_full * memory_full, axis=-1, keepdims=True)) + NORM_EPSILON)
    unit_rows = memory_full * inv_rms
    normed = (unit_rows * norm_gain).astype(jnp.bfloat16)
    key_input = (frame_rows + encoding(offsets, position, frame_rows.shape[1], features)).astype(jnp.bfloat16)
    query_proj = product('brd,de->bre', normed, w_query).astype(jnp.bfloat16)
    key_proj = product('bld,de->ble', key_input, w_key).astype(jnp.bfloat16)
    value_proj = product('bld,de->ble', key_input, w_value).astype(jnp.bfloat16)
    query_heads = query_proj.reshape(batch, row_count, H, HD)
    key_heads = key_proj.reshape(batch, -1, H, HD)
    value_heads = value_proj.reshape(batch, -1, H, HD)
    scores = product('brhd,blhd->bhrl', query_heads, key_heads) * HD ** (-0.5) + bias_rows[:, :, None, :]
    attn_prob = jax.nn.softmax(scores, axis=-1)
    attn_half = attn_prob.astype(jnp.bfloat16)
    attended = product('bhrl,blhd->brhd', attn_half, value_heads).astype(jnp.bfloat16).reshape(batch, row_count, features)
    return (inv_rms, unit_rows, normed, key_input, query_heads, key_heads, value_heads, attn_prob, attn_half, attended)

def chain_part(grad_in, slot_live, unit_rows, inv_rms, attn_prob, key_heads, value_heads, norm_gain, w_query, w_out):
    batch, row_count, features = grad_in.shape
    out_grad = (slot_live[:, None, None] * grad_in).astype(jnp.bfloat16)
    att_grad = product('bre,de->brd', out_grad, w_out).astype(jnp.bfloat16)
    att_heads = att_grad.reshape(batch, row_count, H, HD)
    prob_grad = product('brhd,blhd->bhrl', att_heads, value_heads)
    inner_sum = lax.optimization_barrier(jnp.sum(attn_prob * prob_grad, axis=-1, keepdims=True))
    score_grad = (attn_prob * (prob_grad - inner_sum) * HD ** (-0.5)).astype(jnp.bfloat16)
    query_grad = product('bhrl,blhd->brhd', score_grad, key_heads).astype(jnp.bfloat16).reshape(batch, row_count, features)
    normed_grad = product('bre,de->brd', query_grad, w_query)
    gain_term = lax.optimization_barrier(jnp.sum(normed_grad * unit_rows, axis=(0, 1)))
    scaled_grad = normed_grad * norm_gain
    passed = grad_in + inv_rms * (scaled_grad - unit_rows * lax.optimization_barrier(jnp.mean(scaled_grad * unit_rows, axis=-1, keepdims=True)))
    return (passed, out_grad, att_heads, score_grad, query_grad, gain_term)

def weight_part(normed, key_input, query_heads, attn_half, attended, out_grad, att_heads, score_grad, query_grad):
    batch, length, features = key_input.shape
    value_grad = product('bhrl,brhd->blhd', attn_half, att_heads).astype(jnp.bfloat16).reshape(batch, length, features)
    key_grad = product('bhrl,brhd->blhd', score_grad, query_heads).astype(jnp.bfloat16).reshape(batch, length, features)
    return (product('brd,bre->de', normed, query_grad), product('bld,ble->de', key_input, key_grad), product('bld,ble->de', key_input, value_grad), product('brd,bre->de', attended, out_grad))

def reference(memory, frames, mem_cot, slot_used, key_bias, start_offset, norm_gain, w_query, w_key, w_value, w_out):
    groups, owners, streams, row_count, features = memory.shape
    batch = groups * streams
    offsets = start_offset.reshape(batch)

    def take(array, owner):
        picked = lax.dynamic_index_in_dim(array, owner, 1, keepdims=False)
        return picked.reshape((batch,) + picked.shape[2:])

    def one_clip(carried, owner):
        incoming, sum_query, sum_key, sum_value, sum_out, sum_gain = carried
        parts = recompute(take(memory, owner).astype(jnp.float32), take(frames, owner), take(key_bias, owner), offsets, owner, norm_gain, w_query, w_key, w_value)
        inv_rms, unit_rows, normed, key_input, query_heads, key_heads, value_heads, attn_prob, attn_half, attended = parts
        grad_in = incoming + take(mem_cot, owner).astype(jnp.float32)
        passed, out_grad, att_heads, score_grad, query_grad, gain_term = chain_part(grad_in, take(slot_used, owner).astype(jnp.float32), unit_rows, inv_rms, attn_prob, key_heads, value_heads, norm_gain, w_query, w_out)
        weight_terms = weight_part(normed, key_input, query_heads, attn_half, attended, out_grad, att_heads, score_grad, query_grad)
        return ((passed, sum_query + weight_terms[0], sum_key + weight_terms[1], sum_value + weight_terms[2], sum_out + weight_terms[3], sum_gain + gain_term), passed)
    zero_square = jnp.zeros((features, features), jnp.float32)
    start = (jnp.zeros((batch, row_count, features), jnp.float32), zero_square, zero_square, zero_square, zero_square, jnp.zeros((features,), jnp.float32))
    owner_order = jnp.arange(owners - 1, -1, -1, dtype=jnp.int32)
    final, stacked = lax.scan(one_clip, start, owner_order)
    grad_memory = jnp.flip(stacked, 0).reshape(owners, groups, streams, row_count, features).transpose(1, 0, 2, 3, 4)
    mean_scale = 1.0 / (groups * owners * streams)
    return (grad_memory, final[1] * mean_scale, final[2] * mean_scale, final[3] * mean_scale, final[4] * mean_scale, final[5] * mean_scale)
```

```python
import math

import jax
import jax.numpy as jnp
from jax import lax
from jax.experimental import pallas as pl
from jax.experimental.pallas import tpu as pltpu
from jax.sharding import PartitionSpec as P

D = 768
H = 12
HD = 64
R = 64
L = 128
NORM_EPSILON = 1e-06
SCALE = HD ** (-0.5)
BF = jnp.bfloat16
F32 = jnp.float32
AXES = ("tm", "video")
GROUPS_TM = 8
ROWS = 16
INTERPRET = False


def dot(left, right, form=((1,), (0,))):
    return lax.dot_general(left, right, (form, ((), ())), preferred_element_type=F32)


def lane_head(rows, lanes):
    return lax.broadcasted_iota(jnp.int32, (rows, lanes), 1) // HD


def spread_heads(value, heads, base=0):
    which = lane_head(*value.shape)
    zero = jnp.zeros_like(value)
    parts = [jnp.where(which == base + h, value, zero) for h in range(heads)]
    return jnp.concatenate(parts, axis=0)


def merge_heads(value, heads, rows):
    which = lane_head(rows, value.shape[1])
    total = jnp.where(which == 0, value[:rows], 0.0)
    for h in range(1, heads):
        total = jnp.where(which == h, value[h * rows : (h + 1) * rows], total)
    return total


def prep_kernel(
    rank, x0, x1, x2, x3, enc, gain, w_query, w_key, w_value,
    key_in, keys, values, values_t, normed, queries, attended, prob,
    unit_rows, inv_rows, cot_rows, prob_rows, slots,
):
    r = rank[0]
    first = pl.multiple_of(r * ROWS, ROWS)
    for s, x in enumerate((x0, x1, x2, x3)):
        k = jnp.bitwise_xor(r, s)
        rounded = (x[0:L] + enc[s]).astype(BF)
        key_in[k] = rounded
        mem = x[L : L + R]
        inv = lax.rsqrt(jnp.mean(mem * mem, axis=-1, keepdims=True) + NORM_EPSILON)
        norm = (mem * inv * gain[...]).astype(BF)
        normed[k] = norm
        few = x[pl.ds(L + first, ROWS)]
        few_inv = lax.rsqrt(jnp.mean(few * few, axis=-1, keepdims=True) + NORM_EPSILON)
        unit_rows[k] = few * few_inv
        inv_rows[k] = jnp.broadcast_to(few_inv, (ROWS, 128))
        cot_rows[k] = x[pl.ds(L + R + first, ROWS)]
        slots[k] = jnp.broadcast_to(x[L + 2 * R + 2 : L + 2 * R + 3], (8, D))
        key_f = dot(rounded, w_key[...])
        value_f = dot(rounded, w_value[...])
        query_f = dot(norm, w_query[...])
        key_b = key_f.astype(BF)
        value_b = value_f.astype(BF)
        keys[k] = key_b
        values[k] = value_b
        values_t[k] = value_f.T.astype(BF)
        queries[k] = query_f.astype(BF)
        for j in range(3):
            tile = slice(256 * j, 256 * j + 256)
            spread = spread_heads(query_f[:, tile], 4).astype(BF)
            scores = dot(spread, key_b[:, tile], ((1,), (1,))) * SCALE
            bias = []
            for h in range(4 * j, 4 * j + 4):
                row = L + 2 * R + h // 6
                lane = (h % 6) * 128
                bias.append(jnp.broadcast_to(x[row : row + 1, lane : lane + 128], (R, L)))
            scores = scores + jnp.concatenate(bias, axis=0)
            top = jnp.max(scores, axis=-1, keepdims=True)
            raised = jnp.exp(scores - top)
            probs = raised / jnp.sum(raised, axis=-1, keepdims=True)
            prob[k, 4 * j : 4 * j + 4] = probs.reshape(4, R, L)
            read = dot(probs.astype(BF), value_b[:, tile])
            attended[k, :, tile] = merge_heads(read, 4, R).astype(BF)
        prob_rows[k] = prob[k, :, pl.ds(first, ROWS), :]


def chain_kernel(
    info, incoming, keys, values_t, unit_rows, inv_rows, cot_rows, prob_rows, slots,
    w_out_t, w_query_t, gain, gin_before, passed_before, gacc_before,
    sending, gin_all, passed_all, gacc,
):
    @pl.when(info[0] == 0)
    def _():
        sending[...] = jnp.zeros_like(sending)
        gin_all[...] = gin_before[...]
        passed_all[...] = passed_before[...]
        gacc[...] = gacc_before[...]

    @pl.when(info[0] != 0)
    def _():
        carried = incoming[...]
        total = jnp.zeros((ROWS, D), F32)
        for k in (3, 2, 1, 0):
            grad_in = carried + cot_rows[k]
            gin_all[k] = grad_in
            out_grad = (grad_in * slots[k, 0:1]).astype(BF)
            att = dot(out_grad, w_out_t[...])
            query = []
            for j in range(3):
                tile = slice(256 * j, 256 * j + 256)
                spread = spread_heads(att[:, tile], 4).astype(BF)
                prob_grad = dot(spread, values_t[k, tile])
                prob = prob_rows[k, 4 * j : 4 * j + 4].reshape(4 * ROWS, L)
                inner = jnp.sum(prob * prob_grad, axis=-1, keepdims=True)
                score = (prob * (prob_grad - inner) * SCALE).astype(BF)
                query.append(merge_heads(dot(score, keys[k, :, tile]), 4, ROWS).astype(BF))
            normed_grad = dot(jnp.concatenate(query, axis=1), w_query_t[...])
            unit = unit_rows[k]
            total = total + normed_grad * unit
            scaled = normed_grad * gain[...]
            mean = jnp.mean(scaled * unit, axis=-1, keepdims=True)
            carried = grad_in + inv_rows[k, :, 0:1] * (scaled - unit * mean)
            passed_all[k] = carried
        sending[...] = carried
        gacc[...] = total[0:8] + total[8:16]


def weight_kernel(
    rank, t0, t1, t2, t3, p0, p1, p2, p3, slots, wo_cols, pick_cols,
    keys_pad, values_pad, queries_pad, prob, key_in, normed, attended,
    grad_memory, send_a, send_b,
    gin, qg, kg, vg,
):
    r = rank[0]
    gain = jnp.zeros((8, D), F32)
    for s, (t, p) in enumerate(((t0, p0), (t1, p1), (t2, p2), (t3, p3))):
        first = pl.multiple_of(jnp.bitwise_xor(r, s) * ROWS, ROWS)
        for k in range(4):
            gin[k, pl.ds(first, ROWS)] = t[16 * k : 16 * k + 16] * slots[k, 0:1]
        grad_memory[pl.ds(first, ROWS)] = p[...]
        gain = gain + t[64:72]
    gain = jnp.sum(gain, axis=0, keepdims=True)
    out_grad = gin[...].reshape(4 * R, D).astype(BF)
    att = dot(out_grad, wo_cols[...])
    picked = dot(out_grad, pick_cols[...]).astype(BF)
    for k in range(4):
        spread = spread_heads(att[R * k : R * k + R], 3).astype(BF)
        prob_grad = dot(spread, values_pad[k], ((1,), (1,)))
        probs = prob[k, pl.ds(3 * r, 3)].reshape(3 * R, L)
        inner = jnp.sum(probs * prob_grad, axis=-1, keepdims=True)
        score = (probs * (prob_grad - inner) * SCALE).astype(BF)
        read = dot(score, keys_pad[k])
        qg[R * k : R * k + R] = merge_heads(read, 3, R).astype(BF)
        vg[L * k : L * k + L] = dot(probs.astype(BF), spread, ((0,), (0,))).astype(BF)
        q_spread = spread_heads(queries_pad[k].astype(F32), 3, 3).astype(BF)
        kg[L * k : L * k + L] = dot(score, q_spread, ((0,), (0,))).astype(BF)
    inputs = key_in[...].reshape(4 * L, D)
    both = dot(normed[...].reshape(4 * R, D), qg[...], ((0,), (0,)))
    both = both + dot(inputs, kg[...], ((0,), (0,)))
    for a in range(32):
        y, zp, ra = a // 8, (a // 4) % 2, a % 4
        place = y * 48 + zp * 24
        send_a[ra, place : place + 24] = both[24 * a : 24 * a + 24]
    tail = jnp.concatenate(
        [gain[:, 0:384], gain[:, 384:768], jnp.zeros((6, 384), F32)], axis=0
    )
    for ra in range(4):
        send_a[ra, 192:200] = tail
    both = dot(inputs, vg[...], ((0,), (0,)))
    both = both + dot(attended[...].reshape(4 * R, D), picked, ((0,), (0,)))
    send_b[...] = both.reshape(4, 192, 384)


def shape(*dims, dtype=F32):
    return jax.ShapeDtypeStruct(dims, dtype)


def run(kernel, args, outs, scratch=(), aliases=None, flops=0, nbytes=0):
    smem = pl.BlockSpec(memory_space=pltpu.SMEM)
    vmem = pl.BlockSpec(memory_space=pltpu.VMEM)
    return pl.pallas_call(
        kernel,
        out_shape=outs,
        in_specs=[smem] + [vmem] * (len(args) - 1),
        out_specs=[vmem] * len(outs),
        scratch_shapes=list(scratch),
        input_output_aliases=aliases or {},
        interpret=INTERPRET,
        compiler_params=pltpu.CompilerParams(vmem_limit_bytes=48 * 1024 * 1024),
        cost_estimate=pl.CostEstimate(flops=flops, bytes_accessed=nbytes, transcendentals=0),
    )(*args)


def encoding(offset, clip, length, features):
    frame_time = offset + clip * length + jnp.arange(length, dtype=jnp.int32)
    half = features // 2
    frequency = 0.0625 * jnp.exp(-math.log(1000.0) * jnp.arange(half, dtype=F32) / half)
    phases = frame_time.astype(F32)[:, None] * frequency
    return jnp.concatenate([jnp.sin(phases), jnp.cos(phases)], axis=-1)


def flat(y, zp, r, x, h):
    return (y * 8 + zp * 4 + r) * 8 + x * 2 + h


def pairs(move):
    out = []
    for y in range(4):
        for zp in range(2):
            for r in range(4):
                for x in range(4):
                    for h in range(2):
                        to = move(y, zp, r, x, h)
                        if to is not None:
                            out.append((flat(y, zp, r, x, h), flat(*to)))
    return out


def send(value, move):
    return lax.ppermute(value, AXES, pairs(move))


def swap_core(value):
    return send(value, lambda y, zp, r, x, h: (y, zp, r ^ 1, x, h))


def swap_z(value):
    return send(value, lambda y, zp, r, x, h: (y, zp, r ^ 2, x, h))


def to_next(value, group):
    def move(y, zp, r, x, h):
        if y * 2 + zp != group:
            return None
        return ((group - 1) // 2, (group - 1) % 2, r, x, h)

    return send(value, move)


def pick(array, index):
    return lax.dynamic_index_in_dim(array, index, 0, keepdims=False)


def on_device(
    memory, frames, mem_cot, slot_used, key_bias, start_offset,
    norm_gain, w_query, w_key, w_value, w_out,
):
    position = lax.axis_index("tm")
    video = lax.axis_index("video")
    group = position // 4
    r = position % 4
    core = position % 2
    y, zp = position // 8, (position // 4) % 2
    x, h = video // 2, video % 2
    rank = r[None].astype(jnp.int32)

    slot_row = jnp.full((6, D), slot_used[0, 0, 0], jnp.int32).astype(F32)
    own = jnp.concatenate(
        [
            frames[0, 0, 0],
            memory[0, 0, 0].astype(F32),
            mem_cot[0, 0, 0].astype(F32),
            key_bias[0, 0, 0].reshape(2, D),
            slot_row,
        ],
        axis=0,
    )
    from_z = swap_z(own)
    from_core = swap_core(own)
    from_both = swap_core(from_z)
    enc = jnp.stack(
        [encoding(start_offset[0, 0], 4 * group + (r ^ s), L, D) for s in range(4)]
    )
    gain = norm_gain[None]
    w_out_t = w_out.T
    w_query_t = w_query.T

    (
        key_in, keys, values, values_t, normed, queries, attended, prob,
        unit_rows, inv_rows, cot_rows, prob_rows, slots,
    ) = run(
        prep_kernel,
        (rank, own, from_core, from_z, from_both, enc, gain, w_query, w_key, w_value),
        [
            shape(4, L, D, dtype=BF), shape(4, L, D, dtype=BF), shape(4, L, D, dtype=BF),
            shape(4, D, L, dtype=BF), shape(4, R, D, dtype=BF), shape(4, R, D, dtype=BF),
            shape(4, R, D, dtype=BF), shape(4, H, R, L),
            shape(4, ROWS, D), shape(4, ROWS, 128), shape(4, ROWS, D),
            shape(4, H, ROWS, L), shape(4, 8, D),
        ],
        flops=2 * 10**9, nbytes=10**7,
    )

    gin_all = jnp.zeros((4, ROWS, D), F32)
    passed_all = jnp.zeros((4, ROWS, D), F32)
    gacc = jnp.zeros((8, D), F32)
    incoming = jnp.zeros((ROWS, D), F32)
    for turn in range(GROUPS_TM):
        active = GROUPS_TM - 1 - turn
        info = (group == active).astype(jnp.int32)[None]
        sending, gin_all, passed_all, gacc = run(
            chain_kernel,
            (
                info, incoming, keys, values_t, unit_rows, inv_rows, cot_rows,
                prob_rows, slots, w_out_t, w_query_t, gain, gin_all, passed_all, gacc,
            ),
            [shape(ROWS, D), shape(4, ROWS, D), shape(4, ROWS, D), shape(8, D)],
            aliases={12: 1, 13: 2, 14: 3},
            flops=10**9, nbytes=5 * 10**6,
        )
        if active > 0:
            incoming = to_next(sending, active)

    start = 192 * r
    zero_cols = jnp.zeros((4, L, 192), BF)
    keys_pad = jnp.concatenate([lax.dynamic_slice_in_dim(keys, start, 192, 2), zero_cols], 2)
    values_pad = jnp.concatenate([lax.dynamic_slice_in_dim(values, start, 192, 2), zero_cols], 2)
    queries_pad = jnp.concatenate(
        [zero_cols[:, :R], lax.dynamic_slice_in_dim(queries, start, 192, 2)], 2
    )
    zero_half = jnp.zeros((D, 192), BF)
    wo_cols = jnp.concatenate([lax.dynamic_slice_in_dim(w_out_t, start, 192, 1), zero_half], 1)
    row_id = lax.broadcasted_iota(jnp.int32, (D, 384), 0)
    lane_id = lax.broadcasted_iota(jnp.int32, (D, 384), 1)
    pick_cols = (row_id - start == lane_id - 192).astype(BF)
    pick_cols = jnp.where(lane_id >= 192, pick_cols, jnp.zeros_like(pick_cols))

    flat_gin = gin_all.reshape(4 * ROWS, D)
    t_own = jnp.concatenate([flat_gin, gacc], axis=0)
    other = lax.dynamic_slice_in_dim(passed_all, 2 * (1 - r // 2), 2, 0).reshape(2 * ROWS, D)
    z_got = swap_z(jnp.concatenate([t_own, other], axis=0))
    z_pass = z_got[72:].reshape(2, ROWS, D)
    core_send = jnp.concatenate(
        [t_own, pick(passed_all, r ^ 1), z_got[:72], pick(z_pass, 1 - core)], axis=0
    )
    core_got = swap_core(core_send)
    grad_memory, send_a, send_b = run(
        weight_kernel,
        (
            rank, t_own, core_got[:72], z_got[:72], core_got[88:160],
            pick(passed_all, r), core_got[72:88], pick(z_pass, core), core_got[160:176],
            slots, wo_cols, pick_cols, keys_pad, values_pad, queries_pad,
            prob, key_in, normed, attended,
        ),
        [shape(R, D), shape(4, 200, 384), shape(4, 192, 384)],
        scratch=[
            pltpu.VMEM((4, R, D), F32), pltpu.VMEM((4 * R, 384), BF),
            pltpu.VMEM((4 * L, 384), BF), pltpu.VMEM((4 * L, 384), BF),
        ],
        flops=2 * 10**9, nbytes=10**7,
    )

    def over_x(chunks):
        total = None
        for s in range(4):
            got = send(
                pick(chunks, x ^ s), lambda yy, zz, rr, xx, hh, s=s: (yy, zz, xx ^ s, rr, hh)
            )
            total = got if total is None else total + got
        return total

    def over_y(chunks):
        total = pick(chunks, y)
        for s in range(1, 4):
            total = total + send(
                pick(chunks, (y + s) % 4),
                lambda yy, zz, rr, xx, hh, s=s: ((yy + s) % 4, zz, rr, xx, hh),
            )
        return total

    half_a = over_x(send_a)
    half_b = over_y(send_b)
    chunks_a = jnp.concatenate(
        [half_a[:192].reshape(4, 48, 384), jnp.broadcast_to(half_a[None, 192:], (4, 8, 384))],
        axis=1,
    )
    half_a = over_y(chunks_a)
    half_b = over_x(half_b.reshape(2, 4, 24, 384).transpose(1, 0, 2, 3))
    by_zp = jnp.concatenate(
        [half_a[:48].reshape(2, 24, 2, 2, 96), half_b.reshape(2, 24, 2, 2, 96)], axis=2
    )
    chunks = by_zp.transpose(0, 3, 1, 2, 4).reshape(4, 24, 384)
    chunks = jnp.concatenate([chunks, jnp.broadcast_to(half_a[None, 48:], (4, 8, 384))], axis=1)
    here = zp * 2 + h
    total = pick(chunks, here)
    for s in range(1, 4):
        total = total + send(
            pick(chunks, here ^ s),
            lambda yy, zz, rr, xx, hh, s=s: (yy, zz ^ (s // 2), rr, xx, hh ^ (s % 2)),
        )
    total = total * (1.0 / 256.0)
    return (
        grad_memory[None, None, None],
        total[:24, 0:96],
        total[:24, 96:192],
        total[:24, 192:288],
        total[:24, 288:384],
        total[24:26].reshape(D),
    )


def solution(mesh):
    return jax.shard_map(
        on_device,
        mesh=mesh,
        in_specs=(
            P("video", "tm", None, None, None),
            P("video", "tm", None, None, None),
            P("video", "tm", None, None, None),
            P("video", "tm", None),
            P("video", "tm", None, None, None),
            P("video", None),
            P(),
            P(),
            P(),
            P(),
            P(),
        ),
        out_specs=(
            P("video", "tm", None, None, None),
            P("tm", "video"),
            P("tm", "video"),
            P("tm", "video"),
            P("tm", "video"),
            P(),
        ),
        check_vma=False,
    )
```

```python
import math

import jax
import jax.numpy as jnp
from jax import lax
from jax.experimental import pallas as pl
from jax.experimental.pallas import tpu as pltpu
from jax.sharding import PartitionSpec as P

D = 768
H = 12
HD = 64
R = 64
L = 128
NORM_EPSILON = 1e-06
SCALE = HD ** (-0.5)
BF = jnp.bfloat16
F32 = jnp.float32
AXES = ("tm", "video")
GROUPS_TM = 8
ROWS = 16
INTERPRET = False


def dot(left, right, form=((1,), (0,))):
    return lax.dot_general(left, right, (form, ((), ())), preferred_element_type=F32)


def lane_head(rows, lanes):
    return lax.broadcasted_iota(jnp.int32, (rows, lanes), 1) // HD


def spread_heads(value, heads, base=0):
    which = lane_head(*value.shape)
    zero = jnp.zeros_like(value)
    parts = [jnp.where(which == base + h, value, zero) for h in range(heads)]
    return jnp.concatenate(parts, axis=0)


def merge_heads(value, heads, rows):
    which = lane_head(rows, value.shape[1])
    total = jnp.where(which == 0, value[:rows], 0.0)
    for h in range(1, heads):
        total = jnp.where(which == h, value[h * rows : (h + 1) * rows], total)
    return total


def prep_kernel(
    info, frames_a, pack_a, frames_b, pack_b, enc, gain, w_query, w_key, w_value,
    key_in, keys, values, values_t, unit_rows, inv_rows, cot_rows, prob_rows, slots,
):
    core = info[0]
    place = (core, 1 - core)
    tokens = jnp.concatenate([frames_a[...] + enc[0], frames_b[...] + enc[1]], axis=0).astype(BF)
    mem = jnp.concatenate([pack_a[0:ROWS], pack_b[0:ROWS]], axis=0)
    inv = lax.rsqrt(jnp.mean(mem * mem, axis=-1, keepdims=True) + NORM_EPSILON)
    unit = mem * inv
    query_f = dot((unit * gain[...]).astype(BF), w_query[...])
    key_b = dot(tokens, w_key[...]).astype(BF)
    value_f = dot(tokens, w_value[...])
    inv_wide = jnp.broadcast_to(inv, (2 * ROWS, 128))
    for i, pack in enumerate((pack_a, pack_b)):
        k = place[i]
        row = slice(ROWS * i, ROWS * i + ROWS)
        token = slice(L * i, L * i + L)
        key_in[k] = tokens[token]
        keys[k] = key_b[token]
        values[k] = value_f[token].astype(BF)
        values_t[k] = value_f[token].T.astype(BF)
        unit_rows[k] = unit[row]
        inv_rows[k] = inv_wide[row]
        cot_rows[k] = pack[ROWS : 2 * ROWS]
        slots[k] = jnp.broadcast_to(pack[34:35], (8, D))
        for j in range(3):
            tile = slice(256 * j, 256 * j + 256)
            spread = spread_heads(query_f[row, tile], 4).astype(BF)
            probs = attend(spread, key_b[token, tile], pack, 32, j, ROWS)
            prob_rows[k, 4 * j : 4 * j + 4] = probs.reshape(4, ROWS, L)


def attend(spread, key_tile, pack, base, j, rows):
    scores = dot(spread, key_tile, ((1,), (1,))) * SCALE
    bias = []
    for h in range(4 * j, 4 * j + 4):
        row = base + h // 6
        lane = (h % 6) * 128
        bias.append(jnp.broadcast_to(pack[row : row + 1, lane : lane + 128], (rows, L)))
    scores = scores + jnp.concatenate(bias, axis=0)
    top = jnp.max(scores, axis=-1, keepdims=True)
    raised = jnp.exp(scores - top)
    return raised / jnp.sum(raised, axis=-1, keepdims=True)


def whole_kernel(
    info, m0, m1, m2, m3, pack0, pack1, pack2, pack3, keys_a, values_a, keys_b, values_b,
    gain, w_query,
    normed, queries, attended, prob_mine, prob,
):
    core, r = info[0], info[1]
    for s, (mem_ref, pack) in enumerate(((m0, pack0), (m1, pack1), (m2, pack2), (m3, pack3))):
        keys, values = ((keys_a, values_a), (keys_b, values_b))[s // 2]
        place = core if s % 2 == 0 else 1 - core
        m = 2 * (s // 2) + place
        mem = mem_ref[...]
        inv = lax.rsqrt(jnp.mean(mem * mem, axis=-1, keepdims=True) + NORM_EPSILON)
        norm = (mem * inv * gain[...]).astype(BF)
        normed[m] = norm
        query_f = dot(norm, w_query[...])
        queries[m] = query_f.astype(BF)
        for j in range(3):
            tile = slice(256 * j, 256 * j + 256)
            spread = spread_heads(query_f[:, tile], 4).astype(BF)
            probs = attend(spread, keys[place, :, tile], pack, 32, j, R)
            prob[4 * j : 4 * j + 4] = probs.reshape(4, R, L)
            read = dot(probs.astype(BF), values[place, :, tile])
            attended[m, :, tile] = merge_heads(read, 4, R).astype(BF)
        prob_mine[m] = prob[pl.ds(3 * r, 3)]


def chain_kernel(
    info, incoming,
    keys_a, values_t_a, unit_a, inv_a, cot_a, prob_a, slots_a,
    keys_b, values_t_b, unit_b, inv_b, cot_b, prob_b, slots_b,
    w_out_t, w_query_t, gain, gin_before, passed_before, gacc_before,
    sending, gin_all, passed_all, gacc,
):
    own = (keys_a, values_t_a, unit_a, inv_a, cot_a, prob_a, slots_a)
    other = (keys_b, values_t_b, unit_b, inv_b, cot_b, prob_b, slots_b)

    def walk(order):
        carried = incoming[...]
        total = jnp.zeros((ROWS, D), F32)
        for k in (3, 2, 1, 0):
            keys, values_t, unit_ref, inv_ref, cot, prob_ref, slots = order[1 - k // 2]
            c = k % 2
            grad_in = carried + cot[c]
            gin_all[k] = grad_in
            out_grad = (grad_in * slots[c, 0:1]).astype(BF)
            att = dot(out_grad, w_out_t[...])
            query = []
            for j in range(3):
                tile = slice(256 * j, 256 * j + 256)
                spread = spread_heads(att[:, tile], 4).astype(BF)
                prob_grad = dot(spread, values_t[c, tile])
                prob = prob_ref[c, 4 * j : 4 * j + 4].reshape(4 * ROWS, L)
                inner = jnp.sum(prob * prob_grad, axis=-1, keepdims=True)
                score = (prob * (prob_grad - inner) * SCALE).astype(BF)
                query.append(merge_heads(dot(score, keys[c, :, tile]), 4, ROWS).astype(BF))
            normed_grad = dot(jnp.concatenate(query, axis=1), w_query_t[...])
            unit = unit_ref[c]
            total = total + normed_grad * unit
            scaled = normed_grad * gain[...]
            mean = jnp.mean(scaled * unit, axis=-1, keepdims=True)
            carried = grad_in + inv_ref[c, :, 0:1] * (scaled - unit * mean)
            passed_all[k] = carried
        sending[...] = carried
        gacc[...] = total[0:8] + total[8:16]

    @pl.when(info[0] == 0)
    def _():
        sending[...] = jnp.zeros_like(sending)
        gin_all[...] = gin_before[...]
        passed_all[...] = passed_before[...]
        gacc[...] = gacc_before[...]

    @pl.when((info[0] != 0) & (info[1] == 1))
    def _():
        walk((own, other))

    @pl.when((info[0] != 0) & (info[1] == 0))
    def _():
        walk((other, own))


def weight_kernel(
    info, t0, t1, t2, t3, p0, p1, p2, p3, slots_a, slots_b, wo_cols, pick_cols,
    keys_pad, values_pad, queries_pad, prob, key_in_a, key_in_b, normed, attended,
    grad_memory, send_a, send_b,
    gin, qg, kg, vg,
):
    r, zb, x, y = info[0], info[1], info[2], info[3]
    gain = jnp.zeros((8, D), F32)
    for s, (t, p) in enumerate(((t0, p0), (t1, p1), (t2, p2), (t3, p3))):
        first = pl.multiple_of(jnp.bitwise_xor(r, s) * ROWS, ROWS)
        for m in range(4):
            k = 2 * jnp.bitwise_xor(zb, m // 2) + m % 2
            slot = (slots_a, slots_b)[m // 2][m % 2, 0:1]
            gin[m, pl.ds(first, ROWS)] = t[pl.ds(pl.multiple_of(k * ROWS, ROWS), ROWS)] * slot
        grad_memory[pl.ds(first, ROWS)] = p[...]
        gain = gain + t[64:72]
    gain = jnp.sum(gain, axis=0, keepdims=True)
    out_grad = gin[...].reshape(4 * R, D).astype(BF)
    att = dot(out_grad, wo_cols[...])
    picked = dot(out_grad, pick_cols[...]).astype(BF)
    for k in range(4):
        spread = spread_heads(att[R * k : R * k + R], 3).astype(BF)
        prob_grad = dot(spread, values_pad[k], ((1,), (1,)))
        probs = prob[k].reshape(3 * R, L)
        inner = jnp.sum(probs * prob_grad, axis=-1, keepdims=True)
        score = (probs * (prob_grad - inner) * SCALE).astype(BF)
        read = dot(score, keys_pad[k])
        qg[R * k : R * k + R] = merge_heads(read, 3, R).astype(BF)
        vg[L * k : L * k + L] = dot(probs.astype(BF), spread, ((0,), (0,))).astype(BF)
        q_spread = spread_heads(queries_pad[k].astype(F32), 3, 3).astype(BF)
        kg[L * k : L * k + L] = dot(score, q_spread, ((0,), (0,))).astype(BF)
    inputs = jnp.concatenate(
        [key_in_a[...].reshape(2 * L, D), key_in_b[...].reshape(2 * L, D)], axis=0
    )
    both = dot(normed[...].reshape(4 * R, D), qg[...], ((0,), (0,)))
    both = both + dot(inputs, kg[...], ((0,), (0,)))
    tail = jnp.concatenate(
        [gain[:, 0:384], gain[:, 384:768], jnp.zeros((6, 384), F32)], axis=0
    )
    for ra in range(4):
        at = jnp.bitwise_and(ra - x, 3)
        for yz in range(8):
            a = yz * 4 + ra
            send_a[at, 24 * yz : 24 * yz + 24] = both[24 * a : 24 * a + 24]
        send_a[at, 192:200] = tail
    both = dot(inputs, vg[...], ((0,), (0,)))
    both = both + dot(attended[...].reshape(4 * R, D), picked, ((0,), (0,)))
    for ya in range(4):
        send_b[jnp.bitwise_and(ya - y, 3)] = both[192 * ya : 192 * ya + 192]


def shape(*dims, dtype=F32):
    return jax.ShapeDtypeStruct(dims, dtype)


def run(kernel, args, outs, scratch=(), aliases=None, flops=0, nbytes=0, limit=16):
    smem = pl.BlockSpec(memory_space=pltpu.SMEM)
    vmem = pl.BlockSpec(memory_space=pltpu.VMEM)
    return pl.pallas_call(
        kernel,
        out_shape=outs,
        in_specs=[smem] + [vmem] * (len(args) - 1),
        out_specs=[vmem] * len(outs),
        scratch_shapes=list(scratch),
        input_output_aliases=aliases or {},
        interpret=INTERPRET,
        compiler_params=pltpu.CompilerParams(vmem_limit_bytes=limit * 1024 * 1024),
        cost_estimate=pl.CostEstimate(flops=flops, bytes_accessed=nbytes, transcendentals=0),
    )(*args)


def encoding(offset, clip, length, features):
    frame_time = offset + clip * length + jnp.arange(length, dtype=jnp.int32)
    half = features // 2
    frequency = 0.0625 * jnp.exp(-math.log(1000.0) * jnp.arange(half, dtype=F32) / half)
    phases = frame_time.astype(F32)[:, None] * frequency
    return jnp.concatenate([jnp.sin(phases), jnp.cos(phases)], axis=-1)


def flat(y, zp, r, x, h):
    return (y * 8 + zp * 4 + r) * 8 + x * 2 + h


def pairs(move):
    out = []
    for y in range(4):
        for zp in range(2):
            for r in range(4):
                for x in range(4):
                    for h in range(2):
                        to = move(y, zp, r, x, h)
                        if to is not None:
                            out.append((flat(y, zp, r, x, h), flat(*to)))
    return out


def send(value, move):
    return lax.ppermute(value, AXES, pairs(move))


def swap_core(value):
    return send(value, lambda y, zp, r, x, h: (y, zp, r ^ 1, x, h))


def swap_z(value):
    return send(value, lambda y, zp, r, x, h: (y, zp, r ^ 2, x, h))


def to_next(value, group):
    def move(y, zp, r, x, h):
        if y * 2 + zp != group:
            return None
        return ((group - 1) // 2, (group - 1) % 2, r, x, h)

    return send(value, move)


def pick(array, index):
    return lax.dynamic_index_in_dim(array, index, 0, keepdims=False)


def on_device(
    memory, frames, mem_cot, slot_used, key_bias, start_offset,
    norm_gain, w_query, w_key, w_value, w_out,
):
    position = lax.axis_index("tm")
    video = lax.axis_index("video")
    group = position // 4
    r = position % 4
    core = position % 2
    y, zp = position // 8, (position // 4) % 2
    x, h = video // 2, video % 2
    zb = r // 2
    at_cores = jnp.stack([core, r]).astype(jnp.int32)

    slot_row = jnp.full((6, D), slot_used[0, 0, 0], jnp.int32).astype(F32)
    own_frames = frames[0, 0, 0]
    own_mem = memory[0, 0, 0].astype(F32)
    own_cot = mem_cot[0, 0, 0].astype(F32)
    ends = jnp.concatenate([key_bias[0, 0, 0].reshape(2, D), slot_row], axis=0)

    def rows_of(array, start, count):
        return lax.dynamic_slice_in_dim(array, start, count, 0)

    def pack_for(member):
        return jnp.concatenate(
            [rows_of(own_mem, ROWS * member, ROWS), rows_of(own_cot, ROWS * member, ROWS), ends],
            axis=0,
        )

    far = 2 * ROWS * (1 - zb)
    z_send = jnp.concatenate(
        [rows_of(own_mem, far, 2 * ROWS), rows_of(own_cot, far, 2 * ROWS), ends], axis=0
    )
    frames_z = swap_z(own_frames)
    z_got = swap_z(z_send)
    frames_c = swap_core(own_frames)
    pack_c = swap_core(pack_for(r ^ 1))

    def z_pack(c):
        return jnp.concatenate(
            [rows_of(z_got, ROWS * c, ROWS), rows_of(z_got, 32 + ROWS * c, ROWS), z_got[64:]],
            axis=0,
        )

    enc = [encoding(start_offset[0, 0], 4 * group + (r ^ s), L, D) for s in range(4)]
    enc_a = jnp.stack(enc[:2])
    enc_b = jnp.stack(enc[2:])
    w_out_t = w_out.T
    w_query_t = w_query.T
    gain = norm_gain[None]
    pack_own = pack_for(r)

    def prep(frames_0, pack_0, frames_1, pack_1, enc_pair):
        return run(
            prep_kernel,
            (
                at_cores, frames_0, pack_0, frames_1, pack_1, enc_pair, gain,
                w_query, w_key, w_value,
            ),
            [
                shape(2, L, D, dtype=BF), shape(2, L, D, dtype=BF), shape(2, L, D, dtype=BF),
                shape(2, D, L, dtype=BF), shape(2, ROWS, D), shape(2, ROWS, 128),
                shape(2, ROWS, D), shape(2, H, ROWS, L), shape(2, 8, D),
            ],
            flops=10**9, nbytes=8 * 10**6, limit=20,
        )

    pair_a = prep(own_frames, pack_own, frames_c, pack_c, enc_a)
    frames_z, z_got, enc_b, w_out_t, w_query_t, _ = lax.optimization_barrier(
        (frames_z, z_got, enc_b, w_out_t, w_query_t, pair_a[8])
    )
    frames_cz = swap_core(frames_z)
    pack_z = z_pack(core)
    pack_cz = swap_core(z_pack(1 - core))
    pair_b = prep(frames_z, pack_z, frames_cz, pack_cz, enc_b)
    mem_late, _ = lax.optimization_barrier((own_mem, frames_cz))
    mem_z = swap_z(mem_late)
    mem_c = swap_core(mem_late)
    mem_cz = swap_core(mem_z)

    gin_all = jnp.zeros((4, ROWS, D), F32)
    passed_all = jnp.zeros((4, ROWS, D), F32)
    gacc = jnp.zeros((8, D), F32)
    incoming = jnp.zeros((ROWS, D), F32)
    chain_a = (pair_a[1],) + tuple(pair_a[3:])
    chain_b = (pair_b[1],) + tuple(pair_b[3:])
    start = 192 * r
    for turn in range(GROUPS_TM):
        active = GROUPS_TM - 1 - turn
        info = jnp.stack([(group == active).astype(jnp.int32), zb.astype(jnp.int32)])
        sending, gin_all, passed_all, gacc = run(
            chain_kernel,
            (info, incoming)
            + chain_a
            + chain_b
            + (w_out_t, w_query_t, gain, gin_all, passed_all, gacc),
            [shape(ROWS, D), shape(4, ROWS, D), shape(4, ROWS, D), shape(8, D)],
            aliases={19: 1, 20: 2, 21: 3},
            flops=2 * 10**9, nbytes=5 * 10**6, limit=12,
        )
        if active > 0:
            incoming = to_next(sending, active)
        if turn == 0:
            mems = lax.optimization_barrier((own_mem, mem_c, mem_z, mem_cz, sending))[:4]
            normed, queries, attended, prob = run(
                whole_kernel,
                (at_cores,)
                + tuple(mems)
                + (
                    pack_own, pack_c, pack_z, pack_cz,
                    pair_a[1], pair_a[2], pair_b[1], pair_b[2], gain, w_query,
                ),
                [
                    shape(4, R, D, dtype=BF), shape(4, R, D, dtype=BF),
                    shape(4, R, D, dtype=BF), shape(4, 3, R, L),
                ],
                scratch=[pltpu.VMEM((H, R, L), F32)],
                flops=10**9, nbytes=8 * 10**6, limit=16,
            )
            zero_cols = jnp.zeros((4, L, 192), BF)

            def mine(array):
                return lax.dynamic_slice_in_dim(array, start, 192, array.ndim - 1)

            def both_pairs(index):
                return jnp.concatenate([mine(pair_a[index]), mine(pair_b[index])], axis=0)

            keys_pad = jnp.concatenate([both_pairs(1), zero_cols], 2)
            values_pad = jnp.concatenate([both_pairs(2), zero_cols], 2)
            queries_pad = jnp.concatenate([zero_cols[:, :R], mine(queries)], 2)
            wo_cols = jnp.concatenate([mine(w_out_t), jnp.zeros((D, 192), BF)], 1)
            row_id = lax.broadcasted_iota(jnp.int32, (D, 384), 0)
            lane_id = lax.broadcasted_iota(jnp.int32, (D, 384), 1)
            pick_cols = ((row_id - start == lane_id - 192) & (lane_id >= 192)).astype(BF)
            (
                incoming, keys_pad, values_pad, queries_pad, wo_cols, pick_cols, normed,
            ) = lax.optimization_barrier(
                (incoming, keys_pad, values_pad, queries_pad, wo_cols, pick_cols, normed)
            )

    flat_gin = gin_all.reshape(4 * ROWS, D)
    t_own = jnp.concatenate([flat_gin, gacc], axis=0)
    other = lax.dynamic_slice_in_dim(passed_all, 2 * (1 - zb), 2, 0).reshape(2 * ROWS, D)
    z_got = swap_z(jnp.concatenate([t_own, other], axis=0))
    z_pass = z_got[72:].reshape(2, ROWS, D)
    core_send = jnp.concatenate(
        [t_own, pick(passed_all, r ^ 1), z_got[:72], pick(z_pass, 1 - core)], axis=0
    )
    core_got = swap_core(core_send)
    grad_memory, send_a, send_b = run(
        weight_kernel,
        (
            jnp.stack([r, zb, x, y]).astype(jnp.int32),
            t_own, core_got[:72], z_got[:72], core_got[88:160],
            pick(passed_all, r), core_got[72:88], pick(z_pass, core), core_got[160:176],
            pair_a[8], pair_b[8], wo_cols, pick_cols, keys_pad, values_pad, queries_pad,
            prob, pair_a[0], pair_b[0], normed, attended,
        ),
        [shape(R, D), shape(4, 200, 384), shape(4, 192, 384)],
        scratch=[
            pltpu.VMEM((4, R, D), F32), pltpu.VMEM((4 * R, 384), BF),
            pltpu.VMEM((4 * L, 384), BF), pltpu.VMEM((4 * L, 384), BF),
        ],
        flops=2 * 10**9, nbytes=10**7, limit=24,
    )

    def along_x(step):
        return lambda yy, zz, rr, xx, hh: (yy, zz, rr, (xx + step) % 4, hh)

    def along_y(step):
        return lambda yy, zz, rr, xx, hh: ((yy + step) % 4, zz, rr, xx, hh)

    def ring_sums(parts):
        first = []
        for chunks, axis, half in parts:
            up = send(chunks[2, :half], axis(1))
            down = send(chunks[2, half:], axis(-1))
            first.append((up, down))
        second = []
        for (chunks, axis, half), (up, down) in zip(parts, first):
            up = jnp.concatenate([chunks[1, :half] + up, chunks[1, half:]], axis=0)
            down = jnp.concatenate([chunks[3, :half], chunks[3, half:] + down], axis=0)
            second.append((send(up, axis(1)), send(down, axis(-1))))
        return [
            chunks[0] + up + down for (chunks, axis, half), (up, down) in zip(parts, second)
        ]

    def turned(chunks, index):
        return jnp.stack([pick(chunks, (index + i) % 4) for i in range(4)])

    half_a, half_b = ring_sums([(send_a, along_x, 104), (send_b, along_y, 96)])
    chunks_a = jnp.concatenate(
        [
            turned(half_a[:192].reshape(4, 48, 384), y),
            jnp.broadcast_to(half_a[None, 192:], (4, 8, 384)),
        ],
        axis=1,
    )
    chunks_b = turned(
        half_b.reshape(2, 4, 24, 384).transpose(1, 0, 2, 3).reshape(4, 48, 384), x
    )
    half_a, half_b = ring_sums([(chunks_a, along_y, 32), (chunks_b, along_x, 24)])
    by_zp = jnp.concatenate(
        [half_a[:48].reshape(2, 24, 2, 2, 96), half_b.reshape(2, 24, 2, 2, 96)], axis=2
    )
    chunks = by_zp.transpose(0, 3, 1, 2, 4).reshape(4, 24, 384)
    chunks = jnp.concatenate([chunks, jnp.broadcast_to(half_a[None, 48:], (4, 8, 384))], axis=1)
    here = zp * 2 + h
    total = None
    for s in range(4):
        got = send(
            pick(chunks, here ^ s),
            lambda yy, zz, rr, xx, hh, s=s: (yy, zz ^ (s // 2), xx, rr, hh ^ (s % 2)),
        )
        total = got if total is None else total + got
    total = total * (1.0 / 256.0)
    return (
        grad_memory[None, None, None],
        total[:24, 0:96],
        total[:24, 96:192],
        total[:24, 192:288],
        total[:24, 288:384],
        total[24:26].reshape(D),
    )


def solution(mesh):
    return jax.shard_map(
        on_device,
        mesh=mesh,
        in_specs=(
            P("video", "tm", None, None, None),
            P("video", "tm", None, None, None),
            P("video", "tm", None, None, None),
            P("video", "tm", None),
            P("video", "tm", None, None, None),
            P("video", None),
            P(),
            P(),
            P(),
            P(),
            P(),
        ),
        out_specs=(
            P("video", "tm", None, None, None),
            P("tm", "video"),
            P("tm", "video"),
            P("tm", "video"),
            P("tm", "video"),
            P(),
        ),
        check_vma=False,
    )
```

```python
import math

import jax
import jax.numpy as jnp
from jax import lax
from jax.experimental import pallas as pl
from jax.experimental.pallas import tpu as pltpu
from jax.sharding import PartitionSpec as P

D = 768
H = 12
HD = 64
R = 64
L = 128
NORM_EPSILON = 1e-06
SCALE = HD ** (-0.5)
BF = jnp.bfloat16
F32 = jnp.float32
AXES = ("tm", "video")
GROUPS_TM = 8
ROWS = 16
INTERPRET = False
BIAS = 64
SLOT = BIAS + H


def dot(left, right, form=((1,), (0,))):
    return lax.dot_general(left, right, (form, ((), ())), preferred_element_type=F32)


def lane_head(rows, lanes):
    return lax.broadcasted_iota(jnp.int32, (rows, lanes), 1) // HD


def spread_heads(value, heads, base=0):
    which = lane_head(*value.shape)
    zero = jnp.zeros_like(value)
    parts = [jnp.where(which == base + h, value, zero) for h in range(heads)]
    return jnp.concatenate(parts, axis=0)


def merge_heads(value, heads, rows):
    which = lane_head(rows, value.shape[1])
    total = jnp.where(which == 0, value[:rows], 0.0)
    for h in range(1, heads):
        total = jnp.where(which == h, value[h * rows : (h + 1) * rows], total)
    return total


def prep_kernel(
    info, frames_a, pack_a, frames_b, pack_b, enc, gain, w_query, w_key, w_value,
    key_in, keys, values, values_t, rows, probs_out,
):
    core = info[0]
    place = (core, 1 - core)
    first = pl.multiple_of(core * ROWS, ROWS)
    tokens = jnp.concatenate([frames_a[...] + enc[0], frames_b[...] + enc[1]], axis=0).astype(BF)
    mem = jnp.concatenate([pack_a[pl.ds(first, ROWS)], pack_b[pl.ds(first, ROWS)]], axis=0)
    inv = lax.rsqrt(jnp.mean(mem * mem, axis=-1, keepdims=True) + NORM_EPSILON)
    unit = mem * inv
    query_f = dot((unit * gain[...]).astype(BF), w_query[...])
    key_b = dot(tokens, w_key[...]).astype(BF)
    value_f = dot(tokens, w_value[...])
    inv_wide = jnp.broadcast_to(inv, (2 * ROWS, 128))
    for i, pack in enumerate((pack_a, pack_b)):
        k = place[i]
        row = slice(ROWS * i, ROWS * i + ROWS)
        token = slice(L * i, L * i + L)
        key_in[k] = tokens[token]
        keys[k] = key_b[token]
        values[k] = value_f[token].astype(BF)
        values_t[k] = value_f[token].T.astype(BF)
        rows[k, 0:ROWS] = unit[row]
        rows[k, ROWS : 2 * ROWS] = pack[pl.ds(2 * ROWS + first, ROWS)]
        rows[k, 2 * ROWS : 2 * ROWS + 8] = jnp.broadcast_to(pack[SLOT : SLOT + 1], (8, D))
        probs_out[k, H] = inv_wide[row]
        for j in range(3):
            tile = slice(256 * j, 256 * j + 256)
            spread = spread_heads(query_f[row, tile], 4).astype(BF)
            probs = attend(spread, key_b[token, tile], pack, j, ROWS)
            probs_out[k, 4 * j : 4 * j + 4] = probs.reshape(4, ROWS, L)


def attend(spread, key_tile, pack, j, rows):
    scores = dot(spread, key_tile, ((1,), (1,))) * SCALE
    bias = []
    for h in range(4 * j, 4 * j + 4):
        bias.append(jnp.broadcast_to(pack[BIAS + h : BIAS + h + 1, 0:L], (rows, L)))
    scores = scores + jnp.concatenate(bias, axis=0)
    top = jnp.max(scores, axis=-1, keepdims=True)
    raised = jnp.exp(scores - top)
    return raised / jnp.sum(raised, axis=-1, keepdims=True)


def whole_kernel(
    info, m0, m1, m2, m3, pack0, pack1, pack2, pack3, keys_a, values_a, keys_b, values_b,
    gain, w_query,
    normed, queries, attended, prob_mine, prob,
):
    core, r = info[0], info[1]
    for s, (mem_ref, pack) in enumerate(((m0, pack0), (m1, pack1), (m2, pack2), (m3, pack3))):
        keys, values = ((keys_a, values_a), (keys_b, values_b))[s // 2]
        place = core if s % 2 == 0 else 1 - core
        m = 2 * (s // 2) + place
        mem = mem_ref[...]
        inv = lax.rsqrt(jnp.mean(mem * mem, axis=-1, keepdims=True) + NORM_EPSILON)
        norm = (mem * inv * gain[...]).astype(BF)
        normed[m] = norm
        query_f = dot(norm, w_query[...])
        queries[m] = query_f.astype(BF)
        for j in range(3):
            tile = slice(256 * j, 256 * j + 256)
            spread = spread_heads(query_f[:, tile], 4).astype(BF)
            probs = attend(spread, keys[place, :, tile], pack, j, R)
            prob[4 * j : 4 * j + 4] = probs.reshape(4, R, L)
            read = dot(probs.astype(BF), values[place, :, tile])
            attended[m, :, tile] = merge_heads(read, 4, R).astype(BF)
        prob_mine[m] = prob[pl.ds(3 * r, 3)]


def chain_kernel(
    info, incoming, gain,
    keys_a, values_t_a, rows_a, prob_a, keys_b, values_t_b, rows_b, prob_b,
    w_out_t, w_query_t, share_before,
    sending, share,
    keys, values_t, rows, prob, wo, wq, grads, sems,
):
    own = (rows_a, values_t_a, prob_a, keys_a)
    other = (rows_b, values_t_b, prob_b, keys_b)
    inside = (rows, values_t, prob, keys)

    def copies(order, k):
        return [
            pltpu.make_async_copy(src.at[k % 2], dst.at[k], sems.at[k, i])
            for i, (src, dst) in enumerate(zip(order[1 - k // 2], inside))
        ]

    wo_copy = pltpu.make_async_copy(w_out_t, wo, sems.at[0, 4])
    wq_copy = pltpu.make_async_copy(w_query_t, wq, sems.at[1, 4])

    def begin(order):
        for k in (3, 2, 1, 0):
            for i, copy in enumerate(copies(order, k)):
                copy.start()
                if k == 3 and i == 0:
                    wo_copy.start()
            if k == 3:
                wq_copy.start()

    @pl.when((info[0] != 0) & (info[1] == 1))
    def _():
        begin((own, other))

    @pl.when((info[0] != 0) & (info[1] == 0))
    def _():
        begin((other, own))

    @pl.when(info[0] != 0)
    def _():
        carried = incoming[...]
        total = jnp.zeros((ROWS, D), F32)
        for k in (3, 2, 1, 0):
            landed = copies((own, other), k)
            landed[0].wait()
            if k == 3:
                wo_copy.wait()
            grad_in = carried + rows[k, ROWS : 2 * ROWS]
            grads[ROWS * k : ROWS * k + ROWS] = grad_in
            out_grad = (grad_in * rows[k, 2 * ROWS : 2 * ROWS + 1]).astype(BF)
            att = dot(out_grad, wo[...])
            for copy in landed[1:]:
                copy.wait()
            query = []
            for j in range(3):
                tile = slice(256 * j, 256 * j + 256)
                spread = spread_heads(att[:, tile], 4).astype(BF)
                prob_grad = dot(spread, values_t[k, tile])
                probs = prob[k, 4 * j : 4 * j + 4].reshape(4 * ROWS, L)
                inner = jnp.sum(probs * prob_grad, axis=-1, keepdims=True)
                score = (probs * (prob_grad - inner) * SCALE).astype(BF)
                query.append(merge_heads(dot(score, keys[k, :, tile]), 4, ROWS).astype(BF))
            if k == 3:
                wq_copy.wait()
            normed_grad = dot(jnp.concatenate(query, axis=1), wq[...])
            unit = rows[k, 0:ROWS]
            total = total + normed_grad * unit
            scaled = normed_grad * gain[...]
            mean = jnp.mean(scaled * unit, axis=-1, keepdims=True)
            carried = grad_in + prob[k, H, :, 0:1] * (scaled - unit * mean)
            pair = info[1] if k >= 2 else 1 - info[1]
            place = 72 + 32 * pair + ROWS * (k % 2)
            grads[pl.ds(pl.multiple_of(place, 8), ROWS)] = carried
        sending[...] = carried
        grads[64:72] = total[0:8] + total[8:16]
        out = pltpu.make_async_copy(grads, share, sems.at[2, 4])
        out.start()
        out.wait()


def weight_kernel(
    info, t0, t1, t2, t3, rows_a, rows_b,
    wo_hbm, pick_hbm, keys_hbm, values_hbm, queries_hbm, prob_hbm, in_a_hbm, in_b_hbm,
    normed_hbm, attended_hbm,
    grad_memory, send_a, send_b,
    gin, qg, kg, vg,
    wo_cols, pick_cols, keys_pad, values_pad, queries_pad, prob, key_in, normed, attended, sems,
):
    r, zb, x, y = info[0], info[1], info[2], info[3]
    copies = [
        pltpu.make_async_copy(src, dst, sems.at[i])
        for i, (src, dst) in enumerate(
            (
                (wo_hbm, wo_cols), (values_hbm, values_pad), (prob_hbm, prob),
                (keys_hbm, keys_pad), (queries_hbm, queries_pad), (pick_hbm, pick_cols),
                (in_a_hbm, key_in.at[0:2]), (in_b_hbm, key_in.at[2:4]),
                (normed_hbm, normed), (attended_hbm, attended),
            )
        )
    ]
    for copy in copies:
        copy.start()
    gain = jnp.zeros((8, D), F32)
    for s, t in enumerate((t0, t1, t2, t3)):
        first = pl.multiple_of(jnp.bitwise_xor(r, s) * ROWS, ROWS)
        for m in range(4):
            slot = (rows_a, rows_b)[m // 2][m % 2, 2 * ROWS : 2 * ROWS + 1]
            k = 2 * jnp.bitwise_xor(zb, m // 2) + m % 2
            gin[m, pl.ds(first, ROWS)] = t[pl.ds(pl.multiple_of(k * ROWS, ROWS), ROWS)] * slot
        place = (104 if s < 2 else 72) + ROWS * jnp.bitwise_and(r, 1)
        grad_memory[pl.ds(first, ROWS)] = t[pl.ds(pl.multiple_of(place, 8), ROWS)]
        gain = gain + t[64:72]
    gain = jnp.sum(gain, axis=0, keepdims=True)
    out_grad = gin[...].reshape(4 * R, D).astype(BF)
    copies[0].wait()
    att = dot(out_grad, wo_cols[...])
    for copy in copies[1:]:
        copy.wait()
    picked = dot(out_grad, pick_cols[...]).astype(BF)
    for k in range(4):
        spread = spread_heads(att[R * k : R * k + R], 3).astype(BF)
        prob_grad = dot(spread, values_pad[k], ((1,), (1,)))
        probs = prob[k].reshape(3 * R, L)
        inner = jnp.sum(probs * prob_grad, axis=-1, keepdims=True)
        score = (probs * (prob_grad - inner) * SCALE).astype(BF)
        read = dot(score, keys_pad[k])
        qg[R * k : R * k + R] = merge_heads(read, 3, R).astype(BF)
        vg[L * k : L * k + L] = dot(probs.astype(BF), spread, ((0,), (0,))).astype(BF)
        q_spread = spread_heads(queries_pad[k].astype(F32), 3, 3).astype(BF)
        kg[L * k : L * k + L] = dot(score, q_spread, ((0,), (0,))).astype(BF)
    inputs = key_in[...].reshape(4 * L, D)
    both = dot(normed[...].reshape(4 * R, D), qg[...], ((0,), (0,)))
    both = both + dot(inputs, kg[...], ((0,), (0,)))
    tail = jnp.concatenate(
        [gain[:, 0:384], gain[:, 384:768], jnp.zeros((6, 384), F32)], axis=0
    )
    for ra in range(4):
        at = jnp.bitwise_and(ra - x, 3)
        for yz in range(8):
            a = yz * 4 + ra
            send_a[at, 24 * yz : 24 * yz + 24] = both[24 * a : 24 * a + 24]
        send_a[at, 192:200] = tail
    both = dot(inputs, vg[...], ((0,), (0,)))
    both = both + dot(attended[...].reshape(4 * R, D), picked, ((0,), (0,)))
    for ya in range(4):
        send_b[jnp.bitwise_and(ya - y, 3)] = both[192 * ya : 192 * ya + 192]


def shape(*dims, dtype=F32):
    return jax.ShapeDtypeStruct(dims, dtype)


def run(
    kernel, args, outs, scratch=(), aliases=None, flops=0, nbytes=0, limit=16, far=(), far_outs=()
):
    smem = pl.BlockSpec(memory_space=pltpu.SMEM)
    vmem = pl.BlockSpec(memory_space=pltpu.VMEM)
    hbm = pl.BlockSpec(memory_space=pl.ANY if INTERPRET else pltpu.HBM)
    return pl.pallas_call(
        kernel,
        out_shape=outs,
        in_specs=[smem] + [hbm if i in far else vmem for i in range(1, len(args))],
        out_specs=[hbm if i in far_outs else vmem for i in range(len(outs))],
        scratch_shapes=list(scratch),
        input_output_aliases=aliases or {},
        interpret=INTERPRET,
        compiler_params=pltpu.CompilerParams(vmem_limit_bytes=limit * 1024 * 1024),
        cost_estimate=pl.CostEstimate(flops=flops, bytes_accessed=nbytes, transcendentals=0),
    )(*args)


def encoding(offset, clip, length, features):
    frame_time = offset + clip * length + jnp.arange(length, dtype=jnp.int32)
    half = features // 2
    frequency = 0.0625 * jnp.exp(-math.log(1000.0) * jnp.arange(half, dtype=F32) / half)
    phases = frame_time.astype(F32)[:, None] * frequency
    return jnp.concatenate([jnp.sin(phases), jnp.cos(phases)], axis=-1)


def flat(y, zp, r, x, h):
    return (y * 8 + zp * 4 + r) * 8 + x * 2 + h


def pairs(move):
    out = []
    for y in range(4):
        for zp in range(2):
            for r in range(4):
                for x in range(4):
                    for h in range(2):
                        to = move(y, zp, r, x, h)
                        if to is not None:
                            out.append((flat(y, zp, r, x, h), flat(*to)))
    return out


def send(value, move):
    return lax.ppermute(value, AXES, pairs(move))


def swap_core(value):
    return send(value, lambda y, zp, r, x, h: (y, zp, r ^ 1, x, h))


def swap_z(value):
    return send(value, lambda y, zp, r, x, h: (y, zp, r ^ 2, x, h))


def to_next(value, group):
    def move(y, zp, r, x, h):
        if y * 2 + zp != group:
            return None
        return ((group - 1) // 2, (group - 1) % 2, r, x, h)

    return send(value, move)


def pick(array, index):
    return lax.dynamic_index_in_dim(array, index, 0, keepdims=False)


def on_device(
    memory, frames, mem_cot, slot_used, key_bias, start_offset,
    norm_gain, w_query, w_key, w_value, w_out,
):
    position = lax.axis_index("tm")
    video = lax.axis_index("video")
    group = position // 4
    r = position % 4
    core = position % 2
    y, zp = position // 8, (position // 4) % 2
    x, h = video // 2, video % 2
    zb = r // 2
    at_cores = jnp.stack([core, r]).astype(jnp.int32)

    own_frames = frames[0, 0, 0]
    own_mem = memory[0, 0, 0].astype(F32)
    own_cot = mem_cot[0, 0, 0].astype(F32)
    slot_row = jnp.broadcast_to(slot_used[0, 0].astype(F32)[:, None], (4, D))
    ends = jnp.concatenate(
        [jnp.pad(key_bias[0, 0, 0], ((0, 0), (0, D - L))), slot_row], axis=0
    )

    def pack_for(chip):
        return jnp.concatenate(
            [
                lax.dynamic_slice_in_dim(own_mem, 2 * ROWS * chip, 2 * ROWS, 0),
                lax.dynamic_slice_in_dim(own_cot, 2 * ROWS * chip, 2 * ROWS, 0),
                ends,
            ],
            axis=0,
        )

    pack_own = pack_for(zb)
    frames_z = swap_z(own_frames)
    pack_z = swap_z(pack_for(1 - zb))
    frames_c = swap_core(own_frames)
    pack_c = swap_core(pack_own)
    enc = [encoding(start_offset[0, 0], 4 * group + (r ^ s), L, D) for s in range(4)]
    enc_a = jnp.stack(enc[:2])
    enc_b = jnp.stack(enc[2:])
    w_out_t = w_out.T
    w_query_t = w_query.T
    gain = norm_gain[None]

    def prep(frames_0, pack_0, frames_1, pack_1, enc_pair):
        return run(
            prep_kernel,
            (
                at_cores, frames_0, pack_0, frames_1, pack_1, enc_pair, gain,
                w_query, w_key, w_value,
            ),
            [
                shape(2, L, D, dtype=BF), shape(2, L, D, dtype=BF), shape(2, L, D, dtype=BF),
                shape(2, D, L, dtype=BF), shape(2, 40, D), shape(2, H + 1, ROWS, L),
            ],
            flops=10**9, nbytes=8 * 10**6, limit=20,
        )

    pair_a = prep(own_frames, pack_own, frames_c, pack_c, enc_a)
    frames_z, pack_z, enc_b, w_out_t, w_query_t, _ = lax.optimization_barrier(
        (frames_z, pack_z, enc_b, w_out_t, w_query_t, pair_a[5])
    )
    frames_cz = swap_core(frames_z)
    pack_cz = swap_core(pack_z)
    pair_b = prep(frames_z, pack_z, frames_cz, pack_cz, enc_b)
    mem_late, _ = lax.optimization_barrier((own_mem, frames_cz))
    mem_z = swap_z(mem_late)
    mem_c = swap_core(mem_late)
    mem_cz = swap_core(mem_z)

    share = jnp.zeros((136, D), F32)
    incoming = jnp.zeros((ROWS, D), F32)
    pairs_ab = tuple(p[i] for p in (pair_a, pair_b) for i in (1, 3, 4, 5))
    for turn in range(GROUPS_TM):
        active = GROUPS_TM - 1 - turn
        info = jnp.stack([(group == active).astype(jnp.int32), zb.astype(jnp.int32)])
        sending, share = run(
            chain_kernel,
            (info, incoming, gain) + pairs_ab + (w_out_t, w_query_t, share),
            [shape(ROWS, D), shape(136, D)],
            scratch=[
                pltpu.VMEM((4, L, D), BF), pltpu.VMEM((4, D, L), BF), pltpu.VMEM((4, 40, D), F32),
                pltpu.VMEM((4, H + 1, ROWS, L), F32), pltpu.VMEM((D, D), BF),
                pltpu.VMEM((D, D), BF), pltpu.VMEM((136, D), F32),
                pltpu.SemaphoreType.DMA((4, 5)),
            ],
            aliases={13: 1}, far=range(3, 14), far_outs=(1,),
            flops=2 * 10**9, nbytes=5 * 10**6, limit=16,
        )
        if active > 0:
            incoming = to_next(sending, active)
        if turn == 0:
            mems = lax.optimization_barrier((own_mem, mem_c, mem_z, mem_cz, sending))[:4]
            normed, queries, attended, prob = run(
                whole_kernel,
                (at_cores,)
                + tuple(mems)
                + (
                    pack_own, pack_c, pack_z, pack_cz,
                    pair_a[1], pair_a[2], pair_b[1], pair_b[2], gain, w_query,
                ),
                [
                    shape(4, R, D, dtype=BF), shape(4, R, D, dtype=BF),
                    shape(4, R, D, dtype=BF), shape(4, 3, R, L),
                ],
                scratch=[pltpu.VMEM((H, R, L), F32)],
                flops=10**9, nbytes=8 * 10**6, limit=16,
            )
            start = lax.optimization_barrier((192 * r, mems[1]))[0]
            zero_cols = jnp.zeros((4, L, 192), BF)

            def mine(array):
                return lax.dynamic_slice_in_dim(array, start, 192, array.ndim - 1)

            def both_pairs(index):
                return jnp.concatenate([mine(pair_a[index]), mine(pair_b[index])], axis=0)

            keys_pad = jnp.concatenate([both_pairs(1), zero_cols], 2)
            values_pad = jnp.concatenate([both_pairs(2), zero_cols], 2)
            queries_pad = jnp.concatenate([zero_cols[:, :R], mine(queries)], 2)
            wo_cols = jnp.concatenate([mine(w_out_t), jnp.zeros((D, 192), BF)], 1)
            row_id = lax.broadcasted_iota(jnp.int32, (D, 384), 0)
            lane_id = lax.broadcasted_iota(jnp.int32, (D, 384), 1)
            pick_cols = ((row_id - start == lane_id - 192) & (lane_id >= 192)).astype(BF)
            (
                incoming, keys_pad, values_pad, queries_pad, wo_cols, pick_cols, normed,
            ) = lax.optimization_barrier(
                (incoming, keys_pad, values_pad, queries_pad, wo_cols, pick_cols, normed)
            )

    share_z = swap_z(share[:104])
    share_c = swap_core(share)
    share_cz = swap_core(share_z)
    grad_memory, send_a, send_b = run(
        weight_kernel,
        (
            jnp.stack([r, zb, x, y]).astype(jnp.int32),
            share, share_c, share_z, share_cz, pair_a[4], pair_b[4],
            wo_cols, pick_cols, keys_pad, values_pad, queries_pad,
            prob, pair_a[0], pair_b[0], normed, attended,
        ),
        [shape(R, D), shape(4, 200, 384), shape(4, 192, 384)],
        scratch=[
            pltpu.VMEM((4, R, D), F32), pltpu.VMEM((4 * R, 384), BF),
            pltpu.VMEM((4 * L, 384), BF), pltpu.VMEM((4 * L, 384), BF),
            pltpu.VMEM((D, 384), BF), pltpu.VMEM((D, 384), BF), pltpu.VMEM((4, L, 384), BF),
            pltpu.VMEM((4, L, 384), BF), pltpu.VMEM((4, R, 384), BF),
            pltpu.VMEM((4, 3, R, L), F32), pltpu.VMEM((4, L, D), BF), pltpu.VMEM((4, R, D), BF),
            pltpu.VMEM((4, R, D), BF), pltpu.SemaphoreType.DMA((10,)),
        ],
        flops=2 * 10**9, nbytes=10**7, limit=24, far=range(7, 17),
    )

    def along_x(step):
        return lambda yy, zz, rr, xx, hh: (yy, zz, rr, (xx + step) % 4, hh)

    def along_y(step):
        return lambda yy, zz, rr, xx, hh: ((yy + step) % 4, zz, rr, xx, hh)

    def ring_sums(parts):
        first = []
        for chunks, axis, half in parts:
            up = send(chunks[2, :half], axis(1))
            down = send(chunks[2, half:], axis(-1))
            first.append((up, down))
        second = []
        for (chunks, axis, half), (up, down) in zip(parts, first):
            up = jnp.concatenate([chunks[1, :half] + up, chunks[1, half:]], axis=0)
            down = jnp.concatenate([chunks[3, :half], chunks[3, half:] + down], axis=0)
            second.append((send(up, axis(1)), send(down, axis(-1))))
        return [
            chunks[0] + up + down for (chunks, axis, half), (up, down) in zip(parts, second)
        ]

    def turned(chunks, index):
        return jnp.stack([pick(chunks, (index + i) % 4) for i in range(4)])

    half_a, half_b = ring_sums([(send_a, along_x, 104), (send_b, along_y, 96)])
    chunks_a = jnp.concatenate(
        [
            turned(half_a[:192].reshape(4, 48, 384), y),
            jnp.broadcast_to(half_a[None, 192:], (4, 8, 384)),
        ],
        axis=1,
    )
    chunks_b = turned(
        half_b.reshape(2, 4, 24, 384).transpose(1, 0, 2, 3).reshape(4, 48, 384), x
    )
    half_a, half_b = ring_sums([(chunks_a, along_y, 32), (chunks_b, along_x, 24)])
    by_zp = jnp.concatenate(
        [half_a[:48].reshape(2, 24, 2, 2, 96), half_b.reshape(2, 24, 2, 2, 96)], axis=2
    )
    chunks = by_zp.transpose(0, 3, 1, 2, 4).reshape(4, 24, 384)
    chunks = jnp.concatenate([chunks, jnp.broadcast_to(half_a[None, 48:], (4, 8, 384))], axis=1)
    here = zp * 2 + h
    total = None
    for s in range(4):
        got = send(
            pick(chunks, here ^ s),
            lambda yy, zz, rr, xx, hh, s=s: (yy, zz ^ (s // 2), xx, rr, hh ^ (s % 2)),
        )
        total = got if total is None else total + got
    total = total * (1.0 / 256.0)
    return (
        grad_memory[None, None, None],
        total[:24, 0:96],
        total[:24, 96:192],
        total[:24, 192:288],
        total[:24, 288:384],
        total[24:26].reshape(D),
    )


def solution(mesh):
    return jax.shard_map(
        on_device,
        mesh=mesh,
        in_specs=(
            P("video", "tm", None, None, None),
            P("video", "tm", None, None, None),
            P("video", "tm", None, None, None),
            P("video", "tm", None),
            P("video", "tm", None, None, None),
            P("video", None),
            P(),
            P(),
            P(),
            P(),
            P(),
        ),
        out_specs=(
            P("video", "tm", None, None, None),
            P("tm", "video"),
            P("tm", "video"),
            P("tm", "video"),
            P("tm", "video"),
            P(),
        ),
        check_vma=False,
    )
```

```python
import math

import jax
import jax.numpy as jnp
from jax import lax
from jax.experimental import pallas as pl
from jax.experimental.pallas import tpu as pltpu
from jax.sharding import PartitionSpec as P

D = 768
H = 12
HD = 64
R = 64
L = 128
NORM_EPSILON = 1e-06
SCALE = HD ** (-0.5)
BF = jnp.bfloat16
F32 = jnp.float32
AXES = ("tm", "video")
GROUPS_TM = 8
ROWS = 16
INTERPRET = False
BIAS = 64
SLOT = BIAS + H


def dot(left, right, form=((1,), (0,))):
    return lax.dot_general(left, right, (form, ((), ())), preferred_element_type=F32)


def lane_head(rows, lanes):
    return lax.broadcasted_iota(jnp.int32, (rows, lanes), 1) // HD


def spread_heads(value, heads, base=0):
    which = lane_head(*value.shape)
    zero = jnp.zeros_like(value)
    parts = [jnp.where(which == base + h, value, zero) for h in range(heads)]
    return jnp.concatenate(parts, axis=0)


def merge_heads(value, heads, rows):
    which = lane_head(rows, value.shape[1])
    total = jnp.where(which == 0, value[:rows], 0.0)
    for h in range(1, heads):
        total = jnp.where(which == h, value[h * rows : (h + 1) * rows], total)
    return total


def prep_kernel(
    info, frames_a, pack_a, frames_b, pack_b, enc, gain, w_query, w_key, w_value,
    key_in, keys, values, values_t, rows, probs_out,
):
    core = info[0]
    place = (core, 1 - core)
    first = pl.multiple_of(core * ROWS, ROWS)
    tokens = jnp.concatenate([frames_a[...] + enc[0], frames_b[...] + enc[1]], axis=0).astype(BF)
    mem = jnp.concatenate([pack_a[pl.ds(first, ROWS)], pack_b[pl.ds(first, ROWS)]], axis=0)
    inv = lax.rsqrt(jnp.mean(mem * mem, axis=-1, keepdims=True) + NORM_EPSILON)
    unit = mem * inv
    query_f = dot((unit * gain[...]).astype(BF), w_query[...])
    key_b = dot(tokens, w_key[...]).astype(BF)
    value_f = dot(tokens, w_value[...])
    inv_wide = jnp.broadcast_to(inv, (2 * ROWS, 128))
    for i, pack in enumerate((pack_a, pack_b)):
        k = place[i]
        row = slice(ROWS * i, ROWS * i + ROWS)
        token = slice(L * i, L * i + L)
        key_in[k] = tokens[token]
        keys[k] = key_b[token]
        values[k] = value_f[token].astype(BF)
        values_t[k] = value_f[token].T.astype(BF)
        rows[k, 0:ROWS] = unit[row]
        rows[k, ROWS : 2 * ROWS] = pack[pl.ds(2 * ROWS + first, ROWS)]
        rows[k, 2 * ROWS : 2 * ROWS + 8] = jnp.broadcast_to(pack[SLOT : SLOT + 1], (8, D))
        probs_out[k, H] = inv_wide[row]
        for j in range(3):
            tile = slice(256 * j, 256 * j + 256)
            spread = spread_heads(query_f[row, tile], 4).astype(BF)
            probs = attend(spread, key_b[token, tile], pack, j, ROWS)
            probs_out[k, 4 * j : 4 * j + 4] = probs.reshape(4, ROWS, L)


def attend(spread, key_tile, pack, j, rows):
    scores = dot(spread, key_tile, ((1,), (1,))) * SCALE
    bias = []
    for h in range(4 * j, 4 * j + 4):
        bias.append(jnp.broadcast_to(pack[BIAS + h : BIAS + h + 1, 0:L], (rows, L)))
    scores = scores + jnp.concatenate(bias, axis=0)
    top = jnp.max(scores, axis=-1, keepdims=True)
    raised = jnp.exp(scores - top)
    return raised / jnp.sum(raised, axis=-1, keepdims=True)


def whole_kernel(
    info, m0, m1, m2, m3, pack0, pack1, pack2, pack3, keys_a, values_a, keys_b, values_b,
    gain, w_query, w_out_t,
    normed, attended, prob_mine, keys_pad, values_pad, queries_pad, wo_cols, pick_cols, prob,
):
    core, r = info[0], info[1]
    row_id = lax.broadcasted_iota(jnp.int32, (D, 384), 0) - 192 * r
    lane_id = lax.broadcasted_iota(jnp.int32, (D, 384), 1)
    low = ((row_id == lane_id) & (lane_id < 192)).astype(F32).astype(BF)
    high = ((row_id == lane_id - 192) & (lane_id >= 192)).astype(F32).astype(BF)
    pick_cols[...] = high
    wo_cols[...] = dot(w_out_t[...], low).astype(BF)
    for s, (mem_ref, pack) in enumerate(((m0, pack0), (m1, pack1), (m2, pack2), (m3, pack3))):
        keys, values = ((keys_a, values_a), (keys_b, values_b))[s // 2]
        place = core if s % 2 == 0 else 1 - core
        m = 2 * (s // 2) + place
        mem = mem_ref[...]
        inv = lax.rsqrt(jnp.mean(mem * mem, axis=-1, keepdims=True) + NORM_EPSILON)
        norm = (mem * inv * gain[...]).astype(BF)
        normed[m] = norm
        query_f = dot(norm, w_query[...])
        queries_pad[m] = dot(query_f.astype(BF), high).astype(BF)
        keys_pad[m] = dot(keys[place], low).astype(BF)
        values_pad[m] = dot(values[place], low).astype(BF)
        for j in range(3):
            tile = slice(256 * j, 256 * j + 256)
            spread = spread_heads(query_f[:, tile], 4).astype(BF)
            probs = attend(spread, keys[place, :, tile], pack, j, R)
            prob[4 * j : 4 * j + 4] = probs.reshape(4, R, L)
            read = dot(probs.astype(BF), values[place, :, tile])
            attended[m, :, tile] = merge_heads(read, 4, R).astype(BF)
        prob_mine[m] = prob[pl.ds(3 * r, 3)]


def chain_kernel(
    info, incoming, gain,
    keys_a, values_t_a, rows_a, prob_a, keys_b, values_t_b, rows_b, prob_b,
    w_out_t, w_query_t, share_before,
    sending, share,
    keys, values_t, rows, prob, wo, wq, grads, sems,
):
    own = (rows_a, values_t_a, prob_a, keys_a)
    other = (rows_b, values_t_b, prob_b, keys_b)
    inside = (rows, values_t, prob, keys)

    def copies(order, k):
        return [
            pltpu.make_async_copy(src.at[k % 2], dst.at[k], sems.at[k, i])
            for i, (src, dst) in enumerate(zip(order[1 - k // 2], inside))
        ]

    wo_copy = pltpu.make_async_copy(w_out_t, wo, sems.at[0, 4])
    wq_copy = pltpu.make_async_copy(w_query_t, wq, sems.at[1, 4])

    def begin(order):
        for k in (3, 2, 1, 0):
            for i, copy in enumerate(copies(order, k)):
                copy.start()
                if k == 3 and i == 0:
                    wo_copy.start()
            if k == 3:
                wq_copy.start()

    @pl.when((info[0] != 0) & (info[1] == 1))
    def _():
        begin((own, other))

    @pl.when((info[0] != 0) & (info[1] == 0))
    def _():
        begin((other, own))

    @pl.when(info[0] != 0)
    def _():
        carried = incoming[...]
        total = jnp.zeros((ROWS, D), F32)
        for k in (3, 2, 1, 0):
            landed = copies((own, other), k)
            landed[0].wait()
            if k == 3:
                wo_copy.wait()
            grad_in = carried + rows[k, ROWS : 2 * ROWS]
            grads[ROWS * k : ROWS * k + ROWS] = grad_in
            out_grad = (grad_in * rows[k, 2 * ROWS : 2 * ROWS + 1]).astype(BF)
            att = dot(out_grad, wo[...])
            for copy in landed[1:]:
                copy.wait()
            query = []
            for j in range(3):
                tile = slice(256 * j, 256 * j + 256)
                spread = spread_heads(att[:, tile], 4).astype(BF)
                prob_grad = dot(spread, values_t[k, tile])
                probs = prob[k, 4 * j : 4 * j + 4].reshape(4 * ROWS, L)
                inner = jnp.sum(probs * prob_grad, axis=-1, keepdims=True)
                score = (probs * (prob_grad - inner) * SCALE).astype(BF)
                query.append(merge_heads(dot(score, keys[k, :, tile]), 4, ROWS).astype(BF))
            if k == 3:
                wq_copy.wait()
            normed_grad = dot(jnp.concatenate(query, axis=1), wq[...])
            unit = rows[k, 0:ROWS]
            total = total + normed_grad * unit
            scaled = normed_grad * gain[...]
            mean = jnp.mean(scaled * unit, axis=-1, keepdims=True)
            carried = grad_in + prob[k, H, :, 0:1] * (scaled - unit * mean)
            pair = info[1] if k >= 2 else 1 - info[1]
            place = 72 + 32 * pair + ROWS * (k % 2)
            grads[pl.ds(pl.multiple_of(place, 8), ROWS)] = carried
        sending[...] = carried
        grads[64:72] = total[0:8] + total[8:16]
        out = pltpu.make_async_copy(grads, share, sems.at[2, 4])
        out.start()
        out.wait()


def weight_kernel(
    info, t0_hbm, t1, t2, t3, rows_a, rows_b,
    wo_hbm, pick_hbm, keys_hbm, values_hbm, queries_hbm, prob_hbm, in_a_hbm, in_b_hbm,
    normed_hbm, attended_hbm,
    grad_memory, send_a, send_b,
    gin, qg, kg, vg,
    wo_cols, pick_cols, keys_pad, values_pad, queries_pad, prob, key_in, normed, attended,
    t0, slots, sems,
):
    r, zb, x, y = info[0], info[1], info[2], info[3]
    copies = [
        pltpu.make_async_copy(src, dst, sems.at[i])
        for i, (src, dst) in enumerate(
            (
                (t0_hbm, t0), (rows_a.at[:, 2 * ROWS : 2 * ROWS + 8], slots.at[0:2]),
                (rows_b.at[:, 2 * ROWS : 2 * ROWS + 8], slots.at[2:4]),
                (wo_hbm, wo_cols), (values_hbm, values_pad), (prob_hbm, prob),
                (keys_hbm, keys_pad), (queries_hbm, queries_pad), (pick_hbm, pick_cols),
                (in_a_hbm, key_in.at[0:2]), (in_b_hbm, key_in.at[2:4]),
                (normed_hbm, normed), (attended_hbm, attended),
            )
        )
    ]
    for copy in copies:
        copy.start()
    for copy in copies[:3]:
        copy.wait()
    gain = jnp.zeros((8, D), F32)
    for s, t in enumerate((t0, t1, t2, t3)):
        first = pl.multiple_of(jnp.bitwise_xor(r, s) * ROWS, ROWS)
        for m in range(4):
            slot = slots[m, 0:1]
            k = 2 * jnp.bitwise_xor(zb, m // 2) + m % 2
            gin[m, pl.ds(first, ROWS)] = t[pl.ds(pl.multiple_of(k * ROWS, ROWS), ROWS)] * slot
        place = (104 if s < 2 else 72) + ROWS * jnp.bitwise_and(r, 1)
        grad_memory[pl.ds(first, ROWS)] = t[pl.ds(pl.multiple_of(place, 8), ROWS)]
        gain = gain + t[64:72]
    gain = jnp.sum(gain, axis=0, keepdims=True)
    out_grad = gin[...].reshape(4 * R, D).astype(BF)
    copies[3].wait()
    att = dot(out_grad, wo_cols[...])
    for copy in copies[4:]:
        copy.wait()
    picked = dot(out_grad, pick_cols[...]).astype(BF)
    for k in range(4):
        spread = spread_heads(att[R * k : R * k + R], 3).astype(BF)
        prob_grad = dot(spread, values_pad[k], ((1,), (1,)))
        probs = prob[k].reshape(3 * R, L)
        inner = jnp.sum(probs * prob_grad, axis=-1, keepdims=True)
        score = (probs * (prob_grad - inner) * SCALE).astype(BF)
        read = dot(score, keys_pad[k])
        qg[R * k : R * k + R] = merge_heads(read, 3, R).astype(BF)
        vg[L * k : L * k + L] = dot(probs.astype(BF), spread, ((0,), (0,))).astype(BF)
        q_spread = spread_heads(queries_pad[k].astype(F32), 3, 3).astype(BF)
        kg[L * k : L * k + L] = dot(score, q_spread, ((0,), (0,))).astype(BF)
    inputs = key_in[...].reshape(4 * L, D)
    both = dot(normed[...].reshape(4 * R, D), qg[...], ((0,), (0,)))
    both = both + dot(inputs, kg[...], ((0,), (0,)))
    tail = jnp.concatenate(
        [gain[:, 0:384], gain[:, 384:768], jnp.zeros((6, 384), F32)], axis=0
    )
    for ra in range(4):
        at = jnp.bitwise_and(ra - x, 3)
        for yz in range(8):
            a = yz * 4 + ra
            send_a[at, 24 * yz : 24 * yz + 24] = both[24 * a : 24 * a + 24]
        send_a[at, 192:200] = tail
    both = dot(inputs, vg[...], ((0,), (0,)))
    both = both + dot(attended[...].reshape(4 * R, D), picked, ((0,), (0,)))
    for ya in range(4):
        send_b[jnp.bitwise_and(ya - y, 3)] = both[192 * ya : 192 * ya + 192]


def shape(*dims, dtype=F32):
    return jax.ShapeDtypeStruct(dims, dtype)


def far(*dims, dtype=F32):
    return shape(*dims, dtype=dtype) if INTERPRET else pltpu.HBM(dims, dtype)


def run(
    kernel, args, outs, scratch=(), aliases=None, flops=0, nbytes=0, limit=16, away=(), away_out=()
):
    smem = pl.BlockSpec(memory_space=pltpu.SMEM)
    vmem = pl.BlockSpec(memory_space=pltpu.VMEM)
    hbm = pl.BlockSpec(memory_space=pl.ANY if INTERPRET else pltpu.HBM)
    args = list(args)
    for i in () if INTERPRET else away:
        args[i] = pltpu.with_memory_space_constraint(args[i], pltpu.HBM)
    return pl.pallas_call(
        kernel,
        out_shape=outs,
        in_specs=[smem] + [hbm if i in away else vmem for i in range(1, len(args))],
        out_specs=[hbm if i in away_out else vmem for i in range(len(outs))],
        scratch_shapes=list(scratch),
        input_output_aliases=aliases or {},
        interpret=INTERPRET,
        compiler_params=pltpu.CompilerParams(vmem_limit_bytes=limit * 1024 * 1024),
        cost_estimate=pl.CostEstimate(flops=flops, bytes_accessed=nbytes, transcendentals=0),
    )(*args)


def encoding(offset, clip, length, features):
    frame_time = offset + clip * length + jnp.arange(length, dtype=jnp.int32)
    half = features // 2
    frequency = 0.0625 * jnp.exp(-math.log(1000.0) * jnp.arange(half, dtype=F32) / half)
    phases = frame_time.astype(F32)[:, None] * frequency
    return jnp.concatenate([jnp.sin(phases), jnp.cos(phases)], axis=-1)


def flat(y, zp, r, x, h):
    return (y * 8 + zp * 4 + r) * 8 + x * 2 + h


def pairs(move):
    out = []
    for y in range(4):
        for zp in range(2):
            for r in range(4):
                for x in range(4):
                    for h in range(2):
                        to = move(y, zp, r, x, h)
                        if to is not None:
                            out.append((flat(y, zp, r, x, h), flat(*to)))
    return out


def send(value, move):
    return lax.ppermute(value, AXES, pairs(move))


def swap_core(value):
    return send(value, lambda y, zp, r, x, h: (y, zp, r ^ 1, x, h))


def swap_z(value):
    return send(value, lambda y, zp, r, x, h: (y, zp, r ^ 2, x, h))


def to_next(value, group):
    def move(y, zp, r, x, h):
        if y * 2 + zp != group:
            return None
        return ((group - 1) // 2, (group - 1) % 2, r, x, h)

    return send(value, move)


def pick(array, index):
    return lax.dynamic_index_in_dim(array, index, 0, keepdims=False)


def on_device(
    memory, frames, mem_cot, slot_used, key_bias, start_offset,
    norm_gain, w_query, w_key, w_value, w_out,
):
    position = lax.axis_index("tm")
    video = lax.axis_index("video")
    group = position // 4
    r = position % 4
    core = position % 2
    y, zp = position // 8, (position // 4) % 2
    x, h = video // 2, video % 2
    zb = r // 2
    at_cores = jnp.stack([core, r]).astype(jnp.int32)

    own_frames = frames[0, 0, 0]
    own_mem = memory[0, 0, 0].astype(F32)
    own_cot = mem_cot[0, 0, 0].astype(F32)
    slot_row = jnp.broadcast_to(slot_used[0, 0].astype(F32)[:, None], (4, D))
    ends = jnp.concatenate(
        [jnp.pad(key_bias[0, 0, 0], ((0, 0), (0, D - L))), slot_row], axis=0
    )

    def pack_for(chip):
        return jnp.concatenate(
            [
                lax.dynamic_slice_in_dim(own_mem, 2 * ROWS * chip, 2 * ROWS, 0),
                lax.dynamic_slice_in_dim(own_cot, 2 * ROWS * chip, 2 * ROWS, 0),
                ends,
            ],
            axis=0,
        )

    pack_own = pack_for(zb)
    frames_z = swap_z(own_frames)
    pack_z = swap_z(pack_for(1 - zb))
    frames_c = swap_core(own_frames)
    pack_c = swap_core(pack_own)
    enc = [encoding(start_offset[0, 0], 4 * group + (r ^ s), L, D) for s in range(4)]
    enc_a = jnp.stack(enc[:2])
    enc_b = jnp.stack(enc[2:])
    w_out_t = w_out.T
    w_query_t = w_query.T
    gain = norm_gain[None]

    def prep(frames_0, pack_0, frames_1, pack_1, enc_pair):
        return run(
            prep_kernel,
            (
                at_cores, frames_0, pack_0, frames_1, pack_1, enc_pair, gain,
                w_query, w_key, w_value,
            ),
            [
                far(2, L, D, dtype=BF), far(2, L, D, dtype=BF), far(2, L, D, dtype=BF),
                far(2, D, L, dtype=BF), far(2, 40, D), far(2, H + 1, ROWS, L),
            ],
            flops=10**9, nbytes=8 * 10**6, limit=24,
        )

    pair_a = prep(own_frames, pack_own, frames_c, pack_c, enc_a)
    frames_z, pack_z, enc_b, w_out_t, w_query_t, _ = lax.optimization_barrier(
        (frames_z, pack_z, enc_b, w_out_t, w_query_t, pair_a[5])
    )
    frames_cz = swap_core(frames_z)
    pack_cz = swap_core(pack_z)
    pair_b = prep(frames_z, pack_z, frames_cz, pack_cz, enc_b)
    mem_late, _ = lax.optimization_barrier((own_mem, frames_cz))
    mem_z = swap_z(mem_late)
    mem_c = swap_core(mem_late)
    mem_z, _ = lax.optimization_barrier((mem_z, pair_b[5]))
    mem_cz = swap_core(mem_z)

    share = jnp.zeros((136, D), F32)
    incoming = jnp.zeros((ROWS, D), F32)
    pairs_ab = tuple(p[i] for p in (pair_a, pair_b) for i in (1, 3, 4, 5))
    for turn in range(GROUPS_TM):
        active = GROUPS_TM - 1 - turn
        info = jnp.stack([(group == active).astype(jnp.int32), zb.astype(jnp.int32)])
        sending, share = run(
            chain_kernel,
            (info, incoming, gain) + pairs_ab + (w_out_t, w_query_t, share),
            [shape(ROWS, D), far(136, D)],
            scratch=[
                pltpu.VMEM((4, L, D), BF), pltpu.VMEM((4, D, L), BF), pltpu.VMEM((4, 40, D), F32),
                pltpu.VMEM((4, H + 1, ROWS, L), F32), pltpu.VMEM((D, D), BF),
                pltpu.VMEM((D, D), BF), pltpu.VMEM((136, D), F32),
                pltpu.SemaphoreType.DMA((4, 5)),
            ],
            aliases={13: 1}, away=range(3, 14), away_out=(1,),
            flops=2 * 10**9, nbytes=5 * 10**6, limit=16,
        )
        if active > 0:
            incoming = to_next(sending, active)
        if turn == 0:
            mems = lax.optimization_barrier((own_mem, mem_c, mem_z, mem_cz, sending))[:4]
            ready = run(
                whole_kernel,
                (at_cores,)
                + tuple(mems)
                + (
                    pack_own, pack_c, pack_z, pack_cz,
                    pair_a[1], pair_a[2], pair_b[1], pair_b[2], gain, w_query, w_out_t,
                ),
                [
                    far(4, R, D, dtype=BF), far(4, R, D, dtype=BF), far(4, 3, R, L),
                    far(4, L, 384, dtype=BF), far(4, L, 384, dtype=BF),
                    far(4, R, 384, dtype=BF), far(D, 384, dtype=BF), far(D, 384, dtype=BF),
                ],
                scratch=[pltpu.VMEM((H, R, L), F32)],
                flops=10**9, nbytes=8 * 10**6, limit=20,
            )
            normed, attended, prob, keys_pad, values_pad, queries_pad, wo_cols, pick_cols = ready
            incoming, _ = lax.optimization_barrier((incoming, prob))

    share_z = swap_z(share[:104])
    share_c = swap_core(share)
    share_cz = swap_core(share_z)
    grad_memory, send_a, send_b = run(
        weight_kernel,
        (
            jnp.stack([r, zb, x, y]).astype(jnp.int32),
            share, share_c, share_z, share_cz, pair_a[4], pair_b[4],
            wo_cols, pick_cols, keys_pad, values_pad, queries_pad,
            prob, pair_a[0], pair_b[0], normed, attended,
        ),
        [shape(R, D), shape(4, 200, 384), shape(4, 192, 384)],
        scratch=[
            pltpu.VMEM((4, R, D), F32), pltpu.VMEM((4 * R, 384), BF),
            pltpu.VMEM((4 * L, 384), BF), pltpu.VMEM((4 * L, 384), BF),
            pltpu.VMEM((D, 384), BF), pltpu.VMEM((D, 384), BF), pltpu.VMEM((4, L, 384), BF),
            pltpu.VMEM((4, L, 384), BF), pltpu.VMEM((4, R, 384), BF),
            pltpu.VMEM((4, 3, R, L), F32), pltpu.VMEM((4, L, D), BF), pltpu.VMEM((4, R, D), BF),
            pltpu.VMEM((4, R, D), BF), pltpu.VMEM((136, D), F32), pltpu.VMEM((4, 8, D), F32),
            pltpu.SemaphoreType.DMA((13,)),
        ],
        flops=2 * 10**9, nbytes=10**7, limit=24, away=(1,) + tuple(range(5, 17)),
    )

    def along_x(step):
        return lambda yy, zz, rr, xx, hh: (yy, zz, rr, (xx + step) % 4, hh)

    def along_y(step):
        return lambda yy, zz, rr, xx, hh: ((yy + step) % 4, zz, rr, xx, hh)

    def ring_sums(parts):
        first = []
        for chunks, axis, half in parts:
            up = send(chunks[2, :half], axis(1))
            down = send(chunks[2, half:], axis(-1))
            first.append((up, down))
        second = []
        for (chunks, axis, half), (up, down) in zip(parts, first):
            up = jnp.concatenate([chunks[1, :half] + up, chunks[1, half:]], axis=0)
            down = jnp.concatenate([chunks[3, :half], chunks[3, half:] + down], axis=0)
            second.append((send(up, axis(1)), send(down, axis(-1))))
        return [
            chunks[0] + up + down for (chunks, axis, half), (up, down) in zip(parts, second)
        ]

    def turned(chunks, index):
        return jnp.stack([pick(chunks, (index + i) % 4) for i in range(4)])

    half_a, half_b = ring_sums([(send_a, along_x, 104), (send_b, along_y, 96)])
    chunks_a = jnp.concatenate(
        [
            turned(half_a[:192].reshape(4, 48, 384), y),
            jnp.broadcast_to(half_a[None, 192:], (4, 8, 384)),
        ],
        axis=1,
    )
    chunks_b = turned(
        half_b.reshape(2, 4, 24, 384).transpose(1, 0, 2, 3).reshape(4, 48, 384), x
    )
    half_a, half_b = ring_sums([(chunks_a, along_y, 32), (chunks_b, along_x, 24)])
    by_zp = jnp.concatenate(
        [half_a[:48].reshape(2, 24, 2, 2, 96), half_b.reshape(2, 24, 2, 2, 96)], axis=2
    )
    chunks = by_zp.transpose(0, 3, 1, 2, 4).reshape(4, 24, 384)
    chunks = jnp.concatenate([chunks, jnp.broadcast_to(half_a[None, 48:], (4, 8, 384))], axis=1)
    here = zp * 2 + h
    total = None
    for s in range(4):
        got = send(
            pick(chunks, here ^ s),
            lambda yy, zz, rr, xx, hh, s=s: (yy, zz ^ (s // 2), xx, rr, hh ^ (s % 2)),
        )
        total = got if total is None else total + got
    total = total * (1.0 / 256.0)
    return (
        grad_memory[None, None, None],
        total[:24, 0:96],
        total[:24, 96:192],
        total[:24, 192:288],
        total[:24, 288:384],
        total[24:26].reshape(D),
    )


def solution(mesh):
    return jax.shard_map(
        on_device,
        mesh=mesh,
        in_specs=(
            P("video", "tm", None, None, None),
            P("video", "tm", None, None, None),
            P("video", "tm", None, None, None),
            P("video", "tm", None),
            P("video", "tm", None, None, None),
            P("video", None),
            P(),
            P(),
            P(),
            P(),
            P(),
        ),
        out_specs=(
            P("video", "tm", None, None, None),
            P("tm", "video"),
            P("tm", "video"),
            P("tm", "video"),
            P("tm", "video"),
            P(),
        ),
        check_vma=False,
    )
```

```python
import math

import jax
import jax.numpy as jnp
import numpy as np
from jax import lax
from jax.experimental import pallas as pl
from jax.experimental.pallas import tpu as pltpu
from jax.sharding import PartitionSpec as P

D = 768
H = 12
HD = 64
R = 64
L = 128
NORM_EPSILON = 1e-06
SCALE = HD ** (-0.5)
BF = jnp.bfloat16
F32 = jnp.float32
AXES = ("tm", "video")
GROUPS_TM = 8
ROWS = 16
INTERPRET = False
BIAS = 64
SLOT = BIAS + H


def dot(left, right, form=((1,), (0,))):
    return lax.dot_general(left, right, (form, ((), ())), preferred_element_type=F32)


def lane_head(rows, lanes):
    return lax.broadcasted_iota(jnp.int32, (rows, lanes), 1) // HD


def spread_heads(value, heads, base=0):
    which = lane_head(*value.shape)
    zero = jnp.zeros_like(value)
    parts = [jnp.where(which == base + h, value, zero) for h in range(heads)]
    return jnp.concatenate(parts, axis=0)


def merge_heads(value, heads, rows):
    which = lane_head(rows, value.shape[1])
    total = jnp.where(which == 0, value[:rows], 0.0)
    for h in range(1, heads):
        total = jnp.where(which == h, value[h * rows : (h + 1) * rows], total)
    return total


def pack_kernel(info, memory, cotangent, bias, pack_own, pack_far, mem_wide):
    zb = info[0]
    wide = memory[...].astype(F32)
    mem_wide[...] = wide
    cot = cotangent[...].astype(F32)
    slot = jnp.full((4, D), info[1], jnp.int32).astype(F32)
    ends = jnp.concatenate([bias[...], jnp.zeros((H, D - L), F32)], axis=1)
    ends = jnp.concatenate([ends, slot], axis=0)
    half = 2 * ROWS
    for chip in range(2):
        rows = slice(half * chip, half * chip + half)
        block = jnp.concatenate([wide[rows], cot[rows], ends], axis=0)

        @pl.when(zb == chip)
        def _():
            pack_own[...] = block

        @pl.when(zb != chip)
        def _():
            pack_far[...] = block


def prep_kernel(
    info, frames_a, pack_a, frames_b, pack_b, starts, table, gain, w_query, w_key, w_value,
    key_in, keys, values, values_t, rows, probs_out,
):
    core = info[0]
    place = (core, 1 - core)
    first = pl.multiple_of(core * ROWS, ROWS)
    tokens = []
    for i, frames in enumerate((frames_a, frames_b)):
        sin_0, cos_0 = starts[i, 0:1], starts[2 + i, 0:1]
        sine = sin_0 * table[1] + cos_0 * table[0]
        cosine = cos_0 * table[1] - sin_0 * table[0]
        tokens.append((frames[...] + jnp.concatenate([sine, cosine], axis=1)).astype(BF))
    tokens = jnp.concatenate(tokens, axis=0)
    mem = jnp.concatenate([pack_a[pl.ds(first, ROWS)], pack_b[pl.ds(first, ROWS)]], axis=0)
    inv = lax.rsqrt(jnp.mean(mem * mem, axis=-1, keepdims=True) + NORM_EPSILON)
    unit = mem * inv
    query_f = dot((unit * gain[...]).astype(BF), w_query[...])
    key_b = dot(tokens, w_key[...]).astype(BF)
    value_f = dot(tokens, w_value[...])
    inv_wide = jnp.broadcast_to(inv, (2 * ROWS, 128))
    for i, pack in enumerate((pack_a, pack_b)):
        k = place[i]
        row = slice(ROWS * i, ROWS * i + ROWS)
        token = slice(L * i, L * i + L)
        key_in[k] = tokens[token]
        keys[k] = key_b[token]
        values[k] = value_f[token].astype(BF)
        values_t[k] = value_f[token].T.astype(BF)
        rows[k, 0:ROWS] = unit[row]
        rows[k, ROWS : 2 * ROWS] = pack[pl.ds(2 * ROWS + first, ROWS)]
        rows[k, 2 * ROWS : 2 * ROWS + 8] = jnp.broadcast_to(pack[SLOT : SLOT + 1], (8, D))
        probs_out[k, H] = inv_wide[row]
        for j in range(3):
            tile = slice(256 * j, 256 * j + 256)
            spread = spread_heads(query_f[row, tile], 4).astype(BF)
            probs = attend(spread, key_b[token, tile], pack, j, ROWS)
            probs_out[k, 4 * j : 4 * j + 4] = probs.reshape(4, ROWS, L)


def attend(spread, key_tile, pack, j, rows):
    scores = dot(spread, key_tile, ((1,), (1,))) * SCALE
    bias = []
    for h in range(4 * j, 4 * j + 4):
        bias.append(jnp.broadcast_to(pack[BIAS + h : BIAS + h + 1, 0:L], (rows, L)))
    scores = scores + jnp.concatenate(bias, axis=0)
    top = jnp.max(scores, axis=-1, keepdims=True)
    raised = jnp.exp(scores - top)
    return raised / jnp.sum(raised, axis=-1, keepdims=True)


def whole_kernel(
    info, m0, m1, m2, m3, pack0, pack1, pack2, pack3, keys_a, values_a, keys_b, values_b,
    gain, w_query, w_out_t,
    normed, attended, prob_mine, keys_pad, values_pad, queries_pad, wo_cols, pick_cols, prob,
):
    core, r = info[0], info[1]
    row_id = lax.broadcasted_iota(jnp.int32, (D, 384), 0) - 192 * r
    lane_id = lax.broadcasted_iota(jnp.int32, (D, 384), 1)
    low = ((row_id == lane_id) & (lane_id < 192)).astype(F32).astype(BF)
    high = ((row_id == lane_id - 192) & (lane_id >= 192)).astype(F32).astype(BF)
    pick_cols[...] = high
    wo_cols[...] = dot(w_out_t[...], low).astype(BF)
    for s, (mem_ref, pack) in enumerate(((m0, pack0), (m1, pack1), (m2, pack2), (m3, pack3))):
        keys, values = ((keys_a, values_a), (keys_b, values_b))[s // 2]
        place = core if s % 2 == 0 else 1 - core
        m = 2 * (s // 2) + place
        mem = mem_ref[...]
        inv = lax.rsqrt(jnp.mean(mem * mem, axis=-1, keepdims=True) + NORM_EPSILON)
        norm = (mem * inv * gain[...]).astype(BF)
        normed[m] = norm
        query_f = dot(norm, w_query[...])
        queries_pad[m] = dot(query_f.astype(BF), high).astype(BF)
        keys_pad[m] = dot(keys[place], low).astype(BF)
        values_pad[m] = dot(values[place], low).astype(BF)
        for j in range(3):
            tile = slice(256 * j, 256 * j + 256)
            spread = spread_heads(query_f[:, tile], 4).astype(BF)
            probs = attend(spread, keys[place, :, tile], pack, j, R)
            prob[4 * j : 4 * j + 4] = probs.reshape(4, R, L)
            read = dot(probs.astype(BF), values[place, :, tile])
            attended[m, :, tile] = merge_heads(read, 4, R).astype(BF)
        prob_mine[m] = prob[pl.ds(3 * r, 3)]


def chain_kernel(
    info, incoming, gain,
    keys_a, values_t_a, rows_a, prob_a, keys_b, values_t_b, rows_b, prob_b,
    w_out_t, w_query_t, share_before,
    sending, share,
    keys, values_t, rows, prob, wo, wq, sems,
):
    own = (keys_a, values_t_a, rows_a, prob_a)
    other = (keys_b, values_t_b, rows_b, prob_b)

    def token(order, k, which):
        src, dst = (order[1 - k // 2][which], (keys, values_t)[which])
        return pltpu.make_async_copy(src.at[k % 2], dst.at[k], sems.at[k, which])

    def pair(order, p, which):
        src, dst = (order[1 - p][which], (rows, prob)[which - 2])
        return pltpu.make_async_copy(src, dst.at[2 * p : 2 * p + 2], sems.at[p, which])

    def out_tile(j):
        tile = slice(256 * j, 256 * j + 256)
        return pltpu.make_async_copy(w_out_t.at[:, tile], wo.at[:, tile], sems.at[j, 4])

    query_copy = pltpu.make_async_copy(w_query_t, wq, sems.at[3, 4])

    def begin(order):
        pair(order, 1, 2).start()
        out_tile(0).start()
        token(order, 3, 1).start()
        pair(order, 1, 3).start()
        token(order, 3, 0).start()
        out_tile(1).start()
        out_tile(2).start()
        query_copy.start()
        token(order, 2, 1).start()
        token(order, 2, 0).start()
        pair(order, 0, 2).start()
        pair(order, 0, 3).start()
        for k in (1, 0):
            token(order, k, 1).start()
            token(order, k, 0).start()

    @pl.when(info[0] == 0)
    def _():
        sending[...] = jnp.zeros_like(sending)
        share[...] = share_before[...]

    @pl.when((info[0] != 0) & (info[1] == 1))
    def _():
        begin((own, other))

    @pl.when((info[0] != 0) & (info[1] == 0))
    def _():
        begin((other, own))

    @pl.when(info[0] != 0)
    def _():
        order = (own, other)
        carried = incoming[...]
        total = jnp.zeros((ROWS, D), F32)
        for k in (3, 2, 1, 0):
            if k % 2 == 1:
                pair(order, k // 2, 2).wait()
            grad_in = carried + rows[k, ROWS : 2 * ROWS]
            share[ROWS * k : ROWS * k + ROWS] = grad_in
            out_grad = (grad_in * rows[k, 2 * ROWS : 2 * ROWS + 1]).astype(BF)
            query = []
            for j in range(3):
                tile = slice(256 * j, 256 * j + 256)
                if k == 3:
                    out_tile(j).wait()
                att = dot(out_grad, wo[:, tile])
                if j == 0:
                    token(order, k, 1).wait()
                    if k % 2 == 1:
                        pair(order, k // 2, 3).wait()
                    token(order, k, 0).wait()
                spread = spread_heads(att, 4).astype(BF)
                prob_grad = dot(spread, values_t[k, tile])
                probs = prob[k, 4 * j : 4 * j + 4].reshape(4 * ROWS, L)
                inner = jnp.sum(probs * prob_grad, axis=-1, keepdims=True)
                score = (probs * (prob_grad - inner) * SCALE).astype(BF)
                query.append(merge_heads(dot(score, keys[k, :, tile]), 4, ROWS).astype(BF))
            if k == 3:
                query_copy.wait()
            normed_grad = dot(jnp.concatenate(query, axis=1), wq[...])
            unit = rows[k, 0:ROWS]
            total = total + normed_grad * unit
            scaled = normed_grad * gain[...]
            mean = jnp.mean(scaled * unit, axis=-1, keepdims=True)
            carried = grad_in + prob[k, H, :, 0:1] * (scaled - unit * mean)
            pair_row = info[1] if k >= 2 else 1 - info[1]
            place = 72 + 32 * pair_row + ROWS * (k % 2)
            share[pl.ds(pl.multiple_of(place, 8), ROWS)] = carried
        sending[...] = carried
        share[64:72] = total[0:8] + total[8:16]


def weight_kernel(
    info, t0, t1, t2, t3, rows_a, rows_b,
    wo_hbm, pick_hbm, keys_hbm, values_hbm, queries_hbm, prob_hbm, in_a_hbm, in_b_hbm,
    normed_hbm, attended_hbm,
    grad_memory, send_a, send_b,
    gin, qg, kg, vg,
    wo_cols, pick_cols, keys_pad, values_pad, queries_pad, prob, key_in, normed, attended,
    slots, sems,
):
    r, zb, x, y = info[0], info[1], info[2], info[3]
    copies = [
        pltpu.make_async_copy(src, dst, sems.at[i])
        for i, (src, dst) in enumerate(
            (
                (rows_a.at[:, 2 * ROWS : 2 * ROWS + 8], slots.at[0:2]),
                (rows_b.at[:, 2 * ROWS : 2 * ROWS + 8], slots.at[2:4]),
                (wo_hbm, wo_cols), (values_hbm, values_pad), (prob_hbm, prob),
                (keys_hbm, keys_pad), (queries_hbm, queries_pad), (pick_hbm, pick_cols),
                (in_a_hbm, key_in.at[0:2]), (in_b_hbm, key_in.at[2:4]),
                (normed_hbm, normed), (attended_hbm, attended),
            )
        )
    ]
    for copy in copies:
        copy.start()
    for copy in copies[:2]:
        copy.wait()
    gain = jnp.zeros((8, D), F32)
    for s, t in enumerate((t0, t1, t2, t3)):
        first = pl.multiple_of(jnp.bitwise_xor(r, s) * ROWS, ROWS)
        for m in range(4):
            slot = slots[m, 0:1]
            k = 2 * jnp.bitwise_xor(zb, m // 2) + m % 2
            gin[m, pl.ds(first, ROWS)] = t[pl.ds(pl.multiple_of(k * ROWS, ROWS), ROWS)] * slot
        place = (104 if s < 2 else 72) + ROWS * jnp.bitwise_and(r, 1)
        grad_memory[pl.ds(first, ROWS)] = t[pl.ds(pl.multiple_of(place, 8), ROWS)]
        gain = gain + t[64:72]
    gain = jnp.sum(gain, axis=0, keepdims=True)
    out_grad = gin[...].reshape(4 * R, D).astype(BF)
    copies[2].wait()
    att = dot(out_grad, wo_cols[...])
    for copy in copies[3:]:
        copy.wait()
    picked = dot(out_grad, pick_cols[...]).astype(BF)
    for k in range(4):
        spread = spread_heads(att[R * k : R * k + R], 3).astype(BF)
        prob_grad = dot(spread, values_pad[k], ((1,), (1,)))
        probs = prob[k].reshape(3 * R, L)
        inner = jnp.sum(probs * prob_grad, axis=-1, keepdims=True)
        score = (probs * (prob_grad - inner) * SCALE).astype(BF)
        read = dot(score, keys_pad[k])
        qg[R * k : R * k + R] = merge_heads(read, 3, R).astype(BF)
        vg[L * k : L * k + L] = dot(probs.astype(BF), spread, ((0,), (0,))).astype(BF)
        q_spread = spread_heads(queries_pad[k].astype(F32), 3, 3).astype(BF)
        kg[L * k : L * k + L] = dot(score, q_spread, ((0,), (0,))).astype(BF)
    inputs = key_in[...].reshape(4 * L, D)
    both = dot(normed[...].reshape(4 * R, D), qg[...], ((0,), (0,)))
    both = both + dot(inputs, kg[...], ((0,), (0,)))
    tail = jnp.concatenate(
        [gain[:, 0:384], gain[:, 384:768], jnp.zeros((6, 384), F32)], axis=0
    )
    for ra in range(4):
        at = jnp.bitwise_and(ra - x, 3)
        for yz in range(8):
            a = yz * 4 + ra
            send_a[at, 24 * yz : 24 * yz + 24] = both[24 * a : 24 * a + 24]
        send_a[at, 192:200] = tail
    both = dot(inputs, vg[...], ((0,), (0,)))
    both = both + dot(attended[...].reshape(4 * R, D), picked, ((0,), (0,)))
    for ya in range(4):
        send_b[jnp.bitwise_and(ya - y, 3)] = both[192 * ya : 192 * ya + 192]


def shape(*dims, dtype=F32):
    return jax.ShapeDtypeStruct(dims, dtype)


def far(*dims, dtype=F32):
    return shape(*dims, dtype=dtype) if INTERPRET else pltpu.HBM(dims, dtype)


def near(*dims, dtype=F32):
    return shape(*dims, dtype=dtype) if INTERPRET else pltpu.VMEM(dims, dtype)


def run(
    kernel, args, outs, scratch=(), aliases=None, flops=0, nbytes=0, limit=16, away=(), close=()
):
    smem = pl.BlockSpec(memory_space=pltpu.SMEM)
    vmem = pl.BlockSpec(memory_space=pltpu.VMEM)
    hbm = pl.BlockSpec(memory_space=pl.ANY if INTERPRET else pltpu.HBM)
    args = list(args)
    for i in () if INTERPRET else away:
        args[i] = pltpu.with_memory_space_constraint(args[i], pltpu.HBM)
    for i in () if INTERPRET else close:
        args[i] = pltpu.with_memory_space_constraint(args[i], pltpu.VMEM)
    return pl.pallas_call(
        kernel,
        out_shape=outs,
        in_specs=[smem] + [hbm if i in away else vmem for i in range(1, len(args))],
        out_specs=[vmem] * len(outs),
        scratch_shapes=list(scratch),
        input_output_aliases=aliases or {},
        interpret=INTERPRET,
        compiler_params=pltpu.CompilerParams(vmem_limit_bytes=limit * 1024 * 1024),
        cost_estimate=pl.CostEstimate(flops=flops, bytes_accessed=nbytes, transcendentals=0),
    )(*args)


def frequencies():
    half = D // 2
    return 0.0625 * jnp.exp(-math.log(1000.0) * jnp.arange(half, dtype=F32) / half)


def within_clip():
    half = D // 2
    rate = 0.0625 * np.exp(-math.log(1000.0) * np.arange(half) / half)
    phases = np.arange(L)[:, None] * rate[None]
    return np.stack([np.sin(phases), np.cos(phases)]).astype(np.float32)


def flat(y, zp, r, x, h):
    return (y * 8 + zp * 4 + r) * 8 + x * 2 + h


def pairs(move):
    out = []
    for y in range(4):
        for zp in range(2):
            for r in range(4):
                for x in range(4):
                    for h in range(2):
                        to = move(y, zp, r, x, h)
                        if to is not None:
                            out.append((flat(y, zp, r, x, h), flat(*to)))
    return out


def send(value, move):
    return lax.ppermute(value, AXES, pairs(move))


def swap_core(value):
    return send(value, lambda y, zp, r, x, h: (y, zp, r ^ 1, x, h))


def swap_z(value):
    return send(value, lambda y, zp, r, x, h: (y, zp, r ^ 2, x, h))


def to_next(value, group):
    def move(y, zp, r, x, h):
        if y * 2 + zp != group:
            return None
        return ((group - 1) // 2, (group - 1) % 2, r, x, h)

    return send(value, move)


def pick(array, index):
    return lax.dynamic_index_in_dim(array, index, 0, keepdims=False)


def on_device(
    memory, frames, mem_cot, slot_used, key_bias, start_offset,
    norm_gain, w_query, w_key, w_value, w_out,
):
    position = lax.axis_index("tm")
    video = lax.axis_index("video")
    group = position // 4
    r = position % 4
    core = position % 2
    y, zp = position // 8, (position // 4) % 2
    x, h = video // 2, video % 2
    zb = r // 2
    at_cores = jnp.stack([core, r]).astype(jnp.int32)

    own_frames = frames[0, 0, 0]
    pack_own, pack_far, own_mem = run(
        pack_kernel,
        (
            jnp.stack([zb.astype(jnp.int32), slot_used[0, 0, 0]]),
            memory[0, 0, 0], mem_cot[0, 0, 0], key_bias[0, 0, 0],
        ),
        [shape(80, D), shape(80, D), shape(R, D)],
        flops=10**6, nbytes=10**6, limit=8,
    )
    frames_z = swap_z(own_frames)
    pack_z = swap_z(pack_far)
    frames_c = swap_core(own_frames)
    pack_c = swap_core(pack_own)
    clips = jnp.stack([4 * group + (r ^ s) for s in range(4)])
    first_times = (start_offset[0, 0] + clips * L).astype(F32)
    phases = first_times[:, None, None] * frequencies()[None, None]
    starts = jnp.concatenate([jnp.sin(phases), jnp.cos(phases)], axis=0)
    starts = jnp.broadcast_to(starts, (8, 8, D // 2))
    starts_a = jnp.stack([starts[0], starts[1], starts[4], starts[5]])
    starts_b = jnp.stack([starts[2], starts[3], starts[6], starts[7]])
    table = jnp.asarray(within_clip())
    w_out_t = w_out.T
    w_query_t = w_query.T
    gain = norm_gain[None]

    def prep(frames_0, pack_0, frames_1, pack_1, starts_pair):
        return run(
            prep_kernel,
            (
                at_cores, frames_0, pack_0, frames_1, pack_1, starts_pair, table, gain,
                w_query, w_key, w_value,
            ),
            [
                far(2, L, D, dtype=BF), far(2, L, D, dtype=BF), far(2, L, D, dtype=BF),
                far(2, D, L, dtype=BF), far(2, 40, D), far(2, H + 1, ROWS, L),
            ],
            flops=10**9, nbytes=8 * 10**6, limit=24,
        )

    pair_a = prep(own_frames, pack_own, frames_c, pack_c, starts_a)
    frames_z, pack_z, w_out_t, w_query_t, _ = lax.optimization_barrier(
        (frames_z, pack_z, w_out_t, w_query_t, pair_a[5])
    )
    frames_cz = swap_core(frames_z)
    pack_cz = swap_core(pack_z)
    pair_b = prep(frames_z, pack_z, frames_cz, pack_cz, starts_b)
    mem_late, _ = lax.optimization_barrier((own_mem, frames_cz))
    mem_z = swap_z(mem_late)
    mem_c = swap_core(mem_late)

    share = jnp.zeros((136, D), F32)
    incoming = jnp.zeros((ROWS, D), F32)
    pairs_ab = tuple(p[i] for p in (pair_a, pair_b) for i in (1, 3, 4, 5))
    for turn in range(GROUPS_TM):
        active = GROUPS_TM - 1 - turn
        info = jnp.stack([(group == active).astype(jnp.int32), zb.astype(jnp.int32)])
        sending, share = run(
            chain_kernel,
            (info, incoming, gain) + pairs_ab + (w_out_t, w_query_t, share),
            [shape(ROWS, D), near(136, D)],
            scratch=[
                pltpu.VMEM((4, L, D), BF), pltpu.VMEM((4, D, L), BF), pltpu.VMEM((4, 40, D), F32),
                pltpu.VMEM((4, H + 1, ROWS, L), F32), pltpu.VMEM((D, D), BF),
                pltpu.VMEM((D, D), BF), pltpu.SemaphoreType.DMA((4, 5)),
            ],
            aliases={13: 1}, away=range(3, 13), close=(13,),
            flops=2 * 10**9, nbytes=5 * 10**6, limit=16,
        )
        if active > 0:
            incoming = to_next(sending, active)
        if turn == 0:
            mem_z, _ = lax.optimization_barrier((mem_z, sending))
            mem_cz = swap_core(mem_z)
            mems = lax.optimization_barrier((own_mem, mem_c, mem_z, mem_cz, sending))[:4]
            ready = run(
                whole_kernel,
                (at_cores,)
                + tuple(mems)
                + (
                    pack_own, pack_c, pack_z, pack_cz,
                    pair_a[1], pair_a[2], pair_b[1], pair_b[2], gain, w_query, w_out_t,
                ),
                [
                    far(4, R, D, dtype=BF), far(4, R, D, dtype=BF), far(4, 3, R, L),
                    far(4, L, 384, dtype=BF), far(4, L, 384, dtype=BF),
                    far(4, R, 384, dtype=BF), far(D, 384, dtype=BF), far(D, 384, dtype=BF),
                ],
                scratch=[pltpu.VMEM((H, R, L), F32)],
                flops=10**9, nbytes=8 * 10**6, limit=20,
            )
            normed, attended, prob, keys_pad, values_pad, queries_pad, wo_cols, pick_cols = ready
            incoming, _ = lax.optimization_barrier((incoming, prob))

    share_z = swap_z(share[:104])
    share_c = swap_core(share)
    share_cz = swap_core(share_z)
    grad_memory, send_a, send_b = run(
        weight_kernel,
        (
            jnp.stack([r, zb, x, y]).astype(jnp.int32),
            share, share_c, share_z, share_cz, pair_a[4], pair_b[4],
            wo_cols, pick_cols, keys_pad, values_pad, queries_pad,
            prob, pair_a[0], pair_b[0], normed, attended,
        ),
        [shape(R, D), shape(4, 200, 384), shape(4, 192, 384)],
        scratch=[
            pltpu.VMEM((4, R, D), F32), pltpu.VMEM((4 * R, 384), BF),
            pltpu.VMEM((4 * L, 384), BF), pltpu.VMEM((4 * L, 384), BF),
            pltpu.VMEM((D, 384), BF), pltpu.VMEM((D, 384), BF), pltpu.VMEM((4, L, 384), BF),
            pltpu.VMEM((4, L, 384), BF), pltpu.VMEM((4, R, 384), BF),
            pltpu.VMEM((4, 3, R, L), F32), pltpu.VMEM((4, L, D), BF), pltpu.VMEM((4, R, D), BF),
            pltpu.VMEM((4, R, D), BF), pltpu.VMEM((4, 8, D), F32),
            pltpu.SemaphoreType.DMA((12,)),
        ],
        flops=2 * 10**9, nbytes=10**7, limit=24, away=range(5, 17),
    )

    def along_x(step):
        return lambda yy, zz, rr, xx, hh: (yy, zz, rr, (xx + step) % 4, hh)

    def along_y(step):
        return lambda yy, zz, rr, xx, hh: ((yy + step) % 4, zz, rr, xx, hh)

    def ring_sums(parts):
        first = []
        for chunks, axis, half in parts:
            up = send(chunks[2, :half], axis(1))
            down = send(chunks[2, half:], axis(-1))
            first.append((up, down))
        second = []
        for (chunks, axis, half), (up, down) in zip(parts, first):
            up = jnp.concatenate([chunks[1, :half] + up, chunks[1, half:]], axis=0)
            down = jnp.concatenate([chunks[3, :half], chunks[3, half:] + down], axis=0)
            second.append((send(up, axis(1)), send(down, axis(-1))))
        return [
            chunks[0] + up + down for (chunks, axis, half), (up, down) in zip(parts, second)
        ]

    def at(chunks, index, step):
        return pick(chunks, (index + step) % 4)

    def direct_sums(parts):
        got = []
        for step in (2, 1, 3):
            for chunks, axis, index in parts:
                got.append(send(at(chunks, index, step), axis(step)))
        return [
            at(chunks, index, 0) + got[i] + got[2 + i] + got[4 + i]
            for i, (chunks, axis, index) in enumerate(parts)
        ]

    half_a, half_b = ring_sums([(send_a, along_x, 104), (send_b, along_y, 96)])
    chunks_a = jnp.concatenate(
        [
            half_a[:192].reshape(4, 48, 384),
            jnp.broadcast_to(half_a[None, 192:], (4, 8, 384)),
        ],
        axis=1,
    )
    chunks_b = half_b.reshape(2, 4, 24, 384).transpose(1, 0, 2, 3).reshape(4, 48, 384)
    half_a, half_b = direct_sums([(chunks_a, along_y, y), (chunks_b, along_x, x)])
    by_zp = jnp.concatenate(
        [half_a[:48].reshape(2, 24, 2, 2, 96), half_b.reshape(2, 24, 2, 2, 96)], axis=2
    )
    chunks = by_zp.transpose(0, 3, 1, 2, 4).reshape(4, 24, 384)
    chunks = jnp.concatenate([chunks, jnp.broadcast_to(half_a[None, 48:], (4, 8, 384))], axis=1)
    here = zp * 2 + h
    total = None
    for s in range(4):
        got = send(
            pick(chunks, here ^ s),
            lambda yy, zz, rr, xx, hh, s=s: (yy, zz ^ (s // 2), xx, rr, hh ^ (s % 2)),
        )
        total = got if total is None else total + got
    total = total * (1.0 / 256.0)
    return (
        grad_memory[None, None, None],
        total[:24, 0:96],
        total[:24, 96:192],
        total[:24, 192:288],
        total[:24, 288:384],
        total[24:26].reshape(D),
    )


def solution(mesh):
    return jax.shard_map(
        on_device,
        mesh=mesh,
        in_specs=(
            P("video", "tm", None, None, None),
            P("video", "tm", None, None, None),
            P("video", "tm", None, None, None),
            P("video", "tm", None),
            P("video", "tm", None, None, None),
            P("video", None),
            P(),
            P(),
            P(),
            P(),
            P(),
        ),
        out_specs=(
            P("video", "tm", None, None, None),
            P("tm", "video"),
            P("tm", "video"),
            P("tm", "video"),
            P("tm", "video"),
            P(),
        ),
        check_vma=False,
    )
```

```python
import functools
import math

import jax
import jax.numpy as jnp
import numpy as np
from jax import lax
from jax.experimental import pallas as pl
from jax.experimental.pallas import tpu as pltpu
from jax.sharding import PartitionSpec as P

D = 768
H = 12
HD = 64
R = 64
L = 128
NORM_EPSILON = 1e-06
SCALE = HD ** (-0.5)
BF = jnp.bfloat16
F32 = jnp.float32
AXES = ("tm", "video")
GROUPS_TM = 8
ROWS = 16
INTERPRET = False
BIAS = 64
SLOT = BIAS + H


def dot(left, right, form=((1,), (0,))):
    return lax.dot_general(left, right, (form, ((), ())), preferred_element_type=F32)


def lane_head(rows, lanes):
    return lax.broadcasted_iota(jnp.int32, (rows, lanes), 1) // HD


def spread_heads(value, heads, base=0):
    which = lane_head(*value.shape)
    zero = jnp.zeros_like(value)
    parts = [jnp.where(which == base + h, value, zero) for h in range(heads)]
    return jnp.concatenate(parts, axis=0)


def merge_heads(value, heads, rows):
    which = lane_head(rows, value.shape[1])
    total = jnp.where(which == 0, value[:rows], 0.0)
    for h in range(1, heads):
        total = jnp.where(which == h, value[h * rows : (h + 1) * rows], total)
    return total


def pack_kernel(info, memory, cotangent, bias, pack_own, pack_far, mem_wide):
    zb = info[0]
    wide = memory[...].astype(F32)
    mem_wide[...] = wide
    cot = cotangent[...].astype(F32)
    slot = jnp.full((4, D), info[1], jnp.int32).astype(F32)
    ends = jnp.concatenate([bias[...], jnp.zeros((H, D - L), F32)], axis=1)
    ends = jnp.concatenate([ends, slot], axis=0)
    half = 2 * ROWS
    for chip in range(2):
        rows = slice(half * chip, half * chip + half)
        block = jnp.concatenate([wide[rows], cot[rows], ends], axis=0)

        @pl.when(zb == chip)
        def _():
            pack_own[...] = block

        @pl.when(zb != chip)
        def _():
            pack_far[...] = block


def prep_kernel(
    base, info, frames_a, pack_a, frames_b, pack_b, starts, table, gain, w_query, w_key, w_value,
    key_in, keys, values, values_t, rows, probs_out,
):
    core = info[0]
    place = (core, 1 - core)
    first = pl.multiple_of(core * ROWS, ROWS)
    tokens = []
    for i, frames in enumerate((frames_a, frames_b)):
        at = base + i
        sin_0, cos_0 = starts[at : at + 1], starts[4 + at : 5 + at]
        sine = sin_0 * table[1] + cos_0 * table[0]
        cosine = cos_0 * table[1] - sin_0 * table[0]
        tokens.append((frames[...] + jnp.concatenate([sine, cosine], axis=1)).astype(BF))
    tokens = jnp.concatenate(tokens, axis=0)
    mem = jnp.concatenate([pack_a[pl.ds(first, ROWS)], pack_b[pl.ds(first, ROWS)]], axis=0)
    inv = lax.rsqrt(jnp.mean(mem * mem, axis=-1, keepdims=True) + NORM_EPSILON)
    unit = mem * inv
    query_f = dot((unit * gain[...]).astype(BF), w_query[...])
    key_b = dot(tokens, w_key[...]).astype(BF)
    value_f = dot(tokens, w_value[...])
    inv_wide = jnp.broadcast_to(inv, (2 * ROWS, 128))
    for i, pack in enumerate((pack_a, pack_b)):
        k = place[i]
        row = slice(ROWS * i, ROWS * i + ROWS)
        token = slice(L * i, L * i + L)
        key_in[k] = tokens[token]
        keys[k] = key_b[token]
        values[k] = value_f[token].astype(BF)
        values_t[k] = value_f[token].T.astype(BF)
        rows[k, 0:ROWS] = unit[row]
        rows[k, ROWS : 2 * ROWS] = pack[pl.ds(2 * ROWS + first, ROWS)]
        rows[k, 2 * ROWS : 2 * ROWS + 8] = jnp.broadcast_to(pack[SLOT : SLOT + 1], (8, D))
        probs_out[k, H] = inv_wide[row]
        for j in range(3):
            tile = slice(256 * j, 256 * j + 256)
            spread = spread_heads(query_f[row, tile], 4).astype(BF)
            probs = attend(spread, key_b[token, tile], pack, j, ROWS)
            probs_out[k, 4 * j : 4 * j + 4] = probs.reshape(4, ROWS, L)


def attend(spread, key_tile, pack, j, rows):
    scores = dot(spread, key_tile, ((1,), (1,))) * SCALE
    bias = []
    for h in range(4 * j, 4 * j + 4):
        bias.append(jnp.broadcast_to(pack[BIAS + h : BIAS + h + 1, 0:L], (rows, L)))
    scores = scores + jnp.concatenate(bias, axis=0)
    top = jnp.max(scores, axis=-1, keepdims=True)
    raised = jnp.exp(scores - top)
    return raised / jnp.sum(raised, axis=-1, keepdims=True)


def whole_kernel(
    info, m0, m1, m2, m3, pack0, pack1, pack2, pack3, keys_a, values_a, keys_b, values_b,
    gain, w_query, weights,
    normed, attended, prob_mine, keys_pad, values_pad, queries_pad, wo_cols, pick_cols, prob,
):
    core, r = info[0], info[1]
    row_id = lax.broadcasted_iota(jnp.int32, (D, 384), 0) - 192 * r
    lane_id = lax.broadcasted_iota(jnp.int32, (D, 384), 1)
    low = ((row_id == lane_id) & (lane_id < 192)).astype(F32).astype(BF)
    high = ((row_id == lane_id - 192) & (lane_id >= 192)).astype(F32).astype(BF)
    pick_cols[...] = high
    wo_cols[...] = dot(weights[0], low).astype(BF)
    for s, (mem_ref, pack) in enumerate(((m0, pack0), (m1, pack1), (m2, pack2), (m3, pack3))):
        keys, values = ((keys_a, values_a), (keys_b, values_b))[s // 2]
        place = core if s % 2 == 0 else 1 - core
        m = 2 * (s // 2) + place
        mem = mem_ref[...]
        inv = lax.rsqrt(jnp.mean(mem * mem, axis=-1, keepdims=True) + NORM_EPSILON)
        norm = (mem * inv * gain[...]).astype(BF)
        normed[m] = norm
        query_f = dot(norm, w_query[...])
        queries_pad[m] = dot(query_f.astype(BF), high).astype(BF)
        keys_pad[m] = dot(keys[place], low).astype(BF)
        values_pad[m] = dot(values[place], low).astype(BF)
        for j in range(3):
            tile = slice(256 * j, 256 * j + 256)
            spread = spread_heads(query_f[:, tile], 4).astype(BF)
            probs = attend(spread, keys[place, :, tile], pack, j, R)
            prob[4 * j : 4 * j + 4] = probs.reshape(4, R, L)
            read = dot(probs.astype(BF), values[place, :, tile])
            attended[m, :, tile] = merge_heads(read, 4, R).astype(BF)
        prob_mine[m] = prob[pl.ds(3 * r, 3)]


def chain_kernel(
    info, incoming, gain,
    keys_a, values_t_a, rows_a, prob_a, keys_b, values_t_b, rows_b, prob_b,
    weights, share_before,
    sending, share, weights_same,
    keys, values_t, rows, prob, grads, sems,
):
    own = (rows_a, values_t_a, prob_a, keys_a)
    other = (rows_b, values_t_b, prob_b, keys_b)
    inside = (rows, values_t, prob, keys)

    def copies(order, k):
        return [
            pltpu.make_async_copy(src.at[k % 2], dst.at[k], sems.at[k, i])
            for i, (src, dst) in enumerate(zip(order[1 - k // 2], inside))
        ]

    def begin(order):
        for k in (3, 2, 1, 0):
            for copy in copies(order, k):
                copy.start()

    @pl.when(info[0] == 0)
    def _():
        sending[...] = jnp.zeros_like(sending)

    @pl.when((info[0] != 0) & (info[1] == 1))
    def _():
        begin((own, other))

    @pl.when((info[0] != 0) & (info[1] == 0))
    def _():
        begin((other, own))

    @pl.when(info[0] != 0)
    def _():
        carried = incoming[...]
        total = jnp.zeros((ROWS, D), F32)
        leaving = []

        def leave(where, i):
            copy = pltpu.make_async_copy(grads.at[where], share.at[where], sems.at[i, 4])
            copy.start()
            return copy

        for k in (3, 2, 1, 0):
            landed = copies((own, other), k)
            landed[0].wait()
            grad_in = carried + rows[k, ROWS : 2 * ROWS]
            grads[ROWS * k : ROWS * k + ROWS] = grad_in
            if k == 0:
                leaving.append(leave(slice(0, 64), 0))
            out_grad = (grad_in * rows[k, 2 * ROWS : 2 * ROWS + 1]).astype(BF)
            att = dot(out_grad, weights[0])
            for copy in landed[1:]:
                copy.wait()
            query = []
            for j in range(3):
                tile = slice(256 * j, 256 * j + 256)
                spread = spread_heads(att[:, tile], 4).astype(BF)
                prob_grad = dot(spread, values_t[k, tile])
                probs = prob[k, 4 * j : 4 * j + 4].reshape(4 * ROWS, L)
                inner = jnp.sum(probs * prob_grad, axis=-1, keepdims=True)
                score = (probs * (prob_grad - inner) * SCALE).astype(BF)
                query.append(merge_heads(dot(score, keys[k, :, tile]), 4, ROWS).astype(BF))
            normed_grad = dot(jnp.concatenate(query, axis=1), weights[1])
            unit = rows[k, 0:ROWS]
            total = total + normed_grad * unit
            scaled = normed_grad * gain[...]
            mean = jnp.mean(scaled * unit, axis=-1, keepdims=True)
            carried = grad_in + prob[k, H, :, 0:1] * (scaled - unit * mean)
            pair_row = info[1] if k >= 2 else 1 - info[1]
            place = 72 + 32 * pair_row + ROWS * (k % 2)
            grads[pl.ds(pl.multiple_of(place, 8), ROWS)] = carried
            if k % 2 == 0:
                both = pl.ds(pl.multiple_of(72 + 32 * pair_row, 8), 2 * ROWS)
                leaving.append(leave(both, 1 + k // 2))
        sending[...] = carried
        grads[64:72] = total[0:8] + total[8:16]
        leaving.append(leave(slice(64, 72), 3))
        for copy in leaving:
            copy.wait()


def weight_kernel(
    info, t0_hbm, t1, t2, t3, rows_a, rows_b,
    wo_hbm, pick_hbm, keys_hbm, values_hbm, queries_hbm, prob_hbm, in_a_hbm, in_b_hbm,
    normed_hbm, attended_hbm,
    grad_memory, send_a, send_b,
    gin, qg, kg, vg,
    wo_cols, pick_cols, keys_pad, values_pad, queries_pad, prob, key_in, normed, attended,
    t0, slots, sems,
):
    r, zb, x, y = info[0], info[1], info[2], info[3]
    copies = [
        pltpu.make_async_copy(src, dst, sems.at[i])
        for i, (src, dst) in enumerate(
            (
                (t0_hbm, t0), (rows_a.at[:, 2 * ROWS : 2 * ROWS + 8], slots.at[0:2]),
                (rows_b.at[:, 2 * ROWS : 2 * ROWS + 8], slots.at[2:4]),
                (wo_hbm, wo_cols), (values_hbm, values_pad), (prob_hbm, prob),
                (keys_hbm, keys_pad), (queries_hbm, queries_pad), (pick_hbm, pick_cols),
                (in_a_hbm, key_in.at[0:2]), (in_b_hbm, key_in.at[2:4]),
                (normed_hbm, normed), (attended_hbm, attended),
            )
        )
    ]
    for copy in copies:
        copy.start()
    for copy in copies[:3]:
        copy.wait()
    gain = jnp.zeros((8, D), F32)
    for s, t in enumerate((t0, t1, t2, t3)):
        first = pl.multiple_of(jnp.bitwise_xor(r, s) * ROWS, ROWS)
        for m in range(4):
            slot = slots[m, 0:1]
            k = 2 * jnp.bitwise_xor(zb, m // 2) + m % 2
            gin[m, pl.ds(first, ROWS)] = t[pl.ds(pl.multiple_of(k * ROWS, ROWS), ROWS)] * slot
        place = (104 if s < 2 else 72) + ROWS * jnp.bitwise_and(r, 1)
        grad_memory[pl.ds(first, ROWS)] = t[pl.ds(pl.multiple_of(place, 8), ROWS)]
        gain = gain + t[64:72]
    gain = jnp.sum(gain, axis=0, keepdims=True)
    out_grad = gin[...].reshape(4 * R, D).astype(BF)
    copies[3].wait()
    att = dot(out_grad, wo_cols[...])
    for copy in copies[4:]:
        copy.wait()
    picked = dot(out_grad, pick_cols[...]).astype(BF)
    for k in range(4):
        spread = spread_heads(att[R * k : R * k + R], 3).astype(BF)
        prob_grad = dot(spread, values_pad[k], ((1,), (1,)))
        probs = prob[k].reshape(3 * R, L)
        inner = jnp.sum(probs * prob_grad, axis=-1, keepdims=True)
        score = (probs * (prob_grad - inner) * SCALE).astype(BF)
        read = dot(score, keys_pad[k])
        qg[R * k : R * k + R] = merge_heads(read, 3, R).astype(BF)
        vg[L * k : L * k + L] = dot(probs.astype(BF), spread, ((0,), (0,))).astype(BF)
        q_spread = spread_heads(queries_pad[k].astype(F32), 3, 3).astype(BF)
        kg[L * k : L * k + L] = dot(score, q_spread, ((0,), (0,))).astype(BF)
    inputs = key_in[...].reshape(4 * L, D)
    both = dot(normed[...].reshape(4 * R, D), qg[...], ((0,), (0,)))
    both = both + dot(inputs, kg[...], ((0,), (0,)))
    tail = jnp.concatenate(
        [gain[:, 0:384], gain[:, 384:768], jnp.zeros((6, 384), F32)], axis=0
    )
    for ra in range(4):
        at = jnp.bitwise_and(ra - x, 3)
        for yz in range(8):
            a = yz * 4 + ra
            send_a[at, 24 * yz : 24 * yz + 24] = both[24 * a : 24 * a + 24]
        send_a[at, 192:200] = tail
    both = dot(inputs, vg[...], ((0,), (0,)))
    both = both + dot(attended[...].reshape(4 * R, D), picked, ((0,), (0,)))
    for ya in range(4):
        send_b[jnp.bitwise_and(ya - y, 3)] = both[192 * ya : 192 * ya + 192]


def shape(*dims, dtype=F32):
    return jax.ShapeDtypeStruct(dims, dtype)


def far(*dims, dtype=F32):
    return shape(*dims, dtype=dtype) if INTERPRET else pltpu.HBM(dims, dtype)


def near(*dims, dtype=F32):
    return shape(*dims, dtype=dtype) if INTERPRET else pltpu.VMEM(dims, dtype)


def run(
    kernel, args, outs, scratch=(), aliases=None, flops=0, nbytes=0, limit=16, away=(), close=(),
    away_out=(),
):
    smem = pl.BlockSpec(memory_space=pltpu.SMEM)
    vmem = pl.BlockSpec(memory_space=pltpu.VMEM)
    hbm = pl.BlockSpec(memory_space=pl.ANY if INTERPRET else pltpu.HBM)
    args = list(args)
    for i in () if INTERPRET else away:
        args[i] = pltpu.with_memory_space_constraint(args[i], pltpu.HBM)
    for i in () if INTERPRET else close:
        args[i] = pltpu.with_memory_space_constraint(args[i], pltpu.VMEM)
    return pl.pallas_call(
        kernel,
        out_shape=outs,
        in_specs=[smem] + [hbm if i in away else vmem for i in range(1, len(args))],
        out_specs=[hbm if i in away_out else vmem for i in range(len(outs))],
        scratch_shapes=list(scratch),
        input_output_aliases=aliases or {},
        interpret=INTERPRET,
        compiler_params=pltpu.CompilerParams(vmem_limit_bytes=limit * 1024 * 1024),
        cost_estimate=pl.CostEstimate(flops=flops, bytes_accessed=nbytes, transcendentals=0),
    )(*args)


def frequencies():
    half = D // 2
    return 0.0625 * jnp.exp(-math.log(1000.0) * jnp.arange(half, dtype=F32) / half)


def within_clip():
    half = D // 2
    rate = 0.0625 * np.exp(-math.log(1000.0) * np.arange(half) / half)
    phases = np.arange(L)[:, None] * rate[None]
    return np.stack([np.sin(phases), np.cos(phases)]).astype(np.float32)


def flat(y, zp, r, x, h):
    return (y * 8 + zp * 4 + r) * 8 + x * 2 + h


def pairs(move):
    out = []
    for y in range(4):
        for zp in range(2):
            for r in range(4):
                for x in range(4):
                    for h in range(2):
                        to = move(y, zp, r, x, h)
                        if to is not None:
                            out.append((flat(y, zp, r, x, h), flat(*to)))
    return out


def send(value, move):
    return lax.ppermute(value, AXES, pairs(move))


def swap_core(value):
    return send(value, lambda y, zp, r, x, h: (y, zp, r ^ 1, x, h))


def swap_z(value):
    return send(value, lambda y, zp, r, x, h: (y, zp, r ^ 2, x, h))


def to_next(value, group):
    def move(y, zp, r, x, h):
        if y * 2 + zp != group:
            return None
        return ((group - 1) // 2, (group - 1) % 2, r, x, h)

    return send(value, move)


def pick(array, index):
    return lax.dynamic_index_in_dim(array, index, 0, keepdims=False)


def on_device(
    memory, frames, mem_cot, slot_used, key_bias, start_offset,
    norm_gain, w_query, w_key, w_value, w_out,
):
    position = lax.axis_index("tm")
    video = lax.axis_index("video")
    group = position // 4
    r = position % 4
    core = position % 2
    y, zp = position // 8, (position // 4) % 2
    x, h = video // 2, video % 2
    zb = r // 2
    at_cores = jnp.stack([core, r]).astype(jnp.int32)

    own_frames = frames[0, 0, 0]
    pack_own, pack_far, own_mem = run(
        pack_kernel,
        (
            jnp.stack([zb.astype(jnp.int32), slot_used[0, 0, 0]]),
            memory[0, 0, 0], mem_cot[0, 0, 0], key_bias[0, 0, 0],
        ),
        [shape(80, D), shape(80, D), shape(R, D)],
        flops=10**6, nbytes=10**6, limit=8,
    )
    frames_z = swap_z(own_frames)
    pack_z = swap_z(pack_far)
    frames_c = swap_core(own_frames)
    pack_c = swap_core(pack_own)
    clips = jnp.stack([4 * group + (r ^ s) for s in range(4)])
    first_times = (start_offset[0, 0] + clips * L).astype(F32)
    phases = first_times[:, None] * frequencies()[None]
    starts = jnp.concatenate([jnp.sin(phases), jnp.cos(phases)], axis=0)
    table = jnp.asarray(within_clip())
    weights = jnp.stack([w_out.T, w_query.T])
    gain = norm_gain[None]

    def prep(frames_0, pack_0, frames_1, pack_1, base):
        return run(
            functools.partial(prep_kernel, base),
            (
                at_cores, frames_0, pack_0, frames_1, pack_1, starts, table, gain,
                w_query, w_key, w_value,
            ),
            [
                far(2, L, D, dtype=BF), far(2, L, D, dtype=BF), far(2, L, D, dtype=BF),
                far(2, D, L, dtype=BF), far(2, 40, D), far(2, H + 1, ROWS, L),
            ],
            flops=10**9, nbytes=8 * 10**6, limit=24,
        )

    pair_a = prep(own_frames, pack_own, frames_c, pack_c, 0)
    frames_z, pack_z, weights, _ = lax.optimization_barrier(
        (frames_z, pack_z, weights, pair_a[5])
    )
    frames_cz = swap_core(frames_z)
    pack_cz = swap_core(pack_z)
    pair_b = prep(frames_z, pack_z, frames_cz, pack_cz, 2)
    mem_late, _ = lax.optimization_barrier((own_mem, frames_cz))
    mem_z = swap_z(mem_late)
    mem_c = swap_core(mem_late)

    share = jnp.zeros((136, D), F32)
    incoming = jnp.zeros((ROWS, D), F32)
    pairs_ab = tuple(p[i] for p in (pair_a, pair_b) for i in (1, 3, 4, 5))
    for turn in range(GROUPS_TM):
        active = GROUPS_TM - 1 - turn
        info = jnp.stack([(group == active).astype(jnp.int32), zb.astype(jnp.int32)])
        sending, share, weights = run(
            chain_kernel,
            (info, incoming, gain) + pairs_ab + (weights, share),
            [shape(ROWS, D), far(136, D), near(2, D, D, dtype=BF)],
            scratch=[
                pltpu.VMEM((4, L, D), BF), pltpu.VMEM((4, D, L), BF), pltpu.VMEM((4, 40, D), F32),
                pltpu.VMEM((4, H + 1, ROWS, L), F32), pltpu.VMEM((136, D), F32),
                pltpu.SemaphoreType.DMA((4, 5)),
            ],
            aliases={12: 1, 11: 2}, away=tuple(range(3, 11)) + (12,), close=(11,), away_out=(1,),
            flops=2 * 10**9, nbytes=5 * 10**6, limit=8,
        )
        if active > 0:
            incoming = to_next(sending, active)
        if turn == 0:
            mem_z, _ = lax.optimization_barrier((mem_z, sending))
            mem_cz = swap_core(mem_z)
            mems = lax.optimization_barrier((own_mem, mem_c, mem_z, mem_cz, sending))[:4]
            ready = run(
                whole_kernel,
                (at_cores,)
                + tuple(mems)
                + (
                    pack_own, pack_c, pack_z, pack_cz,
                    pair_a[1], pair_a[2], pair_b[1], pair_b[2], gain, w_query, weights,
                ),
                [
                    far(4, R, D, dtype=BF), far(4, R, D, dtype=BF), far(4, 3, R, L),
                    far(4, L, 384, dtype=BF), far(4, L, 384, dtype=BF),
                    far(4, R, 384, dtype=BF), far(D, 384, dtype=BF), far(D, 384, dtype=BF),
                ],
                scratch=[pltpu.VMEM((H, R, L), F32)],
                flops=10**9, nbytes=8 * 10**6, limit=20,
            )
            normed, attended, prob, keys_pad, values_pad, queries_pad, wo_cols, pick_cols = ready
            incoming, _ = lax.optimization_barrier((incoming, prob))

    share_z = swap_z(share[:104])
    share_c = swap_core(share)
    share_cz = swap_core(share_z)
    grad_memory, send_a, send_b = run(
        weight_kernel,
        (
            jnp.stack([r, zb, x, y]).astype(jnp.int32),
            share, share_c, share_z, share_cz, pair_a[4], pair_b[4],
            wo_cols, pick_cols, keys_pad, values_pad, queries_pad,
            prob, pair_a[0], pair_b[0], normed, attended,
        ),
        [shape(R, D), shape(4, 200, 384), shape(4, 192, 384)],
        scratch=[
            pltpu.VMEM((4, R, D), F32), pltpu.VMEM((4 * R, 384), BF),
            pltpu.VMEM((4 * L, 384), BF), pltpu.VMEM((4 * L, 384), BF),
            pltpu.VMEM((D, 384), BF), pltpu.VMEM((D, 384), BF), pltpu.VMEM((4, L, 384), BF),
            pltpu.VMEM((4, L, 384), BF), pltpu.VMEM((4, R, 384), BF),
            pltpu.VMEM((4, 3, R, L), F32), pltpu.VMEM((4, L, D), BF), pltpu.VMEM((4, R, D), BF),
            pltpu.VMEM((4, R, D), BF), pltpu.VMEM((136, D), F32), pltpu.VMEM((4, 8, D), F32),
            pltpu.SemaphoreType.DMA((13,)),
        ],
        flops=2 * 10**9, nbytes=10**7, limit=24, away=(1,) + tuple(range(5, 17)),
    )

    def along_x(step):
        return lambda yy, zz, rr, xx, hh: (yy, zz, rr, (xx + step) % 4, hh)

    def along_y(step):
        return lambda yy, zz, rr, xx, hh: ((yy + step) % 4, zz, rr, xx, hh)

    def ring_sums(parts):
        first = []
        for chunks, axis, half in parts:
            up = send(chunks[2, :half], axis(1))
            down = send(chunks[2, half:], axis(-1))
            first.append((up, down))
        second = []
        for (chunks, axis, half), (up, down) in zip(parts, first):
            up = jnp.concatenate([chunks[1, :half] + up, chunks[1, half:]], axis=0)
            down = jnp.concatenate([chunks[3, :half], chunks[3, half:] + down], axis=0)
            second.append((send(up, axis(1)), send(down, axis(-1))))
        return [
            chunks[0] + up + down for (chunks, axis, half), (up, down) in zip(parts, second)
        ]

    def at(chunks, index, step):
        return pick(chunks, (index + step) % 4)

    def direct_sums(parts):
        got = []
        for step in (2, 1, 3):
            for chunks, axis, index in parts:
                got.append(send(at(chunks, index, step), axis(step)))
        return [
            at(chunks, index, 0) + got[i] + got[2 + i] + got[4 + i]
            for i, (chunks, axis, index) in enumerate(parts)
        ]

    half_a, half_b = ring_sums([(send_a, along_x, 104), (send_b, along_y, 96)])
    chunks_a = jnp.concatenate(
        [
            half_a[:192].reshape(4, 48, 384),
            jnp.broadcast_to(half_a[None, 192:], (4, 8, 384)),
        ],
        axis=1,
    )
    chunks_b = half_b.reshape(2, 4, 24, 384).transpose(1, 0, 2, 3).reshape(4, 48, 384)
    half_a, half_b = direct_sums([(chunks_a, along_y, y), (chunks_b, along_x, x)])
    by_zp = jnp.concatenate(
        [half_a[:48].reshape(2, 24, 2, 2, 96), half_b.reshape(2, 24, 2, 2, 96)], axis=2
    )
    chunks = by_zp.transpose(0, 3, 1, 2, 4).reshape(4, 24, 384)
    chunks = jnp.concatenate([chunks, jnp.broadcast_to(half_a[None, 48:], (4, 8, 384))], axis=1)
    here = zp * 2 + h
    total = None
    for s in range(4):
        got = send(
            pick(chunks, here ^ s),
            lambda yy, zz, rr, xx, hh, s=s: (yy, zz ^ (s // 2), xx, rr, hh ^ (s % 2)),
        )
        total = got if total is None else total + got
    total = total * (1.0 / 256.0)
    return (
        grad_memory[None, None, None],
        total[:24, 0:96],
        total[:24, 96:192],
        total[:24, 192:288],
        total[:24, 288:384],
        total[24:26].reshape(D),
    )


def solution(mesh):
    return jax.shard_map(
        on_device,
        mesh=mesh,
        in_specs=(
            P("video", "tm", None, None, None),
            P("video", "tm", None, None, None),
            P("video", "tm", None, None, None),
            P("video", "tm", None),
            P("video", "tm", None, None, None),
            P("video", None),
            P(),
            P(),
            P(),
            P(),
            P(),
        ),
        out_specs=(
            P("video", "tm", None, None, None),
            P("tm", "video"),
            P("tm", "video"),
            P("tm", "video"),
            P("tm", "video"),
            P(),
        ),
        check_vma=False,
    )
```

```python
import functools
import math

import jax
import jax.numpy as jnp
import numpy as np
from jax import lax
from jax.experimental import pallas as pl
from jax.experimental.pallas import tpu as pltpu
from jax.sharding import PartitionSpec as P

D = 768
H = 12
HD = 64
R = 64
L = 128
NORM_EPSILON = 1e-06
SCALE = HD ** (-0.5)
BF = jnp.bfloat16
F32 = jnp.float32
AXES = ("tm", "video")
GROUPS_TM = 8
ROWS = 16
INTERPRET = False
BIAS = 64
SLOT = BIAS + H


def dot(left, right, form=((1,), (0,))):
    return lax.dot_general(left, right, (form, ((), ())), preferred_element_type=F32)


def lane_head(rows, lanes):
    return lax.broadcasted_iota(jnp.int32, (rows, lanes), 1) // HD


def spread_heads(value, heads, base=0):
    which = lane_head(*value.shape)
    zero = jnp.zeros_like(value)
    parts = [jnp.where(which == base + h, value, zero) for h in range(heads)]
    return jnp.concatenate(parts, axis=0)


def merge_heads(value, heads, rows):
    which = lane_head(rows, value.shape[1])
    total = jnp.where(which == 0, value[:rows], 0.0)
    for h in range(1, heads):
        total = jnp.where(which == h, value[h * rows : (h + 1) * rows], total)
    return total


def pack_kernel(info, memory, cotangent, bias, pack_own, pack_far, mem_wide):
    zb = info[0]
    wide = memory[...].astype(F32)
    mem_wide[...] = wide
    cot = cotangent[...].astype(F32)
    slot = jnp.full((4, D), info[1], jnp.int32).astype(F32)
    ends = jnp.concatenate([bias[...], jnp.zeros((H, D - L), F32)], axis=1)
    ends = jnp.concatenate([ends, slot], axis=0)
    half = 2 * ROWS
    for chip in range(2):
        rows = slice(half * chip, half * chip + half)
        block = jnp.concatenate([wide[rows], cot[rows], ends], axis=0)

        @pl.when(zb == chip)
        def _():
            pack_own[...] = block

        @pl.when(zb != chip)
        def _():
            pack_far[...] = block


def prep_kernel(info, *refs):
    for pair in range(2):
        prep_pair(
            2 * pair, info, *refs[4 * pair : 4 * pair + 4], *refs[8:14],
            *refs[14 + 6 * pair : 20 + 6 * pair],
        )


def prep_pair(
    base, info, frames_a, pack_a, frames_b, pack_b, starts, table, gain, w_query, w_key, w_value,
    key_in, keys, values, values_t, rows, probs_out,
):
    core = info[0]
    place = (core, 1 - core)
    first = pl.multiple_of(core * ROWS, ROWS)
    tokens = []
    for i, frames in enumerate((frames_a, frames_b)):
        at = base + i
        sin_0, cos_0 = starts[at : at + 1], starts[4 + at : 5 + at]
        sine = sin_0 * table[1] + cos_0 * table[0]
        cosine = cos_0 * table[1] - sin_0 * table[0]
        tokens.append((frames[...] + jnp.concatenate([sine, cosine], axis=1)).astype(BF))
    tokens = jnp.concatenate(tokens, axis=0)
    mem = jnp.concatenate([pack_a[pl.ds(first, ROWS)], pack_b[pl.ds(first, ROWS)]], axis=0)
    inv = lax.rsqrt(jnp.mean(mem * mem, axis=-1, keepdims=True) + NORM_EPSILON)
    unit = mem * inv
    query_f = dot((unit * gain[...]).astype(BF), w_query[...])
    key_b = dot(tokens, w_key[...]).astype(BF)
    value_f = dot(tokens, w_value[...])
    inv_wide = jnp.broadcast_to(inv, (2 * ROWS, 128))
    for i, pack in enumerate((pack_a, pack_b)):
        k = place[i]
        row = slice(ROWS * i, ROWS * i + ROWS)
        token = slice(L * i, L * i + L)
        key_in[k] = tokens[token]
        keys[k] = key_b[token]
        values[k] = value_f[token].astype(BF)
        values_t[k] = value_f[token].T.astype(BF)
        rows[k, 0:ROWS] = unit[row]
        rows[k, ROWS : 2 * ROWS] = pack[pl.ds(2 * ROWS + first, ROWS)]
        rows[k, 2 * ROWS : 2 * ROWS + 8] = jnp.broadcast_to(pack[SLOT : SLOT + 1], (8, D))
        probs_out[k, H] = inv_wide[row]
        for j in range(3):
            tile = slice(256 * j, 256 * j + 256)
            spread = spread_heads(query_f[row, tile], 4).astype(BF)
            probs = attend(spread, key_b[token, tile], pack, j, ROWS)
            probs_out[k, 4 * j : 4 * j + 4] = probs.reshape(4, ROWS, L)


def attend(spread, key_tile, pack, j, rows):
    scores = dot(spread, key_tile, ((1,), (1,))) * SCALE
    bias = []
    for h in range(4 * j, 4 * j + 4):
        bias.append(jnp.broadcast_to(pack[BIAS + h : BIAS + h + 1, 0:L], (rows, L)))
    scores = scores + jnp.concatenate(bias, axis=0)
    top = jnp.max(scores, axis=-1, keepdims=True)
    raised = jnp.exp(scores - top)
    return raised / jnp.sum(raised, axis=-1, keepdims=True)


def whole_kernel(
    info, m0, m1, m2, m3, pack0, pack1, pack2, pack3, keys_a, values_a, keys_b, values_b,
    gain, w_query, weights,
    normed, attended, prob_mine, keys_pad, values_pad, queries_pad, wo_cols, pick_cols, prob,
):
    core, r = info[0], info[1]
    row_id = lax.broadcasted_iota(jnp.int32, (D, 384), 0) - 192 * r
    lane_id = lax.broadcasted_iota(jnp.int32, (D, 384), 1)
    low = ((row_id == lane_id) & (lane_id < 192)).astype(F32).astype(BF)
    high = ((row_id == lane_id - 192) & (lane_id >= 192)).astype(F32).astype(BF)
    pick_cols[...] = high
    wo_cols[...] = dot(weights[0], low).astype(BF)
    for s, (mem_ref, pack) in enumerate(((m0, pack0), (m1, pack1), (m2, pack2), (m3, pack3))):
        keys, values = ((keys_a, values_a), (keys_b, values_b))[s // 2]
        place = core if s % 2 == 0 else 1 - core
        m = 2 * (s // 2) + place
        mem = mem_ref[...]
        inv = lax.rsqrt(jnp.mean(mem * mem, axis=-1, keepdims=True) + NORM_EPSILON)
        norm = (mem * inv * gain[...]).astype(BF)
        normed[m] = norm
        query_f = dot(norm, w_query[...])
        queries_pad[m] = dot(query_f.astype(BF), high).astype(BF)
        keys_pad[m] = dot(keys[place], low).astype(BF)
        values_pad[m] = dot(values[place], low).astype(BF)
        for j in range(3):
            tile = slice(256 * j, 256 * j + 256)
            spread = spread_heads(query_f[:, tile], 4).astype(BF)
            probs = attend(spread, keys[place, :, tile], pack, j, R)
            prob[4 * j : 4 * j + 4] = probs.reshape(4, R, L)
            read = dot(probs.astype(BF), values[place, :, tile])
            attended[m, :, tile] = merge_heads(read, 4, R).astype(BF)
        prob_mine[m] = prob[pl.ds(3 * r, 3)]


def chain_kernel(
    info, incoming, gain,
    keys_a, values_t_a, rows_a, prob_a, keys_b, values_t_b, rows_b, prob_b,
    weights, share_before,
    sending, share, weights_same,
    keys, values_t, rows, prob, grads, sems,
):
    own = (rows_a, values_t_a, prob_a, keys_a)
    other = (rows_b, values_t_b, prob_b, keys_b)
    inside = (rows, values_t, prob, keys)

    def copies(order, k):
        return [
            pltpu.make_async_copy(src.at[k % 2], dst.at[k], sems.at[k, i])
            for i, (src, dst) in enumerate(zip(order[1 - k // 2], inside))
        ]

    def begin(order):
        for k in (3, 2, 1, 0):
            for copy in copies(order, k):
                copy.start()

    @pl.when(info[0] == 0)
    def _():
        sending[...] = jnp.zeros_like(sending)

    @pl.when((info[0] != 0) & (info[1] == 1))
    def _():
        begin((own, other))

    @pl.when((info[0] != 0) & (info[1] == 0))
    def _():
        begin((other, own))

    @pl.when(info[0] != 0)
    def _():
        carried = incoming[...]
        total = jnp.zeros((ROWS, D), F32)
        leaving = []

        def leave(where, i):
            copy = pltpu.make_async_copy(grads.at[where], share.at[where], sems.at[i, 4])
            copy.start()
            return copy

        for k in (3, 2, 1, 0):
            landed = copies((own, other), k)
            landed[0].wait()
            grad_in = carried + rows[k, ROWS : 2 * ROWS]
            grads[ROWS * k : ROWS * k + ROWS] = grad_in
            if k == 0:
                leaving.append(leave(slice(0, 64), 0))
            out_grad = (grad_in * rows[k, 2 * ROWS : 2 * ROWS + 1]).astype(BF)
            att = dot(out_grad, weights[0])
            for copy in landed[1:]:
                copy.wait()
            query = []
            for j in range(3):
                tile = slice(256 * j, 256 * j + 256)
                spread = spread_heads(att[:, tile], 4).astype(BF)
                prob_grad = dot(spread, values_t[k, tile])
                probs = prob[k, 4 * j : 4 * j + 4].reshape(4 * ROWS, L)
                inner = jnp.sum(probs * prob_grad, axis=-1, keepdims=True)
                score = (probs * (prob_grad - inner) * SCALE).astype(BF)
                query.append(merge_heads(dot(score, keys[k, :, tile]), 4, ROWS).astype(BF))
            normed_grad = dot(jnp.concatenate(query, axis=1), weights[1])
            unit = rows[k, 0:ROWS]
            total = total + normed_grad * unit
            scaled = normed_grad * gain[...]
            mean = jnp.mean(scaled * unit, axis=-1, keepdims=True)
            carried = grad_in + prob[k, H, :, 0:1] * (scaled - unit * mean)
            pair_row = info[1] if k >= 2 else 1 - info[1]
            place = 72 + 32 * pair_row + ROWS * (k % 2)
            grads[pl.ds(pl.multiple_of(place, 8), ROWS)] = carried
            if k % 2 == 0:
                both = pl.ds(pl.multiple_of(72 + 32 * pair_row, 8), 2 * ROWS)
                leaving.append(leave(both, 1 + k // 2))
        sending[...] = carried
        grads[64:72] = total[0:8] + total[8:16]
        leaving.append(leave(slice(64, 72), 3))
        for copy in leaving:
            copy.wait()


def weight_kernel(
    info, t0_hbm, t1, t2, t3, rows_a, rows_b,
    wo_hbm, pick_hbm, keys_hbm, values_hbm, queries_hbm, prob_hbm, in_a_hbm, in_b_hbm,
    normed_hbm, attended_hbm,
    grad_memory, send_a, send_b,
    gin, qg, kg, vg,
    wo_cols, pick_cols, keys_pad, values_pad, queries_pad, prob, key_in, normed, attended,
    t0, slots, sems,
):
    r, zb, x, y = info[0], info[1], info[2], info[3]
    copies = [
        pltpu.make_async_copy(src, dst, sems.at[i])
        for i, (src, dst) in enumerate(
            (
                (t0_hbm, t0), (rows_a.at[:, 2 * ROWS : 2 * ROWS + 8], slots.at[0:2]),
                (rows_b.at[:, 2 * ROWS : 2 * ROWS + 8], slots.at[2:4]),
                (wo_hbm, wo_cols), (values_hbm, values_pad), (prob_hbm, prob),
                (keys_hbm, keys_pad), (queries_hbm, queries_pad), (pick_hbm, pick_cols),
                (in_a_hbm, key_in.at[0:2]), (in_b_hbm, key_in.at[2:4]),
                (normed_hbm, normed), (attended_hbm, attended),
            )
        )
    ]
    for copy in copies:
        copy.start()
    for copy in copies[:3]:
        copy.wait()
    gain = jnp.zeros((8, D), F32)
    for s, t in enumerate((t0, t1, t2, t3)):
        first = pl.multiple_of(jnp.bitwise_xor(r, s) * ROWS, ROWS)
        for m in range(4):
            slot = slots[m, 0:1]
            k = 2 * jnp.bitwise_xor(zb, m // 2) + m % 2
            gin[m, pl.ds(first, ROWS)] = t[pl.ds(pl.multiple_of(k * ROWS, ROWS), ROWS)] * slot
        place = (104 if s < 2 else 72) + ROWS * jnp.bitwise_and(r, 1)
        grad_memory[pl.ds(first, ROWS)] = t[pl.ds(pl.multiple_of(place, 8), ROWS)]
        gain = gain + t[64:72]
    gain = jnp.sum(gain, axis=0, keepdims=True)
    out_grad = gin[...].reshape(4 * R, D).astype(BF)
    copies[3].wait()
    att = dot(out_grad, wo_cols[...])
    for copy in copies[4:]:
        copy.wait()
    picked = dot(out_grad, pick_cols[...]).astype(BF)
    for k in range(4):
        spread = spread_heads(att[R * k : R * k + R], 3).astype(BF)
        prob_grad = dot(spread, values_pad[k], ((1,), (1,)))
        probs = prob[k].reshape(3 * R, L)
        inner = jnp.sum(probs * prob_grad, axis=-1, keepdims=True)
        score = (probs * (prob_grad - inner) * SCALE).astype(BF)
        read = dot(score, keys_pad[k])
        qg[R * k : R * k + R] = merge_heads(read, 3, R).astype(BF)
        vg[L * k : L * k + L] = dot(probs.astype(BF), spread, ((0,), (0,))).astype(BF)
        q_spread = spread_heads(queries_pad[k].astype(F32), 3, 3).astype(BF)
        kg[L * k : L * k + L] = dot(score, q_spread, ((0,), (0,))).astype(BF)
    inputs = key_in[...].reshape(4 * L, D)
    both = dot(normed[...].reshape(4 * R, D), qg[...], ((0,), (0,)))
    both = both + dot(inputs, kg[...], ((0,), (0,)))
    tail = jnp.concatenate(
        [gain[:, 0:384], gain[:, 384:768], jnp.zeros((6, 384), F32)], axis=0
    )
    for ra in range(4):
        at = jnp.bitwise_and(ra - x, 3)
        for yz in range(8):
            a = yz * 4 + ra
            send_a[at, 24 * yz : 24 * yz + 24] = both[24 * a : 24 * a + 24]
        send_a[at, 192:200] = tail
    both = dot(inputs, vg[...], ((0,), (0,)))
    both = both + dot(attended[...].reshape(4 * R, D), picked, ((0,), (0,)))
    for ya in range(4):
        send_b[jnp.bitwise_and(ya - y, 3)] = both[192 * ya : 192 * ya + 192]


def shape(*dims, dtype=F32):
    return jax.ShapeDtypeStruct(dims, dtype)


def far(*dims, dtype=F32):
    return shape(*dims, dtype=dtype) if INTERPRET else pltpu.HBM(dims, dtype)


def near(*dims, dtype=F32):
    return shape(*dims, dtype=dtype) if INTERPRET else pltpu.VMEM(dims, dtype)


def run(
    kernel, args, outs, scratch=(), aliases=None, flops=0, nbytes=0, limit=16, away=(), close=(),
    away_out=(),
):
    smem = pl.BlockSpec(memory_space=pltpu.SMEM)
    vmem = pl.BlockSpec(memory_space=pltpu.VMEM)
    hbm = pl.BlockSpec(memory_space=pl.ANY if INTERPRET else pltpu.HBM)
    args = list(args)
    for i in () if INTERPRET else away:
        args[i] = pltpu.with_memory_space_constraint(args[i], pltpu.HBM)
    for i in () if INTERPRET else close:
        args[i] = pltpu.with_memory_space_constraint(args[i], pltpu.VMEM)
    return pl.pallas_call(
        kernel,
        out_shape=outs,
        in_specs=[smem] + [hbm if i in away else vmem for i in range(1, len(args))],
        out_specs=[hbm if i in away_out else vmem for i in range(len(outs))],
        scratch_shapes=list(scratch),
        input_output_aliases=aliases or {},
        interpret=INTERPRET,
        compiler_params=pltpu.CompilerParams(vmem_limit_bytes=limit * 1024 * 1024),
        cost_estimate=pl.CostEstimate(flops=flops, bytes_accessed=nbytes, transcendentals=0),
    )(*args)


def frequencies():
    half = D // 2
    return 0.0625 * jnp.exp(-math.log(1000.0) * jnp.arange(half, dtype=F32) / half)


def within_clip():
    half = D // 2
    rate = 0.0625 * np.exp(-math.log(1000.0) * np.arange(half) / half)
    phases = np.arange(L)[:, None] * rate[None]
    return np.stack([np.sin(phases), np.cos(phases)]).astype(np.float32)


def flat(y, zp, r, x, h):
    return (y * 8 + zp * 4 + r) * 8 + x * 2 + h


def pairs(move):
    out = []
    for y in range(4):
        for zp in range(2):
            for r in range(4):
                for x in range(4):
                    for h in range(2):
                        to = move(y, zp, r, x, h)
                        if to is not None:
                            out.append((flat(y, zp, r, x, h), flat(*to)))
    return out


def send(value, move):
    return lax.ppermute(value, AXES, pairs(move))


def swap_core(value):
    return send(value, lambda y, zp, r, x, h: (y, zp, r ^ 1, x, h))


def swap_z(value):
    return send(value, lambda y, zp, r, x, h: (y, zp, r ^ 2, x, h))


def to_next(value, group):
    def move(y, zp, r, x, h):
        if y * 2 + zp != group:
            return None
        return ((group - 1) // 2, (group - 1) % 2, r, x, h)

    return send(value, move)


def pick(array, index):
    return lax.dynamic_index_in_dim(array, index, 0, keepdims=False)


def on_device(
    memory, frames, mem_cot, slot_used, key_bias, start_offset,
    norm_gain, w_query, w_key, w_value, w_out,
):
    position = lax.axis_index("tm")
    video = lax.axis_index("video")
    group = position // 4
    r = position % 4
    core = position % 2
    y, zp = position // 8, (position // 4) % 2
    x, h = video // 2, video % 2
    zb = r // 2
    at_cores = jnp.stack([core, r]).astype(jnp.int32)

    own_frames = frames[0, 0, 0]
    pack_own, pack_far, own_mem = run(
        pack_kernel,
        (
            jnp.stack([zb.astype(jnp.int32), slot_used[0, 0, 0]]),
            memory[0, 0, 0], mem_cot[0, 0, 0], key_bias[0, 0, 0],
        ),
        [shape(80, D), shape(80, D), shape(R, D)],
        flops=10**6, nbytes=10**6, limit=8,
    )
    frames_z = swap_z(own_frames)
    pack_z = swap_z(pack_far)
    frames_c = swap_core(own_frames)
    pack_c = swap_core(pack_own)
    clips = jnp.stack([4 * group + (r ^ s) for s in range(4)])
    first_times = (start_offset[0, 0] + clips * L).astype(F32)
    phases = first_times[:, None] * frequencies()[None]
    starts = jnp.concatenate([jnp.sin(phases), jnp.cos(phases)], axis=0)
    table = jnp.asarray(within_clip())
    weights = jnp.stack([w_out.T, w_query.T])
    gain = norm_gain[None]

    frames_cz = swap_core(frames_z)
    pack_cz = swap_core(pack_z)
    share = jnp.zeros((136, D), F32)
    frames_cz, weights, share = lax.optimization_barrier((frames_cz, weights, share))
    pair_kinds = [
        far(2, L, D, dtype=BF), far(2, L, D, dtype=BF), far(2, L, D, dtype=BF),
        far(2, D, L, dtype=BF), far(2, 40, D), far(2, H + 1, ROWS, L),
    ]
    prepared = run(
        prep_kernel,
        (
            at_cores, own_frames, pack_own, frames_c, pack_c,
            frames_z, pack_z, frames_cz, pack_cz, starts, table, gain,
            w_query, w_key, w_value,
        ),
        pair_kinds + pair_kinds,
        flops=2 * 10**9, nbytes=10**7, limit=32,
    )
    pair_a, pair_b = prepared[:6], prepared[6:]
    mem_late, _ = lax.optimization_barrier((own_mem, frames_cz))
    mem_z = swap_z(mem_late)
    mem_c = swap_core(mem_late)

    incoming = jnp.zeros((ROWS, D), F32)
    pairs_ab = tuple(p[i] for p in (pair_a, pair_b) for i in (1, 3, 4, 5))
    for turn in range(GROUPS_TM):
        active = GROUPS_TM - 1 - turn
        info = jnp.stack([(group == active).astype(jnp.int32), zb.astype(jnp.int32)])
        sending, share, weights = run(
            chain_kernel,
            (info, incoming, gain) + pairs_ab + (weights, share),
            [shape(ROWS, D), far(136, D), near(2, D, D, dtype=BF)],
            scratch=[
                pltpu.VMEM((4, L, D), BF), pltpu.VMEM((4, D, L), BF), pltpu.VMEM((4, 40, D), F32),
                pltpu.VMEM((4, H + 1, ROWS, L), F32), pltpu.VMEM((136, D), F32),
                pltpu.SemaphoreType.DMA((4, 5)),
            ],
            aliases={12: 1, 11: 2}, away=tuple(range(3, 11)) + (12,), close=(11,), away_out=(1,),
            flops=2 * 10**9, nbytes=5 * 10**6, limit=8,
        )
        if active > 0:
            incoming = to_next(sending, active)
        if turn == 1:
            mem_z, _ = lax.optimization_barrier((mem_z, sending))
            mem_cz = swap_core(mem_z)
            mems = lax.optimization_barrier((own_mem, mem_c, mem_z, mem_cz, sending))[:4]
            ready = run(
                whole_kernel,
                (at_cores,)
                + tuple(mems)
                + (
                    pack_own, pack_c, pack_z, pack_cz,
                    pair_a[1], pair_a[2], pair_b[1], pair_b[2], gain, w_query, weights,
                ),
                [
                    far(4, R, D, dtype=BF), far(4, R, D, dtype=BF), far(4, 3, R, L),
                    far(4, L, 384, dtype=BF), far(4, L, 384, dtype=BF),
                    far(4, R, 384, dtype=BF), far(D, 384, dtype=BF), far(D, 384, dtype=BF),
                ],
                scratch=[pltpu.VMEM((H, R, L), F32)],
                flops=10**9, nbytes=8 * 10**6, limit=20,
            )
            normed, attended, prob, keys_pad, values_pad, queries_pad, wo_cols, pick_cols = ready
            incoming, _ = lax.optimization_barrier((incoming, prob))

    share_z = swap_z(share[:104])
    share_c = swap_core(share)
    share_cz = swap_core(share_z)
    grad_memory, send_a, send_b = run(
        weight_kernel,
        (
            jnp.stack([r, zb, x, y]).astype(jnp.int32),
            share, share_c, share_z, share_cz, pair_a[4], pair_b[4],
            wo_cols, pick_cols, keys_pad, values_pad, queries_pad,
            prob, pair_a[0], pair_b[0], normed, attended,
        ),
        [shape(R, D), shape(4, 200, 384), shape(4, 192, 384)],
        scratch=[
            pltpu.VMEM((4, R, D), F32), pltpu.VMEM((4 * R, 384), BF),
            pltpu.VMEM((4 * L, 384), BF), pltpu.VMEM((4 * L, 384), BF),
            pltpu.VMEM((D, 384), BF), pltpu.VMEM((D, 384), BF), pltpu.VMEM((4, L, 384), BF),
            pltpu.VMEM((4, L, 384), BF), pltpu.VMEM((4, R, 384), BF),
            pltpu.VMEM((4, 3, R, L), F32), pltpu.VMEM((4, L, D), BF), pltpu.VMEM((4, R, D), BF),
            pltpu.VMEM((4, R, D), BF), pltpu.VMEM((136, D), F32), pltpu.VMEM((4, 8, D), F32),
            pltpu.SemaphoreType.DMA((13,)),
        ],
        flops=2 * 10**9, nbytes=10**7, limit=24, away=(1,) + tuple(range(5, 17)),
    )

    def along_x(step):
        return lambda yy, zz, rr, xx, hh: (yy, zz, rr, (xx + step) % 4, hh)

    def along_y(step):
        return lambda yy, zz, rr, xx, hh: ((yy + step) % 4, zz, rr, xx, hh)

    def ring_sums(parts):
        first = []
        for chunks, axis, half in parts:
            up = send(chunks[2, :half], axis(1))
            down = send(chunks[2, half:], axis(-1))
            first.append((up, down))
        second = []
        for (chunks, axis, half), (up, down) in zip(parts, first):
            up = jnp.concatenate([chunks[1, :half] + up, chunks[1, half:]], axis=0)
            down = jnp.concatenate([chunks[3, :half], chunks[3, half:] + down], axis=0)
            second.append((send(up, axis(1)), send(down, axis(-1))))
        return [
            chunks[0] + up + down for (chunks, axis, half), (up, down) in zip(parts, second)
        ]

    def at(chunks, index, step):
        return pick(chunks, (index + step) % 4)

    def direct_sums(parts):
        got = []
        for step in (2, 1, 3):
            for chunks, axis, index in parts:
                got.append(send(at(chunks, index, step), axis(step)))
        return [
            at(chunks, index, 0) + got[i] + got[2 + i] + got[4 + i]
            for i, (chunks, axis, index) in enumerate(parts)
        ]

    half_a, half_b = ring_sums([(send_a, along_x, 104), (send_b, along_y, 96)])
    chunks_a = jnp.concatenate(
        [
            half_a[:192].reshape(4, 48, 384),
            jnp.broadcast_to(half_a[None, 192:], (4, 8, 384)),
        ],
        axis=1,
    )
    chunks_b = half_b.reshape(2, 4, 24, 384).transpose(1, 0, 2, 3).reshape(4, 48, 384)
    half_a, half_b = direct_sums([(chunks_a, along_y, y), (chunks_b, along_x, x)])
    by_zp = jnp.concatenate(
        [half_a[:48].reshape(2, 24, 2, 2, 96), half_b.reshape(2, 24, 2, 2, 96)], axis=2
    )
    chunks = by_zp.transpose(0, 3, 1, 2, 4).reshape(4, 24, 384)
    chunks = jnp.concatenate([chunks, jnp.broadcast_to(half_a[None, 48:], (4, 8, 384))], axis=1)
    here = zp * 2 + h
    total = None
    for s in range(4):
        got = send(
            pick(chunks, here ^ s),
            lambda yy, zz, rr, xx, hh, s=s: (yy, zz ^ (s // 2), xx, rr, hh ^ (s % 2)),
        )
        total = got if total is None else total + got
    total = total * (1.0 / 256.0)
    return (
        grad_memory[None, None, None],
        total[:24, 0:96],
        total[:24, 96:192],
        total[:24, 192:288],
        total[:24, 288:384],
        total[24:26].reshape(D),
    )


def solution(mesh):
    return jax.shard_map(
        on_device,
        mesh=mesh,
        in_specs=(
            P("video", "tm", None, None, None),
            P("video", "tm", None, None, None),
            P("video", "tm", None, None, None),
            P("video", "tm", None),
            P("video", "tm", None, None, None),
            P("video", None),
            P(),
            P(),
            P(),
            P(),
            P(),
        ),
        out_specs=(
            P("video", "tm", None, None, None),
            P("tm", "video"),
            P("tm", "video"),
            P("tm", "video"),
            P("tm", "video"),
            P(),
        ),
        check_vma=False,
    )
```

```python
import functools
import math

import jax
import jax.numpy as jnp
import numpy as np
from jax import lax
from jax.experimental import pallas as pl
from jax.experimental.pallas import tpu as pltpu
from jax.sharding import PartitionSpec as P

D = 768
H = 12
HD = 64
R = 64
L = 128
NORM_EPSILON = 1e-06
SCALE = HD ** (-0.5)
BF = jnp.bfloat16
F32 = jnp.float32
AXES = ("tm", "video")
GROUPS_TM = 8
ROWS = 16
INTERPRET = False
BIAS = 64
SLOT = BIAS + H


def dot(left, right, form=((1,), (0,))):
    return lax.dot_general(left, right, (form, ((), ())), preferred_element_type=F32)


def lane_head(rows, lanes):
    return lax.broadcasted_iota(jnp.int32, (rows, lanes), 1) // HD


def spread_heads(value, heads, base=0):
    which = lane_head(*value.shape)
    zero = jnp.zeros_like(value)
    parts = [jnp.where(which == base + h, value, zero) for h in range(heads)]
    return jnp.concatenate(parts, axis=0)


def merge_heads(value, heads, rows):
    which = lane_head(rows, value.shape[1])
    total = jnp.where(which == 0, value[:rows], 0.0)
    for h in range(1, heads):
        total = jnp.where(which == h, value[h * rows : (h + 1) * rows], total)
    return total


def pack_kernel(info, memory, cotangent, bias, pack_own, pack_far, mem_wide):
    zb = info[0]
    wide = memory[...].astype(F32)
    mem_wide[...] = wide
    cot = cotangent[...].astype(F32)
    slot = jnp.full((4, D), info[1], jnp.int32).astype(F32)
    ends = jnp.concatenate([bias[...], jnp.zeros((H, D - L), F32)], axis=1)
    ends = jnp.concatenate([ends, slot], axis=0)
    half = 2 * ROWS
    for chip in range(2):
        rows = slice(half * chip, half * chip + half)
        block = jnp.concatenate([wide[rows], cot[rows], ends], axis=0)

        @pl.when(zb == chip)
        def _():
            pack_own[...] = block

        @pl.when(zb != chip)
        def _():
            pack_far[...] = block


def prep_kernel(info, *refs):
    for pair in range(2):
        prep_pair(
            2 * pair, info, *refs[4 * pair : 4 * pair + 4], *refs[8:14],
            *refs[14 + 6 * pair : 20 + 6 * pair],
        )


def prep_pair(
    base, info, frames_a, pack_a, frames_b, pack_b, starts, table, gain, w_query, w_key, w_value,
    key_in, keys, values, values_t, rows, probs_out,
):
    core = info[0]
    place = (core, 1 - core)
    first = pl.multiple_of(core * ROWS, ROWS)
    tokens = []
    for i, frames in enumerate((frames_a, frames_b)):
        at = base + i
        sin_0, cos_0 = starts[at : at + 1], starts[4 + at : 5 + at]
        sine = sin_0 * table[1] + cos_0 * table[0]
        cosine = cos_0 * table[1] - sin_0 * table[0]
        tokens.append((frames[...] + jnp.concatenate([sine, cosine], axis=1)).astype(BF))
    tokens = jnp.concatenate(tokens, axis=0)
    mem = jnp.concatenate([pack_a[pl.ds(first, ROWS)], pack_b[pl.ds(first, ROWS)]], axis=0)
    inv = lax.rsqrt(jnp.mean(mem * mem, axis=-1, keepdims=True) + NORM_EPSILON)
    unit = mem * inv
    query_f = dot((unit * gain[...]).astype(BF), w_query[...])
    key_b = dot(tokens, w_key[...]).astype(BF)
    value_f = dot(tokens, w_value[...])
    inv_wide = jnp.broadcast_to(inv, (2 * ROWS, 128))
    for i, pack in enumerate((pack_a, pack_b)):
        k = place[i]
        row = slice(ROWS * i, ROWS * i + ROWS)
        token = slice(L * i, L * i + L)
        key_in[k] = tokens[token]
        keys[k] = key_b[token]
        values[k] = value_f[token].astype(BF)
        values_t[k] = value_f[token].T.astype(BF)
        rows[k, 0:ROWS] = unit[row]
        rows[k, ROWS : 2 * ROWS] = pack[pl.ds(2 * ROWS + first, ROWS)]
        rows[k, 2 * ROWS : 2 * ROWS + 8] = jnp.broadcast_to(pack[SLOT : SLOT + 1], (8, D))
        probs_out[k, H] = inv_wide[row]
        for j in range(3):
            tile = slice(256 * j, 256 * j + 256)
            spread = spread_heads(query_f[row, tile], 4).astype(BF)
            probs = attend(spread, key_b[token, tile], pack, j, ROWS)
            probs_out[k, 4 * j : 4 * j + 4] = probs.reshape(4, ROWS, L)


def attend(spread, key_tile, pack, j, rows):
    scores = dot(spread, key_tile, ((1,), (1,))) * SCALE
    bias = []
    for h in range(4 * j, 4 * j + 4):
        bias.append(jnp.broadcast_to(pack[BIAS + h : BIAS + h + 1, 0:L], (rows, L)))
    scores = scores + jnp.concatenate(bias, axis=0)
    top = jnp.max(scores, axis=-1, keepdims=True)
    raised = jnp.exp(scores - top)
    return raised / jnp.sum(raised, axis=-1, keepdims=True)


def whole_kernel(
    info, m0, m1, m2, m3, pack0, pack1, pack2, pack3, keys_a, values_a, keys_b, values_b,
    gain, w_query, weights,
    normed, attended, prob_mine, keys_pad, values_pad, queries_pad, wo_cols, pick_cols, prob,
):
    core, r = info[0], info[1]
    row_id = lax.broadcasted_iota(jnp.int32, (D, 384), 0) - 192 * r
    lane_id = lax.broadcasted_iota(jnp.int32, (D, 384), 1)
    low = ((row_id == lane_id) & (lane_id < 192)).astype(F32).astype(BF)
    high = ((row_id == lane_id - 192) & (lane_id >= 192)).astype(F32).astype(BF)
    pick_cols[...] = high
    wo_cols[...] = dot(weights[0], low).astype(BF)
    for s, (mem_ref, pack) in enumerate(((m0, pack0), (m1, pack1), (m2, pack2), (m3, pack3))):
        keys, values = ((keys_a, values_a), (keys_b, values_b))[s // 2]
        place = core if s % 2 == 0 else 1 - core
        m = 2 * (s // 2) + place
        mem = mem_ref[...]
        inv = lax.rsqrt(jnp.mean(mem * mem, axis=-1, keepdims=True) + NORM_EPSILON)
        norm = (mem * inv * gain[...]).astype(BF)
        normed[m] = norm
        query_f = dot(norm, w_query[...])
        queries_pad[m] = dot(query_f.astype(BF), high).astype(BF)
        keys_pad[m] = dot(keys[place], low).astype(BF)
        values_pad[m] = dot(values[place], low).astype(BF)
        for j in range(3):
            tile = slice(256 * j, 256 * j + 256)
            spread = spread_heads(query_f[:, tile], 4).astype(BF)
            probs = attend(spread, keys[place, :, tile], pack, j, R)
            prob[4 * j : 4 * j + 4] = probs.reshape(4, R, L)
            read = dot(probs.astype(BF), values[place, :, tile])
            attended[m, :, tile] = merge_heads(read, 4, R).astype(BF)
        prob_mine[m] = prob[pl.ds(3 * r, 3)]


def chain_kernel(
    info, incoming, gain,
    keys_a, values_t_a, rows_a, prob_a, keys_b, values_t_b, rows_b, prob_b,
    weights, main_before, side_before,
    sending, main, side, weights_same,
    keys, values_t, rows, prob, grads, sems,
):
    own = (rows_a, values_t_a, prob_a, keys_a)
    other = (rows_b, values_t_b, prob_b, keys_b)
    inside = (rows, values_t, prob, keys)

    def copies(order, k):
        return [
            pltpu.make_async_copy(src.at[k % 2], dst.at[k], sems.at[k, i])
            for i, (src, dst) in enumerate(zip(order[1 - k // 2], inside))
        ]

    def begin(order):
        for k in (3, 2, 1, 0):
            for copy in copies(order, k):
                copy.start()

    @pl.when(info[0] == 0)
    def _():
        sending[...] = jnp.zeros_like(sending)

    @pl.when((info[0] != 0) & (info[1] == 1))
    def _():
        begin((own, other))

    @pl.when((info[0] != 0) & (info[1] == 0))
    def _():
        begin((other, own))

    @pl.when(info[0] != 0)
    def _():
        carried = incoming[...]
        total = jnp.zeros((ROWS, D), F32)
        leaving = []

        def leave(where, i):
            copy = pltpu.make_async_copy(grads.at[where], main.at[where], sems.at[i, 4])
            copy.start()
            return copy

        for k in (3, 2, 1, 0):
            landed = copies((own, other), k)
            landed[0].wait()
            grad_in = carried + rows[k, ROWS : 2 * ROWS]
            grads[ROWS * k : ROWS * k + ROWS] = grad_in
            if k == 0:
                leaving.append(leave(slice(0, 64), 0))
            out_grad = (grad_in * rows[k, 2 * ROWS : 2 * ROWS + 1]).astype(BF)
            att = dot(out_grad, weights[0])
            for copy in landed[1:]:
                copy.wait()
            query = []
            for j in range(3):
                tile = slice(256 * j, 256 * j + 256)
                spread = spread_heads(att[:, tile], 4).astype(BF)
                prob_grad = dot(spread, values_t[k, tile])
                probs = prob[k, 4 * j : 4 * j + 4].reshape(4 * ROWS, L)
                inner = jnp.sum(probs * prob_grad, axis=-1, keepdims=True)
                score = (probs * (prob_grad - inner) * SCALE).astype(BF)
                query.append(merge_heads(dot(score, keys[k, :, tile]), 4, ROWS).astype(BF))
            normed_grad = dot(jnp.concatenate(query, axis=1), weights[1])
            unit = rows[k, 0:ROWS]
            total = total + normed_grad * unit
            scaled = normed_grad * gain[...]
            mean = jnp.mean(scaled * unit, axis=-1, keepdims=True)
            carried = grad_in + prob[k, H, :, 0:1] * (scaled - unit * mean)
            pair_row = info[1] if k >= 2 else 1 - info[1]
            place = 72 + 32 * pair_row + ROWS * (k % 2)
            grads[pl.ds(pl.multiple_of(place, 8), ROWS)] = carried
            if k % 2 == 0:
                sem = sems.at[1 + k // 2, 4]
                to_main = pltpu.make_async_copy(grads.at[72:104], main.at[72:104], sem)
                to_side = pltpu.make_async_copy(grads.at[104:136], side, sem)
                pl.when(pair_row == 0)(to_main.start)
                pl.when(pair_row != 0)(to_side.start)
                leaving.append(to_main)
        sending[...] = carried
        grads[64:72] = total[0:8] + total[8:16]
        leaving.append(leave(slice(64, 72), 3))
        for copy in leaving:
            copy.wait()


def weight_kernel(
    info, t0_hbm, t1, t2, t3, side_hbm, side_c, rows_a, rows_b,
    wo_hbm, pick_hbm, keys_hbm, values_hbm, queries_hbm, prob_hbm, in_a_hbm, in_b_hbm,
    normed_hbm, attended_hbm,
    grad_memory, send_a, send_b,
    gin, qg, kg, vg,
    wo_cols, pick_cols, keys_pad, values_pad, queries_pad, prob, key_in, normed, attended,
    t0, side, slots, sems,
):
    r, zb, x, y = info[0], info[1], info[2], info[3]
    copies = [
        pltpu.make_async_copy(src, dst, sems.at[i])
        for i, (src, dst) in enumerate(
            (
                (t0_hbm, t0), (side_hbm, side), (rows_a.at[:, 2 * ROWS : 2 * ROWS + 8], slots.at[0:2]),
                (rows_b.at[:, 2 * ROWS : 2 * ROWS + 8], slots.at[2:4]),
                (wo_hbm, wo_cols), (values_hbm, values_pad), (prob_hbm, prob),
                (keys_hbm, keys_pad), (queries_hbm, queries_pad), (pick_hbm, pick_cols),
                (in_a_hbm, key_in.at[0:2]), (in_b_hbm, key_in.at[2:4]),
                (normed_hbm, normed), (attended_hbm, attended),
            )
        )
    ]
    for copy in copies:
        copy.start()
    for copy in copies[:4]:
        copy.wait()
    gain = jnp.zeros((8, D), F32)
    for s, t in enumerate((t0, t1, t2, t3)):
        first = pl.multiple_of(jnp.bitwise_xor(r, s) * ROWS, ROWS)
        for m in range(4):
            slot = slots[m, 0:1]
            k = 2 * jnp.bitwise_xor(zb, m // 2) + m % 2
            gin[m, pl.ds(first, ROWS)] = t[pl.ds(pl.multiple_of(k * ROWS, ROWS), ROWS)] * slot
        place = (0 if s < 2 else 72) + ROWS * jnp.bitwise_and(r, 1)
        grad_memory[pl.ds(first, ROWS)] = (side, side_c, t2, t3)[s][pl.ds(pl.multiple_of(place, 8), ROWS)]
        gain = gain + t[64:72]
    gain = jnp.sum(gain, axis=0, keepdims=True)
    out_grad = gin[...].reshape(4 * R, D).astype(BF)
    copies[4].wait()
    att = dot(out_grad, wo_cols[...])
    for copy in copies[5:]:
        copy.wait()
    picked = dot(out_grad, pick_cols[...]).astype(BF)
    for k in range(4):
        spread = spread_heads(att[R * k : R * k + R], 3).astype(BF)
        prob_grad = dot(spread, values_pad[k], ((1,), (1,)))
        probs = prob[k].reshape(3 * R, L)
        inner = jnp.sum(probs * prob_grad, axis=-1, keepdims=True)
        score = (probs * (prob_grad - inner) * SCALE).astype(BF)
        read = dot(score, keys_pad[k])
        qg[R * k : R * k + R] = merge_heads(read, 3, R).astype(BF)
        vg[L * k : L * k + L] = dot(probs.astype(BF), spread, ((0,), (0,))).astype(BF)
        q_spread = spread_heads(queries_pad[k].astype(F32), 3, 3).astype(BF)
        kg[L * k : L * k + L] = dot(score, q_spread, ((0,), (0,))).astype(BF)
    inputs = key_in[...].reshape(4 * L, D)
    both = dot(normed[...].reshape(4 * R, D), qg[...], ((0,), (0,)))
    both = both + dot(inputs, kg[...], ((0,), (0,)))
    tail = jnp.concatenate(
        [gain[:, 0:384], gain[:, 384:768], jnp.zeros((6, 384), F32)], axis=0
    )
    for ra in range(4):
        at = jnp.bitwise_and(ra - x, 3)
        for yz in range(8):
            a = yz * 4 + ra
            send_a[at, 24 * yz : 24 * yz + 24] = both[24 * a : 24 * a + 24]
        send_a[at, 192:200] = tail
    both = dot(inputs, vg[...], ((0,), (0,)))
    both = both + dot(attended[...].reshape(4 * R, D), picked, ((0,), (0,)))
    for ya in range(4):
        send_b[jnp.bitwise_and(ya - y, 3)] = both[192 * ya : 192 * ya + 192]


def shape(*dims, dtype=F32):
    return jax.ShapeDtypeStruct(dims, dtype)


def far(*dims, dtype=F32):
    return shape(*dims, dtype=dtype) if INTERPRET else pltpu.HBM(dims, dtype)


def near(*dims, dtype=F32):
    return shape(*dims, dtype=dtype) if INTERPRET else pltpu.VMEM(dims, dtype)


def run(
    kernel, args, outs, scratch=(), aliases=None, flops=0, nbytes=0, limit=16, away=(), close=(),
    away_out=(),
):
    smem = pl.BlockSpec(memory_space=pltpu.SMEM)
    vmem = pl.BlockSpec(memory_space=pltpu.VMEM)
    hbm = pl.BlockSpec(memory_space=pl.ANY if INTERPRET else pltpu.HBM)
    args = list(args)
    for i in () if INTERPRET else away:
        args[i] = pltpu.with_memory_space_constraint(args[i], pltpu.HBM)
    for i in () if INTERPRET else close:
        args[i] = pltpu.with_memory_space_constraint(args[i], pltpu.VMEM)
    return pl.pallas_call(
        kernel,
        out_shape=outs,
        in_specs=[smem] + [hbm if i in away else vmem for i in range(1, len(args))],
        out_specs=[hbm if i in away_out else vmem for i in range(len(outs))],
        scratch_shapes=list(scratch),
        input_output_aliases=aliases or {},
        interpret=INTERPRET,
        compiler_params=pltpu.CompilerParams(vmem_limit_bytes=limit * 1024 * 1024),
        cost_estimate=pl.CostEstimate(flops=flops, bytes_accessed=nbytes, transcendentals=0),
    )(*args)


def frequencies():
    half = D // 2
    return 0.0625 * jnp.exp(-math.log(1000.0) * jnp.arange(half, dtype=F32) / half)


def within_clip():
    half = D // 2
    rate = 0.0625 * np.exp(-math.log(1000.0) * np.arange(half) / half)
    phases = np.arange(L)[:, None] * rate[None]
    return np.stack([np.sin(phases), np.cos(phases)]).astype(np.float32)


def flat(y, zp, r, x, h):
    return (y * 8 + zp * 4 + r) * 8 + x * 2 + h


def pairs(move):
    out = []
    for y in range(4):
        for zp in range(2):
            for r in range(4):
                for x in range(4):
                    for h in range(2):
                        to = move(y, zp, r, x, h)
                        if to is not None:
                            out.append((flat(y, zp, r, x, h), flat(*to)))
    return out


def send(value, move):
    return lax.ppermute(value, AXES, pairs(move))


def swap_core(value):
    return send(value, lambda y, zp, r, x, h: (y, zp, r ^ 1, x, h))


def swap_z(value):
    return send(value, lambda y, zp, r, x, h: (y, zp, r ^ 2, x, h))


def to_next(value, group):
    def move(y, zp, r, x, h):
        if y * 2 + zp != group:
            return None
        return ((group - 1) // 2, (group - 1) % 2, r, x, h)

    return send(value, move)


def pick(array, index):
    return lax.dynamic_index_in_dim(array, index, 0, keepdims=False)


def on_device(
    memory, frames, mem_cot, slot_used, key_bias, start_offset,
    norm_gain, w_query, w_key, w_value, w_out,
):
    position = lax.axis_index("tm")
    video = lax.axis_index("video")
    group = position // 4
    r = position % 4
    core = position % 2
    y, zp = position // 8, (position // 4) % 2
    x, h = video // 2, video % 2
    zb = r // 2
    at_cores = jnp.stack([core, r]).astype(jnp.int32)

    own_frames = frames[0, 0, 0]
    pack_own, pack_far, own_mem = run(
        pack_kernel,
        (
            jnp.stack([zb.astype(jnp.int32), slot_used[0, 0, 0]]),
            memory[0, 0, 0], mem_cot[0, 0, 0], key_bias[0, 0, 0],
        ),
        [shape(80, D), shape(80, D), shape(R, D)],
        flops=10**6, nbytes=10**6, limit=8,
    )
    frames_z = swap_z(own_frames)
    pack_z = swap_z(pack_far)
    frames_c = swap_core(own_frames)
    pack_c = swap_core(pack_own)
    clips = jnp.stack([4 * group + (r ^ s) for s in range(4)])
    first_times = (start_offset[0, 0] + clips * L).astype(F32)
    phases = first_times[:, None] * frequencies()[None]
    starts = jnp.concatenate([jnp.sin(phases), jnp.cos(phases)], axis=0)
    table = jnp.asarray(within_clip())
    weights = jnp.stack([w_out.T, w_query.T])
    gain = norm_gain[None]

    frames_cz = swap_core(frames_z)
    pack_cz = swap_core(pack_z)
    main = jnp.zeros((104, D), F32)
    side = jnp.zeros((32, D), F32)
    frames_cz, weights, main, side = lax.optimization_barrier((frames_cz, weights, main, side))
    pair_kinds = [
        far(2, L, D, dtype=BF), far(2, L, D, dtype=BF), far(2, L, D, dtype=BF),
        far(2, D, L, dtype=BF), far(2, 40, D), far(2, H + 1, ROWS, L),
    ]
    prepared = run(
        prep_kernel,
        (
            at_cores, own_frames, pack_own, frames_c, pack_c,
            frames_z, pack_z, frames_cz, pack_cz, starts, table, gain,
            w_query, w_key, w_value,
        ),
        pair_kinds + pair_kinds,
        flops=2 * 10**9, nbytes=10**7, limit=32,
    )
    pair_a, pair_b = prepared[:6], prepared[6:]
    mem_late, _ = lax.optimization_barrier((own_mem, frames_cz))
    mem_z = swap_z(mem_late)
    mem_c = swap_core(mem_late)

    incoming = jnp.zeros((ROWS, D), F32)
    pairs_ab = tuple(p[i] for p in (pair_a, pair_b) for i in (1, 3, 4, 5))
    for turn in range(GROUPS_TM):
        active = GROUPS_TM - 1 - turn
        info = jnp.stack([(group == active).astype(jnp.int32), zb.astype(jnp.int32)])
        sending, main, side, weights = run(
            chain_kernel,
            (info, incoming, gain) + pairs_ab + (weights, main, side),
            [shape(ROWS, D), far(104, D), far(32, D), near(2, D, D, dtype=BF)],
            scratch=[
                pltpu.VMEM((4, L, D), BF), pltpu.VMEM((4, D, L), BF), pltpu.VMEM((4, 40, D), F32),
                pltpu.VMEM((4, H + 1, ROWS, L), F32), pltpu.VMEM((136, D), F32),
                pltpu.SemaphoreType.DMA((4, 5)),
            ],
            aliases={12: 1, 13: 2, 11: 3}, away=tuple(range(3, 11)) + (12, 13), close=(11,), away_out=(1, 2),
            flops=2 * 10**9, nbytes=5 * 10**6, limit=8,
        )
        if active > 0:
            incoming = to_next(sending, active)
        if turn == 1:
            mem_z, _ = lax.optimization_barrier((mem_z, sending))
            mem_cz = swap_core(mem_z)
            mems = lax.optimization_barrier((own_mem, mem_c, mem_z, mem_cz, sending))[:4]
            ready = run(
                whole_kernel,
                (at_cores,)
                + tuple(mems)
                + (
                    pack_own, pack_c, pack_z, pack_cz,
                    pair_a[1], pair_a[2], pair_b[1], pair_b[2], gain, w_query, weights,
                ),
                [
                    far(4, R, D, dtype=BF), far(4, R, D, dtype=BF), far(4, 3, R, L),
                    far(4, L, 384, dtype=BF), far(4, L, 384, dtype=BF),
                    far(4, R, 384, dtype=BF), far(D, 384, dtype=BF), far(D, 384, dtype=BF),
                ],
                scratch=[pltpu.VMEM((H, R, L), F32)],
                flops=10**9, nbytes=8 * 10**6, limit=20,
            )
            normed, attended, prob, keys_pad, values_pad, queries_pad, wo_cols, pick_cols = ready
            incoming, _ = lax.optimization_barrier((incoming, prob))

    main_z = swap_z(main)
    main_c = swap_core(main)
    side_c = swap_core(side)
    main_cz = swap_core(main_z)
    grad_memory, send_a, send_b = run(
        weight_kernel,
        (
            jnp.stack([r, zb, x, y]).astype(jnp.int32),
            main, main_c, main_z, main_cz, side, side_c, pair_a[4], pair_b[4],
            wo_cols, pick_cols, keys_pad, values_pad, queries_pad,
            prob, pair_a[0], pair_b[0], normed, attended,
        ),
        [shape(R, D), shape(4, 200, 384), shape(4, 192, 384)],
        scratch=[
            pltpu.VMEM((4, R, D), F32), pltpu.VMEM((4 * R, 384), BF),
            pltpu.VMEM((4 * L, 384), BF), pltpu.VMEM((4 * L, 384), BF),
            pltpu.VMEM((D, 384), BF), pltpu.VMEM((D, 384), BF), pltpu.VMEM((4, L, 384), BF),
            pltpu.VMEM((4, L, 384), BF), pltpu.VMEM((4, R, 384), BF),
            pltpu.VMEM((4, 3, R, L), F32), pltpu.VMEM((4, L, D), BF), pltpu.VMEM((4, R, D), BF),
            pltpu.VMEM((4, R, D), BF), pltpu.VMEM((104, D), F32), pltpu.VMEM((32, D), F32), pltpu.VMEM((4, 8, D), F32),
            pltpu.SemaphoreType.DMA((14,)),
        ],
        flops=2 * 10**9, nbytes=10**7, limit=24, away=(1, 5) + tuple(range(7, 19)),
    )

    def along_x(step):
        return lambda yy, zz, rr, xx, hh: (yy, zz, rr, (xx + step) % 4, hh)

    def along_y(step):
        return lambda yy, zz, rr, xx, hh: ((yy + step) % 4, zz, rr, xx, hh)

    def ring_sums(parts):
        first = []
        for chunks, axis, half in parts:
            up = send(chunks[2, :half], axis(1))
            down = send(chunks[2, half:], axis(-1))
            first.append((up, down))
        second = []
        for (chunks, axis, half), (up, down) in zip(parts, first):
            up = jnp.concatenate([chunks[1, :half] + up, chunks[1, half:]], axis=0)
            down = jnp.concatenate([chunks[3, :half], chunks[3, half:] + down], axis=0)
            second.append((send(up, axis(1)), send(down, axis(-1))))
        return [
            chunks[0] + up + down for (chunks, axis, half), (up, down) in zip(parts, second)
        ]

    def at(chunks, index, step):
        return pick(chunks, (index + step) % 4)

    def direct_sums(parts):
        got = []
        for step in (2, 1, 3):
            for chunks, axis, index in parts:
                got.append(send(at(chunks, index, step), axis(step)))
        return [
            at(chunks, index, 0) + got[i] + got[2 + i] + got[4 + i]
            for i, (chunks, axis, index) in enumerate(parts)
        ]

    half_a, half_b = ring_sums([(send_a, along_x, 104), (send_b, along_y, 96)])
    chunks_a = jnp.concatenate(
        [
            half_a[:192].reshape(4, 48, 384),
            jnp.broadcast_to(half_a[None, 192:], (4, 8, 384)),
        ],
        axis=1,
    )
    chunks_b = half_b.reshape(2, 4, 24, 384).transpose(1, 0, 2, 3).reshape(4, 48, 384)
    half_a, half_b = direct_sums([(chunks_a, along_y, y), (chunks_b, along_x, x)])
    by_zp = jnp.concatenate(
        [half_a[:48].reshape(2, 24, 2, 2, 96), half_b.reshape(2, 24, 2, 2, 96)], axis=2
    )
    chunks = by_zp.transpose(0, 3, 1, 2, 4).reshape(4, 24, 384)
    chunks = jnp.concatenate([chunks, jnp.broadcast_to(half_a[None, 48:], (4, 8, 384))], axis=1)
    here = zp * 2 + h
    total = None
    for s in range(4):
        got = send(
            pick(chunks, here ^ s),
            lambda yy, zz, rr, xx, hh, s=s: (yy, zz ^ (s // 2), xx, rr, hh ^ (s % 2)),
        )
        total = got if total is None else total + got
    total = total * (1.0 / 256.0)
    return (
        grad_memory[None, None, None],
        total[:24, 0:96],
        total[:24, 96:192],
        total[:24, 192:288],
        total[:24, 288:384],
        total[24:26].reshape(D),
    )


def solution(mesh):
    return jax.shard_map(
        on_device,
        mesh=mesh,
        in_specs=(
            P("video", "tm", None, None, None),
            P("video", "tm", None, None, None),
            P("video", "tm", None, None, None),
            P("video", "tm", None),
            P("video", "tm", None, None, None),
            P("video", None),
            P(),
            P(),
            P(),
            P(),
            P(),
        ),
        out_specs=(
            P("video", "tm", None, None, None),
            P("tm", "video"),
            P("tm", "video"),
            P("tm", "video"),
            P("tm", "video"),
            P(),
        ),
        check_vma=False,
    )
```
